32 devices in a mesh: stream: 2 (over core), dp: 16 (over z, y, x).
Axes of the slice: x: 2, y: 2, z: 4, core: 2. Of those that a mesh axis runs over, the one named last changes fastest.
Arguments:
- tokens: bfloat16 [2, 16, 256, 1152], P('stream', 'dp'), may hold values from -6 to 6
- condition: float32 [2, 16, 1152], P('stream', 'dp'), may hold values from -6 to 6
- kept_index: int32 [16, 256], P('dp'), may hold values from 0 to 255, as said below
- kept_count: int32 [16], P('dp'), may hold values from 160 to 200, as said below
- cotangent: bfloat16 [2, 16, 256, 1152], P('stream', 'dp'), may hold values from -6 to 6
- w_ada: bfloat16 [1152, 6912], P('dp'), may hold values from -0.1875 to 0.1875
- w_qkv: bfloat16 [1152, 3456], P('dp'), may hold values from -0.1875 to 0.1875
- w_proj: bfloat16 [1152, 1152], P('dp'), may hold values from -1.5 to 1.5
- w_fc1: bfloat16 [1152, 4608], P('dp'), may hold values from -0.1875 to 0.1875
- w_fc2: bfloat16 [4608, 1152], P('dp'), may hold values from -0.09375 to 0.09375
- b_ada: float32 [6912], replicated, may hold values from -3 to 3
- b_qv: float32 [2304], replicated, may hold values from -3 to 3
- b_proj: float32 [1152], replicated, may hold values from -3 to 3
- b_fc1: float32 [4608], replicated, may hold values from -3 to 3
- b_fc2: float32 [1152], replicated, may hold values from -3 to 3
- rel_table: float32 [961, 16], replicated, may hold values from -5 to 5
Outputs:
- out_tokens: bfloat16 [2, 16, 256, 1152], P('stream', 'dp')
- grad_tokens: bfloat16 [2, 16, 256, 1152], P('stream', 'dp')
- grad_condition: float32 [2, 16, 1152], P('stream', 'dp')
- grad_w_ada: float32 [1152, 6912], P('dp')
- grad_w_qkv: float32 [1152, 3456], P('dp')
- grad_w_proj: float32 [1152, 1152], P('dp')
- grad_w_fc1: float32 [1152, 4608], P('dp')
- grad_w_fc2: float32 [4608, 1152], P('dp')
- grad_b_ada: float32 [6912], replicated
- grad_b_qv: float32 [2304], replicated
- grad_b_proj: float32 [1152], replicated
- grad_b_fc1: float32 [4608], replicated
- grad_b_fc2: float32 [1152], replicated
- grad_rel_table: float32 [961, 16], replicated
The draws below stay inside these ranges and needn't reach their ends.
Inputs may be any that keep to these rules, and one draw needn't show every extreme that they name: kept_count takes 200 on the first sample and 160 on the last. `kept_index`: the first kept_count entries of a row are distinct and increasing; the rest are 0.
All inputs are finite; a program needn't handle non-finite values.
Results may differ from the reference program's by a relative error of at most 0.015.
The reference program's roundings to bfloat16 on the way count: a program that leaves them out, or rounds other values in their place, can miss the bound.
Values may be sent and summed in bfloat16 or wider, within the bound.
No kernel may reach another device: no remote copies, remote signals or barrier semaphores. Data moves between devices by JAX's collectives and lax.ppermute only.
A program may use at most 384 MiB of HBM per device.

```python
import math
import jax
import jax.numpy as jnp
from jax import lax

D = 1152
HEADS = 16
FF = 4608
GRID = 16
L = 256
NREL = 961
KEEP_LO = 160
KEEP_HI = 200
SAMPLES = 16
N_STREAM = 2


def shared_counts(key):
    counts = jax.random.randint(key, (SAMPLES,), KEEP_LO, KEEP_HI + 1)
    counts = counts.at[0].set(KEEP_HI).at[SAMPLES - 1].set(KEEP_LO)
    return counts.astype(jnp.int32)


def draw_kept_count(key, part):
    return shared_counts(key)


def draw_kept_index(key, part):
    counts = shared_counts(key)
    key = jax.random.fold_in(key, 7)
    sample_keys = jax.random.split(key, SAMPLES)
    ordinal = jnp.arange(L, dtype=jnp.int32)

    def one_row(row_key, count):
        order = jax.random.permutation(row_key, L).astype(jnp.int32)
        marked = jnp.where(ordinal < count, order, order + L)
        ranked = jnp.sort(marked)
        return jnp.where(ranked < L, ranked, 0).astype(jnp.int32)
    return jax.vmap(one_row)(sample_keys, counts)


def block_scale(own_key, dims, cuts, smallest, top_value):
    loudness, own = 1.0, jax.random.fold_in(own_key, 6)
    for axis_at, blocks in cuts:
        heights = jnp.exp(jax.random.uniform(jax.random.fold_in(own, axis_at), (blocks,), jnp.float32, smallest / len(cuts), top_value / len(cuts)))
        loudness = loudness * jnp.repeat(heights, dims[axis_at] // blocks).reshape([-1 if axis == axis_at else 1 for axis in range(len(dims))])
    return loudness


def gaussian(rng, dims, scale, most, pieces=(), kind=jnp.bfloat16):
    entries = jax.random.normal(rng, dims, jnp.float32) * scale
    if len(pieces) > 0:
        entries = block_scale(rng, dims, pieces, -0.22, 0.18) * entries
    return jnp.clip(entries, min=-most, max=most).astype(kind)


def setup_inputs(seed: int = 0) -> dict:
    key_list = jax.random.split(jax.random.key(seed), 17)
    tokens = gaussian(key_list[0], (N_STREAM, SAMPLES, L, D), 1.0, 6.0, ((0, 2), (1, 16)))
    condition = gaussian(key_list[1], (N_STREAM, SAMPLES, D), 1.0, 6.0, ((0, 2), (1, 16)), jnp.float32)
    kept_index = draw_kept_index(jax.random.fold_in(key_list[16], 71), 0)
    kept_count = draw_kept_count(jax.random.fold_in(key_list[16], 71), 0)
    cotangent = gaussian(key_list[4], (N_STREAM, SAMPLES, L, D), 1.0, 6.0, ((0, 2), (1, 16)))
    w_ada = gaussian(key_list[5], (D, 6 * D), D ** -0.5, 0.1875, ((0, 16),))
    w_qkv = gaussian(key_list[6], (D, 3 * D), D ** -0.5, 0.1875, ((0, 16),))
    w_proj = gaussian(key_list[7], (D, D), (D // 64) ** -0.5, 1.5, ((0, 16),))
    w_fc1 = gaussian(key_list[8], (D, FF), D ** -0.5, 0.1875, ((0, 16),))
    w_fc2 = gaussian(key_list[9], (FF, D), FF ** -0.5, 0.09375, ((0, 16),))
    b_ada = gaussian(key_list[10], (6 * D,), 0.5, 3.0, (), jnp.float32)
    b_qv = gaussian(key_list[11], (2 * D,), 0.5, 3.0, (), jnp.float32)
    b_proj = gaussian(key_list[12], (D,), 0.5, 3.0, (), jnp.float32)
    b_fc1 = gaussian(key_list[13], (FF,), 0.5, 3.0, (), jnp.float32)
    b_fc2 = gaussian(key_list[14], (D,), 0.5, 3.0, (), jnp.float32)
    rel_table = gaussian(key_list[15], (NREL, HEADS), 1.0, 5.0, (), jnp.float32)
    return dict(tokens=tokens, condition=condition, kept_index=kept_index, kept_count=kept_count, cotangent=cotangent, w_ada=w_ada, w_qkv=w_qkv, w_proj=w_proj, w_fc1=w_fc1, w_fc2=w_fc2, b_ada=b_ada, b_qv=b_qv, b_proj=b_proj, b_fc1=b_fc1, b_fc2=b_fc2, rel_table=rel_table)


@jax.custom_vjp
def low(v):
    return lax.optimization_barrier(v.astype(jnp.bfloat16)).astype(jnp.float32)

@jax.custom_vjp
def low_back(v):
    return v

def low_keep(v):
    return (low(v), None)

def low_pass(kept, grad):
    return (grad,)

def back_keep(v):
    return (v, None)

def back_low(kept, grad):
    return (low(grad),)
low.defvjp(low_keep, low_pass)
low_back.defvjp(back_keep, back_low)

def normalize(values):
    center = values - lax.optimization_barrier(jnp.mean(values, axis=-1, keepdims=True))
    spread = lax.optimization_barrier(jnp.mean(center * center, axis=-1, keepdims=True))
    return center * lax.rsqrt(spread + 1e-06)

def relative_bias(positions, table, grid):
    coord_y = positions // grid
    coord_x = positions % grid
    offset = (coord_y[:, None] - coord_y[None, :] + grid - 1) * (2 * grid - 1) + (coord_x[:, None] - coord_x[None, :] + grid - 1)
    return jnp.transpose(table[offset.astype(jnp.int32)], (2, 0, 1))

def one_sample(tokens_in, cond_in, positions, count, weights, heads, grid, precision):
    w_ada, w_qkv, w_proj, w_fc1, w_fc2, b_ada, b_qv, b_proj, b_fc1, b_fc2, rel_table = weights
    length = tokens_in.shape[0]
    width = tokens_in.shape[1]
    head_dim = width // heads
    cond_act = low(jax.nn.silu(cond_in))
    modulation = low_back(jnp.dot(cond_act[None, :], w_ada, precision=precision)[0] + b_ada)
    shift_attn, scale_attn, gate_attn, shift_mlp, scale_mlp, gate_mlp = jnp.split(modulation, 6)
    kept_rows = jnp.arange(length, dtype=jnp.int32) < count
    normed = low(normalize(tokens_in) * (1.0 + scale_attn) + shift_attn)
    qkv_bias = jnp.concatenate([b_qv[:width], jnp.zeros((width,), jnp.float32), b_qv[width:]])
    projected = low(low_back(jnp.dot(normed, w_qkv, precision=precision) + qkv_bias))
    split_heads = projected.reshape(length, 3, heads, head_dim)
    queries = jnp.transpose(split_heads[:, 0], (1, 0, 2))
    key_rows = jnp.transpose(split_heads[:, 1], (1, 0, 2))
    value_rows = jnp.transpose(split_heads[:, 2], (1, 0, 2))
    scores = jnp.einsum('hqe,hke->hqk', queries, key_rows, precision=precision) * head_dim ** (-0.5)
    scores = low_back(scores + relative_bias(positions, rel_table, grid))
    scores = jnp.where(kept_rows[None, None, :], scores, -1e+30)
    largest = lax.optimization_barrier(jnp.max(scores, axis=-1, keepdims=True))
    expo = jnp.exp(scores - largest)
    probs = low(expo / lax.optimization_barrier(jnp.sum(expo, axis=-1, keepdims=True)))
    mixed = jnp.einsum('hqk,hke->qhe', probs, value_rows, precision=precision).reshape(length, width)
    mixed = low(low_back(mixed))
    attended = low_back(jnp.dot(mixed, w_proj, precision=precision) + b_proj)
    middle = tokens_in + gate_attn * attended
    normed_two = low(normalize(middle) * (1.0 + scale_mlp) + shift_mlp)
    hidden_pre = low_back(jnp.dot(normed_two, w_fc1, precision=precision) + b_fc1)
    hidden = low(jax.nn.gelu(hidden_pre, approximate=True))
    branch = low_back(jnp.dot(hidden, w_fc2, precision=precision) + b_fc2)
    result = middle + gate_mlp * branch
    return jnp.where(kept_rows[:, None], result, 0.0)

def reference(tokens, condition, kept_index, kept_count, cotangent, w_ada, w_qkv, w_proj, w_fc1, w_fc2, b_ada, b_qv, b_proj, b_fc1, b_fc2, rel_table):
    total = N_STREAM * SAMPLES
    group = math.gcd(total, 16)
    ordinal = jnp.arange(L, dtype=jnp.int32)
    positions = jnp.stack([jnp.broadcast_to(ordinal, (SAMPLES, L)), kept_index.astype(jnp.int32)]).reshape(total // group, group, L)
    counts = jnp.stack([jnp.full((SAMPLES,), L, jnp.int32), kept_count.astype(jnp.int32)]).reshape(total // group, group)
    weights = tuple((item.astype(jnp.float32) for item in (w_ada, w_qkv, w_proj, w_fc1, w_fc2, b_ada, b_qv, b_proj, b_fc1, b_fc2, rel_table)))

    def forward(tokens_all, cond_all, weights_all):

        def per_sample(tok_one, cond_one, pos_one, count_one):
            return one_sample(tok_one, cond_one, pos_one, count_one, weights_all, HEADS, GRID, lax.Precision.HIGHEST)

        def run_group(packed):
            return jax.vmap(per_sample)(packed[0], packed[1], packed[2], packed[3])
        stacked = lax.map(jax.checkpoint(run_group), (tokens_all.reshape(total // group, group, L, D), cond_all.reshape(total // group, group, D), positions, counts))
        return stacked.reshape(N_STREAM, SAMPLES, L, D)
    output, pull = jax.vjp(forward, tokens.astype(jnp.float32), condition.astype(jnp.float32), weights)
    grad_tok, grad_cond, grad_weights = pull(cotangent.astype(jnp.float32))
    return (output.astype(jnp.bfloat16), grad_tok.astype(jnp.bfloat16), grad_cond, grad_weights[0], grad_weights[1], grad_weights[2], grad_weights[3], grad_weights[4], grad_weights[5], grad_weights[6], grad_weights[7], grad_weights[8], grad_weights[9], grad_weights[10])
```

```python
import math

import jax
import jax.numpy as jnp
from jax import lax
from jax.sharding import PartitionSpec as P

HEADS = 16
GRID = 16
BF = jnp.bfloat16
F32 = jnp.float32
HIGHEST = lax.Precision.HIGHEST


def swap(v, bit, n):
    return lax.ppermute(v, "dp", [(i, i ^ bit) for i in range(n)])


def swap_stream(v):
    return lax.ppermute(v, "stream", [(0, 1), (1, 0)])


def axis_bits(n):
    k = n.bit_length() - 1
    s = k // 3
    xs = [1 << i for i in range(s)]
    ys = [1 << (s + i) for i in range(s)]
    zs = [1 << i for i in range(2 * s, k)]
    return xs, ys, zs


def all_bits(n):
    return [1 << i for i in range(n.bit_length() - 1)]


def grow(v, bits, n):
    at = lax.axis_index("dp")
    for b in bits:
        r = swap(v, b, n)
        v = jnp.where((at & b) == 0, jnp.stack([v, r]), jnp.stack([r, v]))
    return v


def halves(v, b):
    up = (lax.axis_index("dp") & b) != 0
    return jnp.where(up, v[1], v[0]), jnp.where(up, v[0], v[1])


def shrink(v, bits, n):
    for b in bits:
        keep, send = halves(v, b)
        v = keep + swap(send, b, n)
    return v


def ordered(v, bits, n):
    lead = list(reversed(bits))
    want = sorted(bits, reverse=True)
    k = len(bits)
    v = jnp.transpose(v, [lead.index(b) for b in want] + list(range(k, v.ndim)))
    return v.reshape((n,) + v.shape[k:])


def unordered(v, bits, n):
    k = len(bits)
    want = sorted(bits, reverse=True)
    v = v.reshape((2,) * k + v.shape[1:])
    return jnp.transpose(v, [want.index(b) for b in bits] + list(range(k, v.ndim)))


def thirds(cols):
    t = cols // 128
    a = t // 3
    return a * 128, (a + (t - a) // 2) * 128


def gather_rows(v, n):
    xs, ys, zs = axis_bits(n)
    a, b = thirds(v.shape[1])
    zq = zs[::-1]
    p = ordered(grow(v[:, :a], xs + ys + zq, n), xs + ys + zq, n)
    q = grow(v[:, a:], zq, n)
    q1 = ordered(grow(q[..., : b - a], xs + ys, n), zq + xs + ys, n)
    q2 = ordered(grow(q[..., b - a :], ys + xs, n), zq + ys + xs, n)
    return jnp.concatenate([p, q1, q2], axis=-1).reshape(n * v.shape[0], v.shape[1])


def reduce_rows(v, n):
    xs, ys, zs = axis_bits(n)
    v = v.reshape((n, v.shape[0] // n, v.shape[1]))
    a, b = thirds(v.shape[2])
    yr, xr = ys[::-1], xs[::-1]
    o = zs + yr + xr
    p = shrink(unordered(v[..., :a], o, n), o, n)
    q1 = shrink(unordered(v[..., a:b], yr + xr + zs, n), yr + xr, n)
    q2 = shrink(unordered(v[..., b:], xr + yr + zs, n), xr + yr, n)
    q = shrink(jnp.concatenate([q1, q2], axis=-1), zs, n)
    return jnp.concatenate([p, q], axis=-1)


def gather_small(v, n):
    bits = all_bits(n)
    v = grow(v, bits, n)
    return v.reshape((n,) + v.shape[len(bits) :])


def reduce_small(v, n):
    bits = all_bits(n)[::-1]
    return shrink(v.reshape((2,) * len(bits) + v.shape[1:]), bits, n)


def trade_small(v, n):
    bits = all_bits(n)[::-1]
    k = len(bits)
    rest = list(v.shape[1:])
    v = v.reshape([2] * k + [1] + rest)
    at = lax.axis_index("dp")
    for i, b in enumerate(bits):
        keep, send = halves(v, b)
        got = swap(send, b, n)
        axis = k - 1 - i
        both = jnp.where(
            (at & b) == 0,
            jnp.stack([keep, got], axis=axis + 1),
            jnp.stack([got, keep], axis=axis + 1),
        )
        v = both.reshape(both.shape[:axis] + (2 * both.shape[axis],) + both.shape[axis + 2 :])
    return v


def sum_all(v, n):
    v = v + swap_stream(v)
    for b in all_bits(n):
        v = v + swap(v, b, n)
    return v


def mm(a, b):
    return lax.dot_general(a, b, (((1,), (0,)), ((), ())), preferred_element_type=F32)


def mm_nt(a, b):
    return lax.dot_general(a, b, (((1,), (1,)), ((), ())), preferred_element_type=F32)


def mm_tn(a, b):
    return lax.dot_general(a, b, (((0,), (0,)), ((), ())), preferred_element_type=F32)


def normal(v):
    center = v - jnp.mean(v, axis=-1, keepdims=True)
    inv = lax.rsqrt(jnp.mean(center * center, axis=-1, keepdims=True) + 1e-06)
    return center * inv, inv


def normal_back(g, n, inv):
    return inv * (g - jnp.mean(g, axis=-1, keepdims=True) - n * jnp.mean(g * n, axis=-1, keepdims=True))


def spread_mark():
    pair = lax.broadcasted_iota(jnp.int32, (2 * GRID - 1, GRID * GRID), 1)
    d = lax.broadcasted_iota(jnp.int32, (2 * GRID - 1, GRID * GRID), 0)
    return (pair // GRID - pair % GRID + GRID - 1 == d).astype(F32)


def bias_strip(table):
    w = 2 * GRID - 1
    t = jnp.transpose(table.reshape(w, w, HEADS), (2, 0, 1))[:, ::-1]
    x = lax.dot_general(t, spread_mark(), (((2,), (0,)), ((), ())), precision=HIGHEST)
    x = x.reshape(HEADS, w, GRID, GRID)
    return jnp.transpose(x, (0, 2, 1, 3)).reshape(HEADS, GRID, w * GRID)


def bias_full(strip):
    rows = [
        lax.slice_in_dim(strip, (GRID - 1 - y) * GRID, (2 * GRID - 1 - y) * GRID, axis=2)
        for y in range(GRID)
    ]
    return jnp.stack(rows, axis=1).reshape(HEADS, GRID * GRID, GRID * GRID)


def bias_back(ds):
    w = 2 * GRID - 1
    ds = ds.astype(F32).reshape(HEADS, GRID, GRID, GRID * GRID)
    total = 0.0
    for y in range(GRID):
        lo = (GRID - 1 - y) * GRID
        total = total + jnp.pad(ds[:, y], ((0, 0), (0, 0), (lo, (w - GRID) * GRID - lo)))
    x = jnp.transpose(total.reshape(HEADS, GRID, w, GRID), (0, 2, 1, 3)).reshape(HEADS, w, GRID * GRID)
    t = lax.dot_general(x, spread_mark(), (((2,), (1,)), ((), ())), precision=HIGHEST)
    return jnp.transpose(t[:, ::-1], (1, 2, 0)).reshape(w * w, HEADS)


def gelu_parts(x):
    k = math.sqrt(2.0 / math.pi)
    th = jnp.tanh(k * (x + 0.044715 * x * x * x))
    value = 0.5 * x * (1.0 + th)
    slope = 0.5 * (1.0 + th) + 0.5 * x * (1.0 - th * th) * k * (1.0 + 3 * 0.044715 * x * x)
    return value, slope


def local(
    n,
    tokens,
    condition,
    kept_index,
    kept_count,
    cotangent,
    w_ada,
    w_qkv,
    w_proj,
    w_fc1,
    w_fc2,
    b_ada,
    b_qv,
    b_proj,
    b_fc1,
    b_fc2,
    rel_table,
):
    side = lax.axis_index("stream")
    chip = lax.axis_index("dp")
    length, width = tokens.shape[2], tokens.shape[3]
    ff = w_fc1.shape[1]
    head_dim = width // HEADS
    scale = head_dim**-0.5
    rows = width // n
    cut = ff // (2 * n)
    first = side == 0

    wide = jnp.concatenate([w_qkv, w_proj], axis=1)
    a_shard = lax.dynamic_slice_in_dim(wide, side * 2 * width, 2 * width, axis=1)
    f1 = w_fc1.reshape(rows, n, 2, cut)
    b_shard = jnp.where(first, f1[:, :, 0], f1[:, :, 1]).reshape(rows, ff // 2)
    c_shard = lax.dynamic_slice_in_dim(w_fc2, side * cut, cut, axis=0)

    def both(own):
        other = swap_stream(own)
        return jnp.where(first, own, other), jnp.where(first, other, own)

    cond = condition[0, 0]
    sig = jax.nn.sigmoid(cond)
    cond_act = (cond * sig).astype(BF)
    acts = gather_small(cond_act, n)
    acts_part = lax.dynamic_slice_in_dim(acts, chip * rows, rows, axis=1)
    modulation = reduce_small(mm(acts_part, w_ada), n) + b_ada
    shift_attn, scale_attn, gate_attn, shift_mlp, scale_mlp, gate_mlp = [
        modulation[i * width : (i + 1) * width] for i in range(6)
    ]

    ordinal = jnp.arange(length, dtype=jnp.int32)
    count = jnp.where(first, length, kept_count[0])
    position = jnp.where(first, ordinal, kept_index[0])
    place = ((position[None, :] == ordinal[:, None]) & (ordinal[None, :] < count)).astype(BF)
    present = jnp.sum(place.astype(F32), axis=1) > 0.0
    x = mm(place, tokens[0, 0])
    cot = mm(place, cotangent[0, 0])

    strip = bias_strip(rel_table)
    bias = bias_full(strip)

    a0, a1 = both(gather_rows(a_shard, n))
    w_v, w_out = a1[:, :width], a1[:, width:]
    n1, inv1 = normal(x)
    normed = (n1 * (1.0 + scale_attn) + shift_attn).astype(BF)
    q = (mm(normed, a0[:, :width]) + b_qv[:width]).astype(BF)
    k = mm(normed, a0[:, width:]).astype(BF)
    v = (mm(normed, w_v) + b_qv[width:]).astype(BF)

    def heads(t):
        return jnp.transpose(t.reshape(length, HEADS, head_dim), (1, 0, 2))

    def flat(t):
        return jnp.transpose(t, (1, 0, 2)).reshape(length, width)

    def bmm(l, r, lc, rc):
        return lax.dot_general(l, r, (((lc,), (rc,)), ((0,), (0,))), preferred_element_type=F32)

    qh, kh, vh = heads(q), heads(k), heads(v)
    scores = bmm(qh, kh, 2, 2) * scale + bias
    scores = jnp.where(present[None, None, :], scores, -1e30)
    expo = jnp.exp(scores - jnp.max(scores, axis=-1, keepdims=True))
    soft = expo / jnp.sum(expo, axis=-1, keepdims=True)
    probs = soft.astype(BF)
    mixed = flat(bmm(probs, vh, 2, 1)).astype(BF)
    attended = mm(mixed, w_out) + b_proj
    middle = x + gate_attn * attended

    b0, b1 = both(gather_rows(b_shard, n))
    bias_f1 = b_fc1.reshape(n, 2, cut)
    n2, inv2 = normal(middle)
    normed_two = (n2 * (1.0 + scale_mlp) + shift_mlp).astype(BF)
    act0, slope0 = gelu_parts(mm(normed_two, b0) + bias_f1[:, 0].reshape(-1))
    act1, slope1 = gelu_parts(mm(normed_two, b1) + bias_f1[:, 1].reshape(-1))
    hid0, hid1 = act0.astype(BF), act1.astype(BF)

    c0, c1 = both(gather_rows(c_shard, n))
    branch = mm(hid0, c0) + mm(hid1, c1) + b_fc2
    result = middle + gate_mlp * branch
    out = jnp.where(present[:, None], result, 0.0).astype(BF)
    out_tokens = mm_tn(place, out).astype(BF)

    g_gate_mlp = jnp.sum(cot * branch, axis=0)
    g_branch = (cot * gate_mlp).astype(BF)

    def pair_rows(mine, theirs):
        return jnp.concatenate([mine, swap_stream(theirs)], axis=0)

    hid_mine = jnp.where(first, hid0, hid1)
    hid_theirs = jnp.where(first, hid1, hid0)
    g_branch2 = pair_rows(g_branch, g_branch)
    d_c = reduce_rows(mm_tn(pair_rows(hid_mine, hid_theirs), g_branch2).astype(BF), n)

    g_pre0 = (mm_nt(g_branch, c0) * slope0).astype(BF)
    g_pre1 = (mm_nt(g_branch, c1) * slope1).astype(BF)
    pre_mine = jnp.where(first, g_pre0, g_pre1)
    pre_theirs = jnp.where(first, g_pre1, g_pre0)
    normed_two2 = pair_rows(normed_two, normed_two)
    d_b = reduce_rows(mm_tn(normed_two2, pair_rows(pre_mine, pre_theirs)).astype(BF), n)

    g_n2 = mm_nt(g_pre0, b0) + mm_nt(g_pre1, b1)
    g_shift_mlp = jnp.sum(g_n2, axis=0)
    g_scale_mlp = jnp.sum(g_n2 * n2, axis=0)
    g_middle = cot + normal_back(g_n2 * (1.0 + scale_mlp), n2, inv2)
    g_gate_attn = jnp.sum(g_middle * attended, axis=0)
    g_att = (g_middle * gate_attn).astype(BF)

    g_mixed = heads(mm_nt(g_att, w_out).astype(BF))
    g_v = flat(bmm(probs, g_mixed, 1, 1)).astype(BF)
    g_probs = bmm(g_mixed, vh, 2, 2)
    g_scores = (soft * (g_probs - jnp.sum(g_probs * soft, axis=-1, keepdims=True))).astype(BF)
    g_q = (flat(bmm(g_scores, kh, 2, 1)) * scale).astype(BF)
    g_k = (flat(bmm(g_scores, qh, 1, 1)) * scale).astype(BF)

    l_mine = jnp.where(first, normed, mixed)
    l_theirs = jnp.where(first, mixed, normed)
    g1_mine, g1_theirs = jnp.where(first, g_q, g_v), jnp.where(first, g_v, g_q)
    g2_mine, g2_theirs = jnp.where(first, g_k, g_att), jnp.where(first, g_att, g_k)
    d_a = jnp.concatenate(
        [
            mm_tn(pair_rows(normed, normed), pair_rows(g1_mine, g1_theirs)),
            mm_tn(pair_rows(l_mine, l_theirs), pair_rows(g2_mine, g2_theirs)),
        ],
        axis=1,
    ).astype(BF)
    d_a = reduce_rows(d_a, n)

    g_n1 = mm_nt(g_q, a0[:, :width]) + mm_nt(g_k, a0[:, width:]) + mm_nt(g_v, w_v)
    g_shift_attn = jnp.sum(g_n1, axis=0)
    g_scale_attn = jnp.sum(g_n1 * n1, axis=0)
    g_x = g_middle + normal_back(g_n1 * (1.0 + scale_attn), n1, inv1)
    grad_tokens = mm_tn(place, g_x.astype(BF)).astype(BF)

    g_mod = jnp.concatenate(
        [g_shift_attn, g_scale_attn, g_gate_attn, g_shift_mlp, g_scale_mlp, g_gate_mlp]
    ).astype(BF)
    g_mods = gather_small(g_mod, n)
    g_mods_twin = swap_stream(g_mods)
    acts_twin = swap_stream(acts_part)
    grad_w_ada = mm_tn(acts_part, g_mods) + mm_tn(acts_twin, g_mods_twin)
    own_sum, twin_sum = (jnp.sum(t.astype(F32), axis=0) for t in (g_mods, g_mods_twin))
    grad_b_ada = own_sum + twin_sum
    g_acts = trade_small(mm_nt(g_mods, w_ada), n).reshape(width)
    grad_condition = g_acts * sig * (1.0 + cond * (1.0 - sig))

    def col_sum(t):
        return jnp.sum(t.astype(F32), axis=0)

    pre_sum = jnp.stack([col_sum(g_pre0).reshape(n, cut), col_sum(g_pre1).reshape(n, cut)], axis=1)
    smalls = [
        col_sum(g_q),
        col_sum(g_v),
        col_sum(g_att),
        pre_sum.reshape(-1),
        col_sum(g_branch),
        bias_back(g_scores).reshape(-1),
    ]
    sizes = [t.shape[0] for t in smalls]
    packed = jnp.concatenate(smalls)
    pad = -packed.shape[0] % 1024
    packed = sum_all(jnp.pad(packed, (0, pad)).reshape(-1, 128), n).reshape(-1)
    parts, at = [], 0
    for s in sizes:
        parts.append(packed[at : at + s])
        at += s

    d_a0, d_a1 = both(d_a)
    d_b0, d_b1 = both(d_b)
    d_c0, d_c1 = both(d_c)
    grad_w_qkv = jnp.concatenate([d_a0, d_a1[:, :width]], axis=1).astype(F32)
    grad_w_proj = d_a1[:, width:].astype(F32)
    grad_w_fc1 = (
        jnp.stack([d_b0.reshape(rows, n, cut), d_b1.reshape(rows, n, cut)], axis=2)
        .reshape(rows, ff)
        .astype(F32)
    )
    grad_w_fc2 = jnp.concatenate([d_c0, d_c1], axis=0).astype(F32)
    return (
        out_tokens[None, None],
        grad_tokens[None, None],
        grad_condition[None, None],
        grad_w_ada,
        grad_w_qkv,
        grad_w_proj,
        grad_w_fc1,
        grad_w_fc2,
        grad_b_ada,
        jnp.concatenate(parts[:2]),
        parts[2],
        parts[3],
        parts[4],
        parts[5].reshape(rel_table.shape),
    )


def solution(mesh):
    n = mesh.shape["dp"]

    def body(*args):
        return local(n, *args)

    return jax.shard_map(
        body,
        mesh=mesh,
        in_specs=(
            P("stream", "dp", None, None),
            P("stream", "dp", None),
            P("dp", None),
            P("dp"),
            P("stream", "dp", None, None),
            P("dp", None),
            P("dp", None),
            P("dp", None),
            P("dp", None),
            P("dp", None),
            P(),
            P(),
            P(),
            P(),
            P(),
            P(),
        ),
        out_specs=(
            P("stream", "dp", None, None),
            P("stream", "dp", None, None),
            P("stream", "dp", None),
            P("dp", None),
            P("dp", None),
            P("dp", None),
            P("dp", None),
            P("dp", None),
            P(),
            P(),
            P(),
            P(),
            P(),
            P(),
        ),
        check_vma=False,
    )
```

```python
import functools
import math

import jax
import jax.numpy as jnp
from jax import lax
from jax.experimental import pallas as pl
from jax.experimental.pallas import tpu as pltpu
from jax.sharding import PartitionSpec as P

HEADS = 16
GRID = 16
BF = jnp.bfloat16
F32 = jnp.float32


def swap(v, bit, n):
    return lax.ppermute(v, "dp", [(i, i ^ bit) for i in range(n)])


def swap_stream(v):
    return lax.ppermute(v, "stream", [(0, 1), (1, 0)])


def axis_bits(n):
    k = n.bit_length() - 1
    s = k // 3
    xs = [1 << i for i in range(s)]
    ys = [1 << (s + i) for i in range(s)]
    zs = [1 << i for i in range(2 * s, k)]
    return xs, ys, zs


def all_bits(n):
    return [1 << i for i in range(n.bit_length() - 1)]


def orders_out(n):
    xs, ys, zs = axis_bits(n)
    near = zs[:1]
    return zs[1:][::-1], (near + ys + xs, xs + near + ys, ys + xs + near)


def trade(v):
    return lax.all_to_all(v, "dp", 0, 0, tiled=True)


def mm(a, b):
    return lax.dot_general(a, b, (((1,), (0,)), ((), ())), preferred_element_type=F32)


def mm_nt(a, b):
    return lax.dot_general(a, b, (((1,), (1,)), ((), ())), preferred_element_type=F32)


def mm_tn(a, b):
    return lax.dot_general(a, b, (((0,), (0,)), ((), ())), preferred_element_type=F32)


def normal(v):
    center = v - jnp.mean(v, axis=-1, keepdims=True)
    inv = lax.rsqrt(jnp.mean(center * center, axis=-1, keepdims=True) + 1e-06)
    return center * inv, inv


def normal_back(g, n, inv):
    return inv * (g - jnp.mean(g, axis=-1, keepdims=True) - n * jnp.mean(g * n, axis=-1, keepdims=True))


def bias_windows(table):
    w = 2 * GRID - 1
    t = jnp.transpose(table.reshape(w, w, HEADS)[::-1, ::-1], (2, 0, 1))
    t = jnp.pad(t, ((0, 0), (0, 1), (0, 1))).reshape(HEADS, w + 1, 2, GRID)
    return t[:, :, 0].reshape(HEADS, -1), t[:, :, 1].reshape(HEADS, -1)


def table_of(lo, hi):
    w = 2 * GRID - 1
    t = jnp.stack([lo.reshape(HEADS, w + 1, GRID), hi.reshape(HEADS, w + 1, GRID)], axis=2)
    t = t.reshape(HEADS, w + 1, 2 * GRID)[:, :w, :w]
    return jnp.transpose(t, (1, 2, 0))[::-1, ::-1].reshape(w * w, HEADS)


def gelu_parts(x):
    k = math.sqrt(2.0 / math.pi)
    th = jnp.tanh(k * (x + 0.044715 * x * x * x))
    value = 0.5 * x * (1.0 + th)
    slope = 0.5 * (1.0 + th) + 0.5 * x * (1.0 - th * th) * k * (1.0 + 3 * 0.044715 * x * x)
    return value, slope


VMEM_BYTES = 56 * 1024 * 1024
SUM_ROWS = 200
WHOLE = pl.BlockSpec(memory_space=pltpu.VMEM)
HBM = pl.BlockSpec(memory_space=pl.ANY)
SCALAR = pl.BlockSpec(memory_space=pltpu.SMEM)


def shape(dims, dtype):
    return jax.ShapeDtypeStruct(dims, dtype)


def params():
    return pltpu.CompilerParams(vmem_limit_bytes=VMEM_BYTES)


def cost(flops, size):
    return pl.CostEstimate(flops=int(flops), bytes_accessed=int(size), transcendentals=0)


def strips(total, tile, body):
    def step(i, carry):
        body(pl.multiple_of(i * tile, tile))
        return carry

    lax.fori_loop(0, total // tile, step, 0)


def fetch_halves(side_ref, own_ref, other_ref, w_ref, sem):
    side = side_ref[0]
    mine = pltpu.make_async_copy(own_ref, w_ref.at[side], sem.at[side])
    twin = pltpu.make_async_copy(other_ref, w_ref.at[1 - side], sem.at[1 - side])
    mine.start()
    twin.start()

    def wait(slot):
        pltpu.make_async_copy(own_ref, w_ref.at[slot], sem.at[slot]).wait()

    return wait


def pieces(n, rows, cut, s):
    half = cut // 2
    for part in range(2):
        for k in range(n):
            yield (k * 2 + s) * cut + part * half, (part * n + k) * half, half


def fc1_rows_kernel(n, side_ref, own_ref, other_ref, out_ref):
    rows, ff = out_ref.shape
    cut = ff // (2 * n)
    for s in range(2):

        @pl.when(side_ref[0] == s)
        def _():
            for half, ref in ((s, own_ref), (1 - s, other_ref)):
                for src, dst, w in pieces(n, rows, cut, half):
                    out_ref[:, src : src + w] = ref[:, dst : dst + w]


def fc1_rows(n, side, own, other):
    return pl.pallas_call(
        functools.partial(fc1_rows_kernel, n),
        out_shape=shape((own.shape[0], 2 * own.shape[1]), F32),
        in_specs=[SCALAR, WHOLE, WHOLE],
        out_specs=WHOLE,
        compiler_params=params(),
        name="fc1_rows",
    )(side, own, other)


def strip_kernel(lo_ref, hi_ref, out_ref):
    lanes = lo_ref.shape[1]
    lo, hi = lo_ref[...], hi_ref[...]
    j = lax.broadcasted_iota(jnp.int32, lo.shape, 1) % GRID
    for i in range(GRID):
        k = GRID - 1 - i
        a = pltpu.roll(lo, lanes - k, 1) if k else lo
        out_ref[:, i, :] = jnp.where(j < GRID - k, a, pltpu.roll(hi, GRID - k, 1))


def bias_strip(table):
    lo, hi = bias_windows(table)
    return pl.pallas_call(
        strip_kernel,
        out_shape=shape((HEADS, GRID, lo.shape[1]), F32),
        in_specs=[WHOLE, WHOLE],
        out_specs=WHOLE,
        name="bias_strip",
    )(lo, hi)


def bias_of(strip):
    return jnp.concatenate(
        [strip[:, (GRID - 1 - y) * GRID : (2 * GRID - 1 - y) * GRID] for y in range(GRID)], axis=0
    )


def put(i, pos):
    return (i >> pos) << (pos + 1) | (i & ((1 << pos) - 1))


def attn_shard_kernel(side_ref, qkv_ref, proj_ref, out_ref):
    width = proj_ref.shape[1]
    for s in range(2):

        @pl.when(side_ref[0] == s)
        def _():
            if s == 0:
                out_ref[0] = qkv_ref[:, 0 : 2 * width]
            else:
                out_ref[0, :, 0:width] = qkv_ref[:, 2 * width :]
                out_ref[0, :, width:] = proj_ref[...]


def mlp_shard_kernel(n, side_ref, f1_ref, f2_ref, *rest):
    out_ref = rest[-1]
    rows, ff = f1_ref.shape
    width = f2_ref.shape[1]
    cut = ff // (2 * n)
    for s in range(2):

        @pl.when(side_ref[0] == s)
        def _():
            for src, dst, w in pieces(n, rows, cut, s):
                out_ref[0, :, dst : dst + w] = f1_ref[:, src : src + w]
            for part in range(2):
                lo = s * cut + part * rows
                cols = slice(ff // 2 + part * width, ff // 2 + (part + 1) * width)
                out_ref[0, :, cols] = f2_ref[lo : lo + rows, :]


def mlp_shard(n, side, f1, f2, after=()):
    return pl.pallas_call(
        functools.partial(mlp_shard_kernel, n),
        out_shape=shape((1,) + f1.shape, BF),
        in_specs=[SCALAR, WHOLE, WHOLE] + [HBM] * len(after),
        out_specs=WHOLE,
        compiler_params=params(),
        name="mlp_shard",
    )(side, f1, f2, *after)


def attn_shard(side, w_qkv, w_proj):
    rows, width = w_proj.shape
    return pl.pallas_call(
        attn_shard_kernel,
        out_shape=shape((1, rows, 2 * width), BF),
        in_specs=[SCALAR, WHOLE, WHOLE],
        out_specs=WHOLE,
        compiler_params=params(),
        name="attn_shard",
    )(side, w_qkv, w_proj)


def join_kernel(jobs, chip_ref, *refs):
    outs = refs[-sum(len(cols) for _, cols in jobs) :]
    at = 0
    for k, (bit, cols) in enumerate(jobs):
        v_ref, r_ref = refs[2 * k], refs[2 * k + 1]
        m = v_ref.shape[0]
        up = (chip_ref[0] & bit) // bit
        lo = 0
        for c in cols:
            for i in range(m):
                outs[at][up * m + i] = v_ref[i, :, lo : lo + c]
                outs[at][(1 - up) * m + i] = r_ref[i, :, lo : lo + c]
            lo += c
            at += 1


def join(chip, jobs, after=()):
    flat = [t for v, r, _, _ in jobs for t in (v, r)]
    return pl.pallas_call(
        functools.partial(join_kernel, [(bit, cols) for _, _, bit, cols in jobs]),
        out_shape=tuple(
            shape((2 * v.shape[0], v.shape[1], c), v.dtype) for v, _, _, cols in jobs for c in cols
        ),
        in_specs=[SCALAR] + [WHOLE] * len(flat) + [HBM] * len(after),
        out_specs=(WHOLE,) * sum(len(cols) for _, _, _, cols in jobs),
        compiler_params=params(),
        name="join",
    )(chip, *flat, *after)


def assemble_kernel(orders, chip_ref, *refs):
    out_ref = refs[-1]
    lo = 0
    for k, bits in enumerate(orders):
        v_ref, r_ref = refs[2 * k], refs[2 * k + 1]
        m, _, c = v_ref.shape
        last = bits[-1]
        up = (chip_ref[0] & last) // last
        lead = bits[:-1][::-1]
        for i in range(m):
            base = sum(b for j, b in enumerate(lead) if (i >> (len(lead) - 1 - j)) & 1)
            out_ref[base + up * last, :, lo : lo + c] = v_ref[i]
            out_ref[base + (1 - up) * last, :, lo : lo + c] = r_ref[i]
        lo += c


def assemble(chip, orders, pairs, after=()):
    flat = [t for pair in pairs for t in pair]
    m, rows, _ = flat[0].shape
    cols = sum(v.shape[2] for v, _ in pairs)
    out = pl.pallas_call(
        functools.partial(assemble_kernel, orders),
        out_shape=shape((2 * m, rows, cols), BF),
        in_specs=[SCALAR] + [WHOLE] * len(flat) + [HBM] * len(after),
        out_specs=WHOLE,
        compiler_params=params(),
        name="assemble",
    )(chip, *flat, *after)
    return out.reshape(2 * m * rows, cols)


class Gathering:
    def __init__(self, chip, v, n):
        first, parts = orders_out(n)
        self.chip, self.n = chip, n
        self.orders = [first + part for part in parts]
        self.turn, self.cut_at = 0, len(first)
        self.parts = [v]
        self.exchange()

    def exchange(self):
        self.came = [swap(v, self.orders[k][self.turn], self.n) for k, v in enumerate(self.parts)]
        self.turn += 1

    def step(self, *after):
        jobs = []
        for k, (v, r) in enumerate(zip(self.parts, self.came)):
            c = v.shape[2]
            cut = (c // 3,) * 3 if self.turn == self.cut_at else (c,)
            jobs.append((v, r, self.orders[k][self.turn - 1], cut))
        self.parts = list(join(self.chip, jobs, after))
        self.exchange()
        return tuple(self.parts)

    def done(self):
        return self.turn == len(self.orders[0])

    def result(self, *after):
        return assemble(self.chip, self.orders, tuple(zip(self.parts, self.came)), after=after)


def product_kernel(n, firsts, steps, half_step, count, chip_ref, l0_ref, l1_ref, *rest):
    turned_ref = rest[-1]
    r_refs = rest[:count]
    outs = rest[-7:-1]
    t = pl.program_id(0)
    length = l0_ref.shape[0]
    width = turned_ref.shape[1]
    rows = width // n

    @pl.when(t == 0)
    def _():
        for k in range(turned_ref.shape[0]):
            cols = slice(k * width, (k + 1) * width)
            turned_ref[k, :, 0:length] = l0_ref[:, cols].T
            turned_ref[k, :, length:] = l1_ref[:, cols].T

    slot = jnp.where(t >= half_step, turned_ref.shape[0] - 1, 0)
    value, at = 0.0, 0
    for r_ref in r_refs:
        rows_here = r_ref.shape[0]
        value = value + mm(turned_ref[slot, :, at : at + rows_here], r_ref[...])
        at += rows_here
    for part, (bit, (lo, hi)) in enumerate(zip(firsts, steps)):
        pos = bit.bit_length() - 1
        for up in range(2):

            @pl.when((t >= lo) & (t < hi) & ((chip_ref[0] & bit) // bit == up))
            def _():
                for i in range(n // 2):
                    at = put(i, pos)
                    for goes, ref in ((up, outs[2 * part]), (1 - up, outs[2 * part + 1])):
                        k = at + goes * bit
                        ref[i] = value[k * rows : (k + 1) * rows].astype(BF)


def product(chip, l0, l1, r0, r1, width, n, firsts, after=()):
    length = l0.shape[0]
    tile = width // 3
    per = width // tile
    rights = (r0,) + (r1 if isinstance(r1, tuple) else (r1,))
    two_l, two_r = l0.shape[1] > width, r0.shape[1] > width
    cols = (2 * width // 3,) * 3
    steps = []
    for c in cols:
        lo = steps[-1][1] if steps else 0
        steps.append((lo, lo + c // tile))
    left = pl.BlockSpec(l0.shape, lambda t: (0, 0))
    right = [pl.BlockSpec((r.shape[0], tile), lambda t: (0, t if two_r else t % per)) for r in rights]
    spec = lambda lo, hi: pl.BlockSpec(
        (n // 2, width // n, tile), lambda t: (0, 0, jnp.clip(t - lo, 0, hi - lo - 1))
    )
    out = pl.pallas_call(
        functools.partial(product_kernel, n, firsts, steps, per, len(rights)),
        grid=(2 * per,),
        out_shape=tuple(shape((n // 2, width // n, c), BF) for c in cols for _ in range(2)),
        in_specs=[SCALAR, left, left] + right + [HBM] * len(after),
        out_specs=tuple(spec(*s) for s in steps for _ in range(2)),
        scratch_shapes=[pltpu.VMEM((1 + two_l, width, 2 * length), BF)],
        compiler_params=params(),
        cost_estimate=cost(8 * length * width * width, 12e6),
        name="product",
    )(chip, l0, l1, *rights, *after)
    return tuple((out[2 * k], out[2 * k + 1]) for k in range(3))


def split_kernel(jobs, chip_ref, *refs):
    outs = refs[-2 * len(jobs) :]
    at = 0
    for k, (bit, pos, count) in enumerate(jobs):
        keep_ref, send_ref = outs[2 * k], outs[2 * k + 1]
        up = (chip_ref[0] & bit) // bit
        lo = 0
        for _ in range(count):
            v_ref, r_ref = refs[at], refs[at + 1]
            at += 2
            c = v_ref.shape[2]
            for i in range(keep_ref.shape[0]):
                for out_ref, goes in ((send_ref, 1 - up), (keep_ref, up)):
                    j = put(i, pos) + goes * (1 << pos)
                    total = v_ref[j].astype(F32) + r_ref[j].astype(F32)
                    out_ref[i, :, lo : lo + c] = total.astype(BF)
            lo += c


def split(chip, jobs, after=()):
    flat = [t for pairs, _, _ in jobs for pair in pairs for t in pair]
    outs, plan = [], []
    for pairs, bit, left in jobs:
        m, rows, _ = pairs[0][0].shape
        cols = sum(v.shape[2] for v, _ in pairs)
        outs += [shape((m // 2, rows, cols), BF)] * 2
        plan.append((bit, len(left) - 1 - left.index(bit), len(pairs)))
    out = pl.pallas_call(
        functools.partial(split_kernel, plan),
        out_shape=tuple(outs),
        in_specs=[SCALAR] + [WHOLE] * len(flat) + [HBM] * len(after),
        out_specs=(WHOLE,) * len(outs),
        compiler_params=params(),
        name="split",
    )(chip, *flat, *after)
    return [(out[2 * k], out[2 * k + 1]) for k in range(len(jobs))]


def finish_kernel(v_ref, r_ref, *rest):
    rest[-1][...] = v_ref[0].astype(F32) + r_ref[0].astype(F32)


def finish(v, r, after=()):
    return pl.pallas_call(
        finish_kernel,
        out_shape=shape(v.shape[1:], F32),
        in_specs=[WHOLE] * 2 + [HBM] * len(after),
        out_specs=WHOLE,
        compiler_params=params(),
        name="finish",
    )(v, r, *after)


def meet_kernel(bit, rows, chip_ref, v_ref, r_ref, *rest):
    out_ref = rest[-1]
    out_ref[0:SUM_ROWS, :] = v_ref[0:SUM_ROWS, :] + r_ref[0:SUM_ROWS, :]
    up = (chip_ref[0] & bit) // bit
    for i in range((v_ref.shape[0] - SUM_ROWS) // rows):
        src = slice(SUM_ROWS + i * rows, SUM_ROWS + (i + 1) * rows)
        for ref, side in ((v_ref, up), (r_ref, 1 - up)):
            at = pl.multiple_of(SUM_ROWS + (2 * i + side) * rows, 8)
            out_ref[pl.ds(at, rows), :] = ref[src, :]


def meet(chip, v, r, bit, rows, after=()):
    total = 2 * v.shape[0] - SUM_ROWS
    return pl.pallas_call(
        functools.partial(meet_kernel, bit, rows),
        out_shape=shape((total, v.shape[1]), F32),
        in_specs=[SCALAR, WHOLE, WHOLE] + [HBM] * len(after),
        out_specs=WHOLE,
        compiler_params=params(),
        name="meet",
    )(chip, v, r, *after)


class Reduction:
    def __init__(self, chip, parts, n):
        last, orders = orders_out(n)
        self.chip, self.n = chip, n
        self.orders = [part[::-1] for part in orders]
        self.tail = last[::-1]
        self.left = [all_bits(n)[::-1] for _ in range(3)]
        self.pairs = [
            (keep, self.exchange(k, self.orders[k].pop(0), send)) for k, (keep, send) in enumerate(parts)
        ]

    def exchange(self, k, bit, send):
        self.left[k] = [b for b in self.left[k] if b != bit]
        return swap(send, bit, self.n)

    def plan(self):
        chains = [[k] for k in range(len(self.pairs))]
        if len(self.pairs) == 3 and not self.orders[0]:
            chains = [[0, 1, 2]]
            self.orders = [list(self.tail)]
        bits = [self.orders[chain[0]].pop(0) for chain in chains]
        return [
            ([self.pairs[j] for j in chain], bit, list(self.left[chain[0]]))
            for chain, bit in zip(chains, bits)
        ]

    def go(self, jobs, outs):
        self.pairs = [
            (keep, self.exchange(k, bit, send))
            for k, ((_, bit, _), (keep, send)) in enumerate(zip(jobs, outs))
        ]

    def done(self):
        return len(self.pairs) == 1 and not self.orders[0]

    def result(self, *after):
        return finish(*self.pairs[0], after)


def step(sums, *after):
    plans = [s.plan() for s in sums]
    outs = split(sums[0].chip, [job for jobs in plans for job in jobs], after)
    kept = tuple(keep for keep, _ in outs)
    for s, jobs in zip(sums, plans):
        s.go(jobs, outs[: len(jobs)])
        outs = outs[len(jobs) :]
    return kept


def fc2_rows_kernel(side_ref, own_ref, other_ref, out_ref):
    rows = own_ref.shape[0]
    width = out_ref.shape[1]
    for s in range(2):

        @pl.when(side_ref[0] == s)
        def _():
            for half, ref in ((s, own_ref), (1 - s, other_ref)):
                for part in range(2):
                    lo = (2 * half + part) * rows
                    out_ref[lo : lo + rows, :] = ref[:, part * width : (part + 1) * width]


def fc2_rows(side, own, other):
    return pl.pallas_call(
        fc2_rows_kernel,
        out_shape=shape((4 * own.shape[0], own.shape[1] // 2), F32),
        in_specs=[SCALAR, WHOLE, WHOLE],
        out_specs=WHOLE,
        compiler_params=params(),
        name="fc2_rows",
    )(side, own, other)


def attn_rows_kernel(side_ref, own_ref, other_ref, qkv_ref, proj_ref):
    width = proj_ref.shape[1]
    for s in range(2):

        @pl.when(side_ref[0] == s)
        def _():
            low, high = (own_ref, other_ref) if s == 0 else (other_ref, own_ref)
            qkv_ref[:, 0 : 2 * width] = low[...]
            qkv_ref[:, 2 * width :] = high[:, 0:width]
            proj_ref[...] = high[:, width:]


def attn_rows(side, own, other):
    rows, width = own.shape[0], own.shape[1] // 2
    return pl.pallas_call(
        attn_rows_kernel,
        out_shape=(shape((rows, 3 * width), F32), shape((rows, width), F32)),
        in_specs=[SCALAR, WHOLE, WHOLE],
        out_specs=(WHOLE, WHOLE),
        compiler_params=params(),
        name="attn_rows",
    )(side, own, other)


def hold_kernel(*refs):
    pass


def hold(values, *after):
    many = isinstance(values, tuple)
    values = values if many else (values,)
    out = pl.pallas_call(
        hold_kernel,
        out_shape=tuple(shape(v.shape, v.dtype) for v in values),
        in_specs=[HBM] * (len(values) + len(after)),
        out_specs=(HBM,) * len(values),
        input_output_aliases={k: k for k in range(len(values))},
        name="hold",
    )(*values, *after)
    return out if many else out[0]


def attention_kernel(
    side_ref,
    own_ref,
    other_ref,
    normed_ref,
    bqv_ref,
    strip_ref,
    keep_ref,
    x_ref,
    mod_ref,
    bproj_ref,
    qh_ref,
    kh_ref,
    vh_ref,
    mine_ref,
    theirs_ref,
    attended_ref,
    middle_ref,
    normed_two_ref,
    w_ref,
    flat_ref,
    mix_ref,
    sem,
):
    length, width = x_ref.shape
    hd = width // HEADS
    tile = 384
    wait = fetch_halves(side_ref, own_ref, other_ref, w_ref, sem)
    normed = normed_ref[...]

    def project(slot, lo, cols, at, bias_at):
        def body(o):
            y = mm(normed, w_ref[slot, :, pl.ds(lo + o, tile)])
            if bias_at is not None:
                y = y + bqv_ref[:, pl.ds(bias_at + o, tile)]
            flat_ref[:, pl.ds(at + o, tile)] = y.astype(BF)

        strips(cols, tile, body)

    wait(0)
    project(0, 0, width, 0, 0)
    project(0, width, width, width, None)
    wait(1)
    project(1, 0, width, 2 * width, width)
    for h in range(HEADS):
        qh_ref[h] = flat_ref[:, h * hd : (h + 1) * hd]
        kh_ref[h] = flat_ref[:, width + h * hd : width + (h + 1) * hd]
        vh_ref[h] = flat_ref[:, 2 * width + h * hd : 2 * width + (h + 1) * hd]
    keep = keep_ref[...] > 0.0

    def head(h, carry):
        sc = mm_nt(qh_ref[h], kh_ref[h]) * (hd**-0.5) + bias_of(strip_ref[h])
        sc = jnp.where(keep, sc, -1e30)
        ex = jnp.exp(sc - jnp.max(sc, axis=-1, keepdims=True))
        soft = ex / jnp.sum(ex, axis=-1, keepdims=True)
        mix_ref[h] = mm(soft.astype(BF), vh_ref[h]).astype(BF)
        return carry

    lax.fori_loop(0, HEADS, head, 0)
    for h in range(HEADS):
        flat_ref[:, h * hd : (h + 1) * hd] = mix_ref[h]
    mixed = flat_ref[:, 0:width]
    mine_ref[:, 0:width] = normed
    theirs_ref[:, 0:width] = normed
    for s, (normed_at, mixed_at) in enumerate(((mine_ref, theirs_ref), (theirs_ref, mine_ref))):

        @pl.when(side_ref[0] == s)
        def _():
            normed_at[:, width:] = normed
            mixed_at[:, width:] = mixed

    def out(o):
        y = mm(mixed, w_ref[1, :, pl.ds(width + o, tile)]) + bproj_ref[:, pl.ds(o, tile)]
        attended_ref[:, pl.ds(o, tile)] = y

    strips(width, tile, out)
    middle = x_ref[...] + mod_ref[2:3, :] * attended_ref[...]
    middle_ref[...] = middle
    n2, _ = normal(middle)
    normed_two_ref[...] = (n2 * (1.0 + mod_ref[4:5, :]) + mod_ref[3:4, :]).astype(BF)


def attention(side, own, other, normed, b_qv, bias, keep, x, mod, b_proj):
    length, width = x.shape
    hd = width // HEADS
    per_head = shape((HEADS, length, hd), BF)
    return pl.pallas_call(
        attention_kernel,
        out_shape=(
            per_head,
            per_head,
            per_head,
            shape((length, 2 * width), BF),
            shape((length, 2 * width), BF),
            shape((length, width), F32),
            shape((length, width), F32),
            shape((length, width), BF),
        ),
        in_specs=[SCALAR, HBM, HBM] + [WHOLE] * 7,
        out_specs=(WHOLE,) * 8,
        scratch_shapes=[
            pltpu.VMEM((2, width, 2 * width), BF),
            pltpu.VMEM((length, 3 * width), BF),
            pltpu.VMEM((HEADS, length, hd), BF),
            pltpu.SemaphoreType.DMA((2,)),
        ],
        compiler_params=params(),
        cost_estimate=cost(8 * length * width * width + 4 * length * length * width, 24e6),
        name="attention",
    )(side, own, other, normed, b_qv, bias, keep, x, mod, b_proj)


def mlp_half(normed_two_ref, b_ref, c_ref, bf1_ref, hid_ref, slope_ref):
    act, slope = gelu_parts(mm(normed_two_ref[...], b_ref[...]) + bf1_ref[...])
    hid = act.astype(BF)
    hid_ref[...] = hid
    slope_ref[...] = slope
    return mm(hid, c_ref[...])


def mlp_first_kernel(normed_two_ref, b_ref, c_ref, bf1_ref, hid_ref, slope_ref, part_ref):
    total = mlp_half(normed_two_ref, b_ref, c_ref, bf1_ref, hid_ref, slope_ref)

    @pl.when(pl.program_id(0) == 0)
    def _():
        part_ref[...] = total

    @pl.when(pl.program_id(0) > 0)
    def _():
        part_ref[...] += total


def mlp_last_kernel(
    normed_two_ref,
    b_ref,
    c_ref,
    bf1_ref,
    part_ref,
    bf2_ref,
    middle_ref,
    cot_ref,
    mod_ref,
    place_ref,
    present_ref,
    hid_ref,
    slope_ref,
    g_branch_ref,
    out_ref,
    sums_ref,
    acc_ref,
):
    t = pl.program_id(0)
    total = mlp_half(normed_two_ref, b_ref, c_ref, bf1_ref, hid_ref, slope_ref)

    @pl.when(t == 0)
    def _():
        acc_ref[...] = part_ref[...] + total

    @pl.when(t > 0)
    def _():
        acc_ref[...] += total

    @pl.when(t == pl.num_programs(0) - 1)
    def _():
        branch = acc_ref[...] + bf2_ref[...]
        cot = cot_ref[...]
        gate = mod_ref[5:6, :]
        result = middle_ref[...] + gate * branch
        out = jnp.where(present_ref[...] > 0.0, result, 0.0).astype(BF)
        out_ref[...] = mm_tn(place_ref[...], out).astype(BF)
        g_branch = (cot * gate).astype(BF)
        g_branch_ref[...] = g_branch
        sums_ref[0:1, :] = jnp.sum(cot * branch, axis=0, keepdims=True)
        sums_ref[1:2, :] = jnp.sum(g_branch.astype(F32), axis=0, keepdims=True)


def mlp(normed_two, weights, bf1, last=None):
    length, width = normed_two.shape
    half = weights.shape[1] // 2
    tile = 384
    fixed = lambda a: pl.BlockSpec(a.shape, lambda t: (0, 0))
    cols = lambda r: pl.BlockSpec((r, tile), lambda t: (0, t))
    per = width // tile
    rows = pl.BlockSpec((tile, width), lambda t: (t % per, half // width + t // per))
    whole = lambda r: pl.BlockSpec((r, width), lambda t: (0, 0))
    more = last or ()
    outs = [shape((length, half), BF), shape((length, half), F32)]
    if last:
        outs += [shape((length, width), BF), shape((length, width), BF), shape((8, width), F32)]
    else:
        outs += [shape((length, width), F32)]
    return pl.pallas_call(
        mlp_last_kernel if last else mlp_first_kernel,
        grid=(half // tile,),
        out_shape=tuple(outs),
        in_specs=[fixed(normed_two), cols(width), rows, cols(1)] + [fixed(a) for a in more],
        out_specs=tuple([cols(length), cols(length)] + [whole(o.shape[0]) for o in outs[2:]]),
        scratch_shapes=[pltpu.VMEM((length, width), F32)] if last else [],
        compiler_params=params(),
        cost_estimate=cost(4 * length * width * half, 16e6),
        name="mlp",
    )(normed_two, weights, weights, bf1, *more)


def mlp_back_kernel(
    g_branch_ref,
    b0_ref,
    b1_ref,
    c0_ref,
    c1_ref,
    slope0_ref,
    slope1_ref,
    middle_ref,
    attended_ref,
    cot_ref,
    mod_ref,
    w_out_ref,
    *rest,
):
    pre0_ref, pre1_ref, bsum_ref, g_middle_ref, g_att_ref, g_mixed_ref, sums_ref, acc_ref = rest[-8:]
    t = pl.program_id(0)
    g_branch = g_branch_ref[...]
    total = None
    for i, (b_ref, c_ref, slope_ref, pre_ref) in enumerate(
        ((b0_ref, c0_ref, slope0_ref, pre0_ref), (b1_ref, c1_ref, slope1_ref, pre1_ref))
    ):
        pre = (mm_nt(g_branch, c_ref[...]) * slope_ref[...]).astype(BF)
        pre_ref[...] = pre
        bsum_ref[i : i + 1, :] = jnp.sum(pre.astype(F32), axis=0, keepdims=True)
        part = mm_nt(pre, b_ref[...])
        total = part if total is None else total + part

    @pl.when(t == 0)
    def _():
        acc_ref[...] = total

    @pl.when(t > 0)
    def _():
        acc_ref[...] += total

    @pl.when(t == pl.num_programs(0) - 1)
    def _():
        g_n2 = acc_ref[...]
        n2, inv2 = normal(middle_ref[...])
        sums_ref[0:1, :] = jnp.sum(g_n2, axis=0, keepdims=True)
        sums_ref[1:2, :] = jnp.sum(g_n2 * n2, axis=0, keepdims=True)
        g_middle = cot_ref[...] + normal_back(g_n2 * (1.0 + mod_ref[4:5, :]), n2, inv2)
        g_middle_ref[...] = g_middle
        sums_ref[2:3, :] = jnp.sum(g_middle * attended_ref[...], axis=0, keepdims=True)
        g_att = (g_middle * mod_ref[2:3, :]).astype(BF)
        g_att_ref[...] = g_att
        sums_ref[3:4, :] = jnp.sum(g_att.astype(F32), axis=0, keepdims=True)
        g_mixed_ref[...] = mm_nt(g_att, w_out_ref[...]).astype(BF)


def mlp_back(g_branch, weights, slope0, slope1, middle, attended, cot, mod, w_out, after=()):
    length, width = middle.shape
    half = weights[0].shape[1] // 2
    tile = 384
    fixed = lambda a: pl.BlockSpec(a.shape, lambda t: (0, 0))
    cols = lambda r: pl.BlockSpec((r, tile), lambda t: (0, t))
    per = width // tile
    rows = pl.BlockSpec((tile, width), lambda t: (t % per, half // width + t // per))
    whole = lambda r: pl.BlockSpec((r, width), lambda t: (0, 0))
    return pl.pallas_call(
        mlp_back_kernel,
        grid=(half // tile,),
        out_shape=(
            shape((length, half), BF),
            shape((length, half), BF),
            shape((2, half), F32),
            shape((length, width), F32),
            shape((length, width), BF),
            shape((length, width), BF),
            shape((8, width), F32),
        ),
        in_specs=[
            fixed(g_branch),
            cols(width),
            cols(width),
            rows,
            rows,
            cols(length),
            cols(length),
            fixed(middle),
            fixed(attended),
            fixed(cot),
            fixed(mod),
            fixed(w_out),
        ]
        + [HBM] * len(after),
        out_specs=(
            cols(length),
            cols(length),
            cols(2),
            whole(length),
            whole(length),
            whole(length),
            whole(8),
        ),
        scratch_shapes=[pltpu.VMEM((length, width), F32)],
        compiler_params=params(),
        cost_estimate=cost(8 * length * width * half, 32e6),
        name="mlp_back",
    )(g_branch, *weights, *weights, slope0, slope1, middle, attended, cot, mod, w_out, *after)


def heads_back(q_ref, k_ref, v_ref, strip_ref, keep, gm_ref, dq_ref, dk_ref, dv_ref, sums_ref, start):
    scale = q_ref.shape[2] ** -0.5
    length = q_ref.shape[1]

    def head(i, carry):
        h = start + i
        q, k, v, gm = q_ref[h], k_ref[h], v_ref[h], gm_ref[i]
        sc = mm_nt(q, k) * scale + bias_of(strip_ref[h])
        sc = jnp.where(keep, sc, -1e30)
        ex = jnp.exp(sc - jnp.max(sc, axis=-1, keepdims=True))
        soft = ex / jnp.sum(ex, axis=-1, keepdims=True)
        dv_ref[i] = mm_tn(soft.astype(BF), gm).astype(BF)
        dp = mm_nt(gm, v)
        ds = (soft * (dp - jnp.sum(dp * soft, axis=-1, keepdims=True))).astype(BF)
        dq_ref[i] = (mm(ds, k) * scale).astype(BF)
        dk_ref[i] = (mm_tn(ds, q) * scale).astype(BF)
        dsf = ds.astype(F32)
        total = jnp.zeros((GRID, sums_ref.shape[2]), F32)
        blank = jnp.zeros((GRID, sums_ref.shape[2] - length), F32)
        for y in range(GRID):
            rows = jnp.concatenate([dsf[y * GRID : (y + 1) * GRID, :], blank], axis=1)
            by = (GRID - 1 - y) * GRID
            total = total + (pltpu.roll(rows, by, 1) if by else rows)
        sums_ref[i] = total
        return carry

    lax.fori_loop(0, dq_ref.shape[0], head, 0)


def first_heads_kernel(qh_ref, kh_ref, vh_ref, strip_ref, keep_ref, g_mixed_ref, *rest):
    dq_ref, dk_ref, dv_ref, sums_ref, gm_ref = rest[-5:]
    hd = qh_ref.shape[2]
    for i in range(HEADS // 2):
        gm_ref[i] = g_mixed_ref[:, i * hd : (i + 1) * hd]
    heads_back(
        qh_ref, kh_ref, vh_ref, strip_ref, keep_ref[...] > 0.0, gm_ref, dq_ref, dk_ref, dv_ref, sums_ref, 0
    )


def first_heads(qh, kh, vh, strip, keep, g_mixed, after=()):
    heads, length, hd = qh.shape
    some = shape((heads // 2, length, hd), BF)
    return pl.pallas_call(
        first_heads_kernel,
        out_shape=(some, some, some, shape((heads // 2,) + strip.shape[1:], F32)),
        in_specs=[WHOLE] * 6 + [HBM] * len(after),
        out_specs=(WHOLE,) * 4,
        scratch_shapes=[pltpu.VMEM((heads // 2, length, hd), BF)],
        compiler_params=params(),
        cost_estimate=cost(5 * length * length * heads * hd, 16e6),
        name="first_heads",
    )(qh, kh, vh, strip, keep, g_mixed, *after)


def last_heads_kernel(
    side_ref,
    qh_ref,
    kh_ref,
    vh_ref,
    strip_ref,
    keep_ref,
    g_mixed_ref,
    g_att_ref,
    fq_ref,
    fk_ref,
    fv_ref,
    fsum_ref,
    *rest,
):
    mine_ref, top_ref, low_ref, lo_ref, hi_ref, sums_ref, both_ref, gm_ref, dq_ref, dk_ref, dv_ref, strips_ref = rest[-12:]
    theirs_ref = both_ref
    width = g_mixed_ref.shape[1]
    hd = qh_ref.shape[2]
    half = HEADS // 2
    for i in range(half):
        gm_ref[i] = g_mixed_ref[:, (half + i) * hd : (half + i + 1) * hd]
    heads_back(
        qh_ref, kh_ref, vh_ref, strip_ref, keep_ref[...] > 0.0, gm_ref, dq_ref, dk_ref, dv_ref, strips_ref, half
    )
    for s, (qk_at, v_at) in enumerate(((mine_ref, theirs_ref), (theirs_ref, mine_ref))):

        @pl.when(side_ref[0] == s)
        def _():
            for h in range(HEADS):
                q, k, v = (fq_ref, fk_ref, fv_ref) if h < half else (dq_ref, dk_ref, dv_ref)
                i = h % half
                qk_at[:, h * hd : (h + 1) * hd] = q[i]
                qk_at[:, width + h * hd : width + (h + 1) * hd] = k[i]
                v_at[:, h * hd : (h + 1) * hd] = v[i]
            v_at[:, width:] = g_att_ref[...]
            sums_ref[0:1, :] = jnp.sum(qk_at[:, 0:width].astype(F32), axis=0, keepdims=True)
            sums_ref[1:2, :] = jnp.sum(v_at[:, 0:width].astype(F32), axis=0, keepdims=True)

    length = both_ref.shape[0]
    top_ref[...] = both_ref[0 : length // 2, :]
    low_ref[...] = both_ref[length // 2 :, :]
    lanes = lo_ref.shape[1]
    for part, ref in enumerate((fsum_ref, strips_ref)):
        lo = jnp.zeros((half, lanes), F32)
        hi = jnp.zeros((half, lanes), F32)
        j = lax.broadcasted_iota(jnp.int32, lo.shape, 1) % GRID
        for i in range(GRID):
            k = GRID - 1 - i
            row = ref[:, i, :]
            a = jnp.where(j < GRID - k, row, 0.0)
            lo = lo + (pltpu.roll(a, k, 1) if k else a)
            if k:
                hi = hi + pltpu.roll(jnp.where(j < GRID - k, 0.0, row), lanes - (GRID - k), 1)
        lo_ref[part * half : (part + 1) * half, :] = lo
        hi_ref[part * half : (part + 1) * half, :] = hi


def last_heads(side, qh, kh, vh, strip, keep, g_mixed, g_att, firsts, after=()):
    length, width = g_mixed.shape
    heads, _, hd = qh.shape
    per_head = pltpu.VMEM((heads // 2, length, hd), BF)
    window = shape((heads, strip.shape[2]), F32)
    return pl.pallas_call(
        last_heads_kernel,
        out_shape=(
            shape((length, 2 * width), BF),
            shape((length // 2, 2 * width), BF),
            shape((length // 2, 2 * width), BF),
            window,
            window,
            shape((8, width), F32),
        ),
        in_specs=[SCALAR] + [WHOLE] * 11 + [HBM] * len(after),
        out_specs=(WHOLE,) * 6,
        scratch_shapes=[pltpu.VMEM((length, 2 * width), BF)]
        + [per_head] * 4 + [pltpu.VMEM((heads // 2,) + strip.shape[1:], F32)],
        compiler_params=params(),
        cost_estimate=cost(5 * length * length * width, 16e6),
        name="last_heads",
    )(side, qh, kh, vh, strip, keep, g_mixed, g_att, *firsts, *after)


def tokens_back_kernel(
    side_ref,
    own_ref,
    other_ref,
    mine_ref,
    top_ref,
    low_ref,
    x_ref,
    g_middle_ref,
    mod_ref,
    place_ref,
    *rest,
):
    out_ref, sums_ref, w_ref, acc_ref, qk_ref, v_ref, sem = rest[-7:]
    length, width = x_ref.shape
    tile = 384
    wait = fetch_halves(side_ref, own_ref, other_ref, w_ref, sem)
    half = length // 2

    @pl.when(side_ref[0] == 0)
    def _():
        qk_ref[...] = mine_ref[...]
        v_ref[0:half, :] = top_ref[:, 0:width]
        v_ref[half:, :] = low_ref[:, 0:width]

    @pl.when(side_ref[0] == 1)
    def _():
        qk_ref[0:half, :] = top_ref[...]
        qk_ref[half:, :] = low_ref[...]
        v_ref[...] = mine_ref[:, 0:width]

    wait(0)
    wait(1)

    def body(o):
        rows = pl.ds(o, tile)
        acc_ref[:, rows] = (
            mm_nt(qk_ref[...], w_ref[0, rows, :]) + mm_nt(v_ref[...], w_ref[1, rows, 0:width])
        )

    strips(width, tile, body)
    g_n1 = acc_ref[...]
    n1, inv1 = normal(x_ref[...])
    sums_ref[0:1, :] = jnp.sum(g_n1, axis=0, keepdims=True)
    sums_ref[1:2, :] = jnp.sum(g_n1 * n1, axis=0, keepdims=True)
    g_x = g_middle_ref[...] + normal_back(g_n1 * (1.0 + mod_ref[1:2, :]), n1, inv1)
    out_ref[...] = mm_tn(place_ref[...], g_x.astype(BF)).astype(BF)


def tokens_back(side, own, other, mine, theirs, x, g_middle, mod, place, after=()):
    length, width = x.shape
    return pl.pallas_call(
        tokens_back_kernel,
        out_shape=(shape((length, width), BF), shape((8, width), F32)),
        in_specs=[SCALAR, HBM, HBM] + [WHOLE] * 7 + [HBM] * len(after),
        out_specs=(WHOLE,) * 2,
        scratch_shapes=[
            pltpu.VMEM((2, width, 2 * width), BF),
            pltpu.VMEM((length, width), F32),
            pltpu.VMEM((length, 2 * width), BF),
            pltpu.VMEM((length, width), BF),
            pltpu.SemaphoreType.DMA((2,)),
        ],
        compiler_params=params(),
        cost_estimate=cost(6 * length * width * width, 16e6),
        name="tokens_back",
    )(side, own, other, mine, *theirs, x, g_middle, mod, place, *after)


def local(
    n,
    tokens,
    condition,
    kept_index,
    kept_count,
    cotangent,
    w_ada,
    w_qkv,
    w_proj,
    w_fc1,
    w_fc2,
    b_ada,
    b_qv,
    b_proj,
    b_fc1,
    b_fc2,
    rel_table,
):
    side = lax.axis_index("stream")
    chip = lax.axis_index("dp")
    length, width = tokens.shape[2], tokens.shape[3]
    ff = w_fc1.shape[1]
    rows = width // n
    cut = ff // (2 * n)
    first = side == 0
    side_word = side.astype(jnp.int32).reshape(1)
    chip_word = chip.astype(jnp.int32).reshape(1)

    order_first, order_parts = orders_out(n)
    firsts = tuple(part[-1] for part in order_parts)

    ordinal = jnp.arange(length, dtype=jnp.int32)
    count = jnp.where(first, length, kept_count[0])
    position = jnp.where(first, ordinal, kept_index[0])
    place = ((position[None, :] == ordinal[:, None]) & (ordinal[None, :] < count)).astype(BF)
    present = jnp.sum(place.astype(F32), axis=1)
    keep = present.reshape(1, length)
    present = present.reshape(length, 1)
    x = mm(place, tokens[0, 0])
    cot = mm(place, cotangent[0, 0])
    bias = bias_strip(rel_table)

    cond = condition[0, 0]
    sig = jax.nn.sigmoid(cond)
    cond_act = (cond * sig).astype(BF)
    shard_a = attn_shard(side_word, w_qkv, w_proj)
    all_a = Gathering(chip_word, shard_a, n)
    acts = trade(hold(jnp.broadcast_to(cond_act[None], (n, width)), shard_a))
    acts_part = lax.dynamic_slice_in_dim(acts, chip * rows, rows, axis=1)
    shard_bc = mlp_shard(n, side_word, w_fc1, w_fc2, after=(shard_a,))
    last = all_a.step(shard_bc, bias, x, cot, acts_part)
    all_bc = Gathering(chip_word, hold(shard_bc, *last), n)
    last = all_a.step(*last)
    acts_twin = swap_stream(acts_part)
    while not all_a.done():
        last = all_a.step(*last, acts_twin, *all_bc.came)
    mod_part = trade(hold(mm(acts_part, w_ada), *last))
    last = all_bc.step(mod_part)
    a_own = all_a.result(*last)
    a_other = swap_stream(a_own)
    modulation = jnp.sum(mod_part, axis=0) + b_ada
    mod = modulation.reshape(6, width)
    last = (a_own,)
    while not all_bc.done():
        last = all_bc.step(*last)
    w_out = jnp.where(first, a_other[:, width:], a_own[:, width:])

    n1, _ = normal(x)
    normed = (n1 * (1.0 + mod[1]) + mod[0]).astype(BF)
    qh, kh, vh, lhs_mine, lhs_theirs, attended, middle, normed_two = attention(
        side_word,
        a_own,
        a_other,
        normed,
        b_qv.reshape(1, -1),
        bias,
        keep,
        x,
        mod,
        b_proj.reshape(1, -1),
    )

    bc_own = all_bc.result(normed_two)
    bc_other = swap_stream(bc_own)
    lhs_twin = swap_stream(lhs_theirs)
    n2_twin = swap_stream(normed_two)
    bf1 = jnp.transpose(b_fc1.reshape(n, 2, 2, cut // 2), (1, 2, 0, 3)).reshape(2, 1, ff // 2)
    hid0, slope0, part = mlp(normed_two, bc_own, jnp.where(first, bf1[0], bf1[1]))
    hid1, slope1, g_branch, out_tokens, sums_a = mlp(
        normed_two,
        bc_other,
        jnp.where(first, bf1[1], bf1[0]),
        (part, b_fc2.reshape(1, -1), middle, cot, mod, place, present),
    )

    parts_c = product(
        chip_word, hid0, swap_stream(hid1), g_branch, swap_stream(g_branch), width, n, firsts
    )
    sum_c = Reduction(chip_word, parts_c, n)
    pre0, pre1, pre_sum, g_middle, g_att, g_mixed, sums_b = mlp_back(
        g_branch,
        (bc_own, bc_other),
        slope0,
        slope1,
        middle,
        attended,
        cot,
        mod,
        w_out,
        after=(parts_c[0][0], lhs_twin, n2_twin),
    )
    kept = step([sum_c], g_mixed)
    pre_twin = swap_stream(pre1)
    one = first_heads(qh, kh, vh, bias, keep, g_mixed, after=kept + (pre_twin,))
    kept = step([sum_c], one[0])
    kept = step([sum_c], *kept)
    parts_b = product(
        chip_word,
        normed_two,
        n2_twin,
        pre0,
        pre_twin,
        width,
        n,
        firsts,
        after=kept,
    )
    sum_b = Reduction(chip_word, parts_b, n)
    g_mine, top, low, lo, hi, sums_c = last_heads(
        side_word, qh, kh, vh, bias, keep, g_mixed, g_att, one, after=(parts_b[0][0],)
    )
    g_theirs = (top, low)
    g_twin = (swap_stream(top), swap_stream(low))
    while not sum_c.done():
        step([sum_c])
    d_c = sum_c.result(g_mine)
    kept = step([sum_b], g_mine, d_c) + g_twin
    grad_tokens, sums_d = tokens_back(
        side_word, a_own, a_other, g_mine, g_theirs, x, g_middle, mod, place, after=kept
    )
    kept = step([sum_b], sums_d)
    parts_a = product(
        chip_word,
        lhs_mine,
        lhs_twin,
        g_mine,
        g_twin,
        width,
        n,
        firsts,
        after=kept,
    )
    kept = step([sum_b], parts_a[0][0])
    sum_a = Reduction(chip_word, parts_a, n)

    sums_a, sums_b, sums_c, lo, hi, pre_sum = hold(
        (sums_a, sums_b, sums_c, lo, hi, pre_sum), parts_a[0][0]
    )
    g_mod = jnp.concatenate([sums_d[0], sums_d[1], sums_b[2], sums_b[0], sums_b[1], sums_a[0]])
    g_mod = g_mod.astype(BF).astype(F32).reshape(-1, 128)
    pre_sum = jnp.where(first, pre_sum, jnp.concatenate([pre_sum[1:], pre_sum[:1]]))
    pre_sum = jnp.transpose(pre_sum.reshape(2, 2, n, cut // 2), (2, 0, 1, 3))
    smalls = [
        sums_c[0],
        sums_c[1],
        sums_b[3],
        pre_sum.reshape(-1),
        sums_a[1],
        table_of(lo, hi).reshape(-1),
    ]
    sizes = [t.shape[0] for t in smalls]
    packed = jnp.concatenate(smalls)
    packed = jnp.pad(packed, (0, 128 * SUM_ROWS - packed.shape[0])).reshape(-1, 128)
    mod_rows = g_mod.shape[0]
    pad = -mod_rows % 8
    told = jnp.concatenate([packed, jnp.pad(g_mod, ((0, pad), (0, 0)))], axis=0)
    group = told.shape[0] - SUM_ROWS
    grad_w_fc2 = None
    for b in all_bits(n)[::-1]:
        running = [t for t in (sum_a, sum_b) if not t.done()]
        if running:
            kept = step(running[:1], *([grad_w_fc2] if grad_w_fc2 is not None else []))
        if grad_w_fc2 is None:
            grad_w_fc2 = fc2_rows(side_word, d_c, swap_stream(d_c))
        told = meet(chip_word, told, swap(told, b, n), b, group, after=kept)
    while not sum_a.done():
        kept = step([sum_a])
    while not sum_b.done():
        step([sum_b])
    twin = swap_stream(told)

    def mods_of(t):
        return t[SUM_ROWS:].reshape(n, -1, 128)[:, :mod_rows].reshape(n, -1)

    g_own, g_twin = mods_of(told), mods_of(twin)
    grad_w_ada = mm_tn(acts_part, g_own.astype(BF)) + mm_tn(acts_twin, g_twin.astype(BF))
    grad_b_ada = jnp.sum(g_own, axis=0) + jnp.sum(g_twin, axis=0)
    g_acts = trade(mm_nt(g_own.astype(BF), w_ada)).reshape(width)
    grad_condition = g_acts * sig * (1.0 + cond * (1.0 - sig))
    d_b = sum_b.result(*kept)
    grad_w_fc1 = fc1_rows(n, side_word, d_b, swap_stream(d_b))
    d_a = sum_a.result(grad_w_fc1, g_acts)
    packed = (told[:SUM_ROWS] + twin[:SUM_ROWS]).reshape(-1)
    parts, at = [], 0
    for size in sizes:
        parts.append(packed[at : at + size])
        at += size

    grad_w_qkv, grad_w_proj = attn_rows(side_word, d_a, swap_stream(d_a))
    return (
        out_tokens[None, None],
        grad_tokens[None, None],
        grad_condition[None, None],
        grad_w_ada,
        grad_w_qkv,
        grad_w_proj,
        grad_w_fc1,
        grad_w_fc2,
        grad_b_ada,
        jnp.concatenate(parts[:2]),
        parts[2],
        parts[3],
        parts[4],
        parts[5].reshape(rel_table.shape),
    )


def solution(mesh):
    n = mesh.shape["dp"]

    def body(*args):
        return local(n, *args)

    return jax.shard_map(
        body,
        mesh=mesh,
        in_specs=(
            P("stream", "dp", None, None),
            P("stream", "dp", None),
            P("dp", None),
            P("dp"),
            P("stream", "dp", None, None),
            P("dp", None),
            P("dp", None),
            P("dp", None),
            P("dp", None),
            P("dp", None),
            P(),
            P(),
            P(),
            P(),
            P(),
            P(),
        ),
        out_specs=(
            P("stream", "dp", None, None),
            P("stream", "dp", None, None),
            P("stream", "dp", None),
            P("dp", None),
            P("dp", None),
            P("dp", None),
            P("dp", None),
            P("dp", None),
            P(),
            P(),
            P(),
            P(),
            P(),
            P(),
        ),
        check_vma=False,
    )
```

```python
import functools
import math

import jax
import jax.numpy as jnp
from jax import lax
from jax.experimental import pallas as pl
from jax.experimental.pallas import tpu as pltpu
from jax.sharding import PartitionSpec as P

HEADS = 16
GRID = 16
BF = jnp.bfloat16
F32 = jnp.float32


def swap(v, bit, n):
    return lax.ppermute(v, "dp", [(i, i ^ bit) for i in range(n)])


def swap_stream(v):
    return lax.ppermute(v, "stream", [(0, 1), (1, 0)])


def axis_bits(n):
    k = n.bit_length() - 1
    s = k // 3
    xs = [1 << i for i in range(s)]
    ys = [1 << (s + i) for i in range(s)]
    zs = [1 << i for i in range(2 * s, k)]
    return xs, ys, zs


def all_bits(n):
    return [1 << i for i in range(n.bit_length() - 1)]


def orders_out(n):
    xs, ys, zs = axis_bits(n)
    near = zs[:1]
    return zs[1:][::-1], (near + ys + xs, xs + near + ys, ys + xs + near)


def trade(v):
    return lax.all_to_all(v, "dp", 0, 0, tiled=True)


def mm(a, b):
    return lax.dot_general(a, b, (((1,), (0,)), ((), ())), preferred_element_type=F32)


def mm_nt(a, b):
    return lax.dot_general(a, b, (((1,), (1,)), ((), ())), preferred_element_type=F32)


def mm_tn(a, b):
    return lax.dot_general(a, b, (((0,), (0,)), ((), ())), preferred_element_type=F32)


def normal(v):
    center = v - jnp.mean(v, axis=-1, keepdims=True)
    inv = lax.rsqrt(jnp.mean(center * center, axis=-1, keepdims=True) + 1e-06)
    return center * inv, inv


def normal_back(g, n, inv):
    return inv * (g - jnp.mean(g, axis=-1, keepdims=True) - n * jnp.mean(g * n, axis=-1, keepdims=True))


def bias_windows(table):
    w = 2 * GRID - 1
    t = jnp.transpose(table.reshape(w, w, HEADS)[::-1, ::-1], (2, 0, 1))
    t = jnp.pad(t, ((0, 0), (0, 1), (0, 1))).reshape(HEADS, w + 1, 2, GRID)
    return t[:, :, 0].reshape(HEADS, -1), t[:, :, 1].reshape(HEADS, -1)


def table_of(lo, hi):
    w = 2 * GRID - 1
    t = jnp.stack([lo.reshape(HEADS, w + 1, GRID), hi.reshape(HEADS, w + 1, GRID)], axis=2)
    t = t.reshape(HEADS, w + 1, 2 * GRID)[:, :w, :w]
    return jnp.transpose(t, (1, 2, 0))[::-1, ::-1].reshape(w * w, HEADS)


def gelu_parts(x):
    k = math.sqrt(2.0 / math.pi)
    th = jnp.tanh(k * (x + 0.044715 * x * x * x))
    value = 0.5 * x * (1.0 + th)
    slope = 0.5 * (1.0 + th) + 0.5 * x * (1.0 - th * th) * k * (1.0 + 3 * 0.044715 * x * x)
    return value, slope


VMEM_BYTES = 56 * 1024 * 1024
SUM_ROWS = 200
WHOLE = pl.BlockSpec(memory_space=pltpu.VMEM)
HBM = pl.BlockSpec(memory_space=pl.ANY)
SCALAR = pl.BlockSpec(memory_space=pltpu.SMEM)


def shape(dims, dtype):
    return jax.ShapeDtypeStruct(dims, dtype)


def params():
    return pltpu.CompilerParams(vmem_limit_bytes=VMEM_BYTES)


def cost(flops, size):
    return pl.CostEstimate(flops=int(flops), bytes_accessed=int(size), transcendentals=0)


def strips(total, tile, body):
    def step(i, carry):
        body(pl.multiple_of(i * tile, tile))
        return carry

    lax.fori_loop(0, total // tile, step, 0)


def fetch_halves(side_ref, own_ref, other_ref, w_ref, sem):
    side = side_ref[0]
    mine = pltpu.make_async_copy(own_ref, w_ref.at[side], sem.at[side])
    twin = pltpu.make_async_copy(other_ref, w_ref.at[1 - side], sem.at[1 - side])
    mine.start()
    twin.start()

    def wait(slot):
        pltpu.make_async_copy(own_ref, w_ref.at[slot], sem.at[slot]).wait()

    return wait


def pieces(n, rows, cut, s):
    half = cut // 2
    for part in range(2):
        for k in range(n):
            yield (k * 2 + s) * cut + part * half, (part * n + k) * half, half


def fc1_rows_kernel(n, side_ref, own_ref, other_ref, out_ref):
    rows, ff = out_ref.shape
    cut = ff // (2 * n)
    for s in range(2):

        @pl.when(side_ref[0] == s)
        def _():
            for half, ref in ((s, own_ref), (1 - s, other_ref)):
                for src, dst, w in pieces(n, rows, cut, half):
                    out_ref[:, src : src + w] = ref[:, dst : dst + w]


def fc1_rows(n, side, own, other):
    return pl.pallas_call(
        functools.partial(fc1_rows_kernel, n),
        out_shape=shape((own.shape[0], 2 * own.shape[1]), F32),
        in_specs=[SCALAR, WHOLE, WHOLE],
        out_specs=WHOLE,
        compiler_params=params(),
        name="fc1_rows",
    )(side, own, other)


def strip_kernel(lo_ref, hi_ref, out_ref):
    lanes = lo_ref.shape[1]
    lo, hi = lo_ref[...], hi_ref[...]
    j = lax.broadcasted_iota(jnp.int32, lo.shape, 1) % GRID
    for i in range(GRID):
        k = GRID - 1 - i
        a = pltpu.roll(lo, lanes - k, 1) if k else lo
        out_ref[:, i, :] = jnp.where(j < GRID - k, a, pltpu.roll(hi, GRID - k, 1))


def bias_strip(table):
    lo, hi = bias_windows(table)
    return pl.pallas_call(
        strip_kernel,
        out_shape=shape((HEADS, GRID, lo.shape[1]), F32),
        in_specs=[WHOLE, WHOLE],
        out_specs=WHOLE,
        name="bias_strip",
    )(lo, hi)


def bias_of(strip):
    return jnp.concatenate(
        [strip[:, (GRID - 1 - y) * GRID : (2 * GRID - 1 - y) * GRID] for y in range(GRID)], axis=0
    )


def put(i, pos):
    return (i >> pos) << (pos + 1) | (i & ((1 << pos) - 1))


def attn_shard_kernel(side_ref, qkv_ref, proj_ref, out_ref):
    width = proj_ref.shape[1]
    for s in range(2):

        @pl.when(side_ref[0] == s)
        def _():
            if s == 0:
                out_ref[0] = qkv_ref[:, 0 : 2 * width]
            else:
                out_ref[0, :, 0:width] = qkv_ref[:, 2 * width :]
                out_ref[0, :, width:] = proj_ref[...]


def mlp_shard_kernel(n, side_ref, f1_ref, f2_ref, *rest):
    out_ref = rest[-1]
    rows, ff = f1_ref.shape
    width = f2_ref.shape[1]
    cut = ff // (2 * n)
    for s in range(2):

        @pl.when(side_ref[0] == s)
        def _():
            for src, dst, w in pieces(n, rows, cut, s):
                out_ref[0, :, dst : dst + w] = f1_ref[:, src : src + w]
            for part in range(2):
                lo = s * cut + part * rows
                cols = slice(ff // 2 + part * width, ff // 2 + (part + 1) * width)
                out_ref[0, :, cols] = f2_ref[lo : lo + rows, :]


def mlp_shard(n, side, f1, f2, after=()):
    return pl.pallas_call(
        functools.partial(mlp_shard_kernel, n),
        out_shape=shape((1,) + f1.shape, BF),
        in_specs=[SCALAR, WHOLE, WHOLE] + [HBM] * len(after),
        out_specs=WHOLE,
        compiler_params=params(),
        name="mlp_shard",
    )(side, f1, f2, *after)


def attn_shard(side, w_qkv, w_proj):
    rows, width = w_proj.shape
    return pl.pallas_call(
        attn_shard_kernel,
        out_shape=shape((1, rows, 2 * width), BF),
        in_specs=[SCALAR, WHOLE, WHOLE],
        out_specs=WHOLE,
        compiler_params=params(),
        name="attn_shard",
    )(side, w_qkv, w_proj)


def join_kernel(jobs, chip_ref, *refs):
    outs = refs[-sum(len(cols) for _, cols in jobs) :]
    at = 0
    for k, (bit, cols) in enumerate(jobs):
        v_ref, r_ref = refs[2 * k], refs[2 * k + 1]
        m = v_ref.shape[0]
        up = (chip_ref[0] & bit) // bit
        lo = 0
        for c in cols:
            for i in range(m):
                outs[at][up * m + i] = v_ref[i, :, lo : lo + c]
                outs[at][(1 - up) * m + i] = r_ref[i, :, lo : lo + c]
            lo += c
            at += 1


def join(chip, jobs, after=()):
    flat = [t for v, r, _, _ in jobs for t in (v, r)]
    return pl.pallas_call(
        functools.partial(join_kernel, [(bit, cols) for _, _, bit, cols in jobs]),
        out_shape=tuple(
            shape((2 * v.shape[0], v.shape[1], c), v.dtype) for v, _, _, cols in jobs for c in cols
        ),
        in_specs=[SCALAR] + [WHOLE] * len(flat) + [HBM] * len(after),
        out_specs=(WHOLE,) * sum(len(cols) for _, _, _, cols in jobs),
        compiler_params=params(),
        name="join",
    )(chip, *flat, *after)


def assemble_kernel(orders, chip_ref, *refs):
    out_ref = refs[-1]
    lo = 0
    m = out_ref.shape[0] // 2
    for k, bits in enumerate(orders):
        v_ref, r_ref = refs[2 * k], refs[2 * k + 1]
        c = v_ref.shape[2]
        last = bits[-1]
        up = (chip_ref[0] & last) // last
        lead = bits[:-1][::-1]
        for i in range(m):
            base = sum(b for j, b in enumerate(lead) if (i >> (len(lead) - 1 - j)) & 1)
            out_ref[base + up * last, :, lo : lo + c] = v_ref[i]
            out_ref[base + (1 - up) * last, :, lo : lo + c] = r_ref[i]
        lo += c


def assemble(chip, orders, pairs, after=()):
    flat = [t for pair in pairs for t in pair]
    m, rows = 1 << (len(orders[0]) - 1), flat[0].shape[1]
    cols = sum(v.shape[2] for v, _ in pairs)
    out = pl.pallas_call(
        functools.partial(assemble_kernel, orders),
        out_shape=shape((2 * m, rows, cols), BF),
        in_specs=[SCALAR] + [WHOLE] * len(flat) + [HBM] * len(after),
        out_specs=WHOLE,
        compiler_params=params(),
        name="assemble",
    )(chip, *flat, *after)
    return out.reshape(2 * m * rows, cols)


class Gathering:
    def __init__(self, chip, v, n):
        first, parts = orders_out(n)
        self.chip, self.n = chip, n
        self.orders = [first + part for part in parts]
        self.turn, self.cut_at = 0, len(first)
        self.parts = [v]
        self.exchange()

    def exchange(self):
        self.came = [swap(v, self.orders[k][self.turn], self.n) for k, v in enumerate(self.parts)]
        self.turn += 1

    def step(self, *after):
        jobs = []
        for k, (v, r) in enumerate(zip(self.parts, self.came)):
            c = v.shape[2]
            cut = (c // 3,) * 3 if self.turn == self.cut_at else (c,)
            jobs.append((v, r, self.orders[k][self.turn - 1], cut))
        self.parts = list(join(self.chip, jobs, after))
        self.exchange()
        return tuple(self.parts)

    def done(self):
        return self.turn == len(self.orders[0])

    def result(self, *after):
        return assemble(self.chip, self.orders, tuple(zip(self.parts, self.came)), after=after)


def merge_kernel(bits, mates, chip_ref, *refs):
    small, (v_ref, r_ref), outs = refs[:6], refs[6:8], refs[-3:]
    up = lambda bit: (chip_ref[0] & bit) // bit
    m = small[0].shape[0]
    c = small[0].shape[2]
    far = v_ref.shape[0]
    for k in range(3):
        for ref, side in ((small[2 * k], up(bits[k])), (small[2 * k + 1], 1 - up(bits[k]))):
            for i in range(m):
                outs[k][side * m + i] = ref[i]
    for k in range(3):
        out_ref = outs[mates[k]]
        wide = v_ref.shape[2] // 3
        for ref, side in ((v_ref, up(bits[3])), (r_ref, 1 - up(bits[3]))):
            for h in range(wide // c):
                for i in range(far):
                    lo = k * wide + h * c
                    out_ref[2 * m + h * 2 * far + side * far + i] = ref[i, :, lo : lo + c]


def cross_kernel(bits, skip, chip_ref, *refs):
    outs = refs[-3:]
    for k, bit in enumerate(bits):
        v_ref, r_ref, out_ref = refs[2 * k], refs[2 * k + 1], outs[k]
        up = (chip_ref[0] & bit) // bit
        c = v_ref.shape[2]
        m = out_ref.shape[0] // 2
        for ref, side in ((v_ref, up), (r_ref, 1 - up)):
            for h in range(out_ref.shape[2] // c):
                for i in range(m):
                    out_ref[side * m + i, :, h * c : (h + 1) * c] = ref[skip + h * m + i]


def merge_steps(small, large, *after):
    n, turn = small.n, len(small.orders[0]) - 1
    next_small = [order[turn] for order in small.orders]
    next_large = [order[large.cut_at] for order in large.orders]
    mates = [next_small.index(bit) for bit in next_large]
    bits = [order[turn - 1] for order in small.orders] + [large.orders[0][large.cut_at - 1]]
    v, r = large.parts[0], large.came[0]
    _, rows, c = small.parts[0].shape
    m = 2 * small.parts[0].shape[0]
    far = 2 * v.shape[0]
    wide = v.shape[2] // 3
    flat = [t for pair in zip(small.parts, small.came) for t in pair]
    outs = pl.pallas_call(
        functools.partial(merge_kernel, bits, mates),
        out_shape=(shape((m + far * (wide // c), rows, c), BF),) * 3,
        in_specs=[SCALAR] + [WHOLE] * 8 + [HBM] * len(after),
        out_specs=(WHOLE,) * 3,
        compiler_params=params(),
        name="merge",
    )(small.chip, *flat, v, r, *after)
    came = [swap(t, bit, n) for t, bit in zip(outs, next_small)]

    def small_result(*after):
        return assemble(small.chip, small.orders, tuple(zip(outs, came)), after=after)

    def large_on(*after):
        pairs = [t for k in range(3) for t in (outs[mates[k]], came[mates[k]])]
        parts = pl.pallas_call(
            functools.partial(cross_kernel, next_large, m),
            out_shape=(shape((2 * far, rows, wide), BF),) * 3,
            in_specs=[SCALAR] + [WHOLE] * 6 + [HBM] * len(after),
            out_specs=(WHOLE,) * 3,
            compiler_params=params(),
            name="cross",
        )(large.chip, *pairs, *after)
        large.parts = list(parts)
        large.turn = large.cut_at + 1
        large.exchange()
        return tuple(parts)

    return outs, small_result, large_on


def product_kernel(n, firsts, steps, half_step, count, chip_ref, l0_ref, l1_ref, *rest):
    turned_ref = rest[-1]
    r_refs = rest[:count]
    outs = rest[-7:-1]
    t = pl.program_id(0)
    length = l0_ref.shape[0]
    width = turned_ref.shape[1]
    rows = width // n

    @pl.when(t == 0)
    def _():
        for k in range(turned_ref.shape[0]):
            cols = slice(k * width, (k + 1) * width)
            turned_ref[k, :, 0:length] = l0_ref[:, cols].T
            turned_ref[k, :, length:] = l1_ref[:, cols].T

    slot = jnp.where(t >= half_step, turned_ref.shape[0] - 1, 0)
    value, at = 0.0, 0
    for r_ref in r_refs:
        rows_here = r_ref.shape[0]
        value = value + mm(turned_ref[slot, :, at : at + rows_here], r_ref[...])
        at += rows_here
    for part, (bit, (lo, hi)) in enumerate(zip(firsts, steps)):
        pos = bit.bit_length() - 1
        for up in range(2):

            @pl.when((t >= lo) & (t < hi) & ((chip_ref[0] & bit) // bit == up))
            def _():
                for i in range(n // 2):
                    at = put(i, pos)
                    for goes, ref in ((up, outs[2 * part]), (1 - up, outs[2 * part + 1])):
                        k = at + goes * bit
                        ref[i] = value[k * rows : (k + 1) * rows].astype(BF)


def product(chip, l0, l1, r0, r1, width, n, firsts, after=()):
    length = l0.shape[0]
    tile = width // 3
    per = width // tile
    rights = (r0,) + (r1 if isinstance(r1, tuple) else (r1,))
    two_l, two_r = l0.shape[1] > width, r0.shape[1] > width
    cols = (2 * width // 3,) * 3
    steps = []
    for c in cols:
        lo = steps[-1][1] if steps else 0
        steps.append((lo, lo + c // tile))
    left = pl.BlockSpec(l0.shape, lambda t: (0, 0))
    right = [pl.BlockSpec((r.shape[0], tile), lambda t: (0, t if two_r else t % per)) for r in rights]
    spec = lambda lo, hi: pl.BlockSpec(
        (n // 2, width // n, tile), lambda t: (0, 0, jnp.clip(t - lo, 0, hi - lo - 1))
    )
    out = pl.pallas_call(
        functools.partial(product_kernel, n, firsts, steps, per, len(rights)),
        grid=(2 * per,),
        out_shape=tuple(shape((n // 2, width // n, c), BF) for c in cols for _ in range(2)),
        in_specs=[SCALAR, left, left] + right + [HBM] * len(after),
        out_specs=tuple(spec(*s) for s in steps for _ in range(2)),
        scratch_shapes=[pltpu.VMEM((1 + two_l, width, 2 * length), BF)],
        compiler_params=params(),
        cost_estimate=cost(8 * length * width * width, 12e6),
        name="product",
    )(chip, l0, l1, *rights, *after)
    return tuple((out[2 * k], out[2 * k + 1]) for k in range(3))


def split_kernel(jobs, chip_ref, *refs):
    outs = refs[-2 * len(jobs) :]
    at = 0
    for k, (bit, pos, count) in enumerate(jobs):
        keep_ref, send_ref = outs[2 * k], outs[2 * k + 1]
        up = (chip_ref[0] & bit) // bit
        lo = 0
        for _ in range(count):
            v_ref, r_ref = refs[at], refs[at + 1]
            at += 2
            c = v_ref.shape[2]
            for i in range(keep_ref.shape[0]):
                for out_ref, goes in ((send_ref, 1 - up), (keep_ref, up)):
                    j = put(i, pos) + goes * (1 << pos)
                    total = v_ref[j].astype(F32) + r_ref[j].astype(F32)
                    out_ref[i, :, lo : lo + c] = total.astype(BF)
            lo += c


def split(chip, jobs, after=()):
    flat = [t for pairs, _, _ in jobs for pair in pairs for t in pair]
    outs, plan = [], []
    for pairs, bit, left in jobs:
        m, rows, _ = pairs[0][0].shape
        cols = sum(v.shape[2] for v, _ in pairs)
        outs += [shape((m // 2, rows, cols), BF)] * 2
        plan.append((bit, len(left) - 1 - left.index(bit), len(pairs)))
    out = pl.pallas_call(
        functools.partial(split_kernel, plan),
        out_shape=tuple(outs),
        in_specs=[SCALAR] + [WHOLE] * len(flat) + [HBM] * len(after),
        out_specs=(WHOLE,) * len(outs),
        compiler_params=params(),
        name="split",
    )(chip, *flat, *after)
    return [(out[2 * k], out[2 * k + 1]) for k in range(len(jobs))]


def finish_kernel(v_ref, r_ref, *rest):
    rest[-1][...] = v_ref[0].astype(F32) + r_ref[0].astype(F32)


def finish(v, r, after=()):
    return pl.pallas_call(
        finish_kernel,
        out_shape=shape(v.shape[1:], F32),
        in_specs=[WHOLE] * 2 + [HBM] * len(after),
        out_specs=WHOLE,
        compiler_params=params(),
        name="finish",
    )(v, r, *after)


def meet_kernel(bit, rows, chip_ref, v_ref, r_ref, *rest):
    out_ref = rest[-1]
    out_ref[0:SUM_ROWS, :] = v_ref[0:SUM_ROWS, :] + r_ref[0:SUM_ROWS, :]
    up = (chip_ref[0] & bit) // bit
    for i in range((v_ref.shape[0] - SUM_ROWS) // rows):
        src = slice(SUM_ROWS + i * rows, SUM_ROWS + (i + 1) * rows)
        for ref, side in ((v_ref, up), (r_ref, 1 - up)):
            at = pl.multiple_of(SUM_ROWS + (2 * i + side) * rows, 8)
            out_ref[pl.ds(at, rows), :] = ref[src, :]


def meet(chip, v, r, bit, rows, after=()):
    total = 2 * v.shape[0] - SUM_ROWS
    return pl.pallas_call(
        functools.partial(meet_kernel, bit, rows),
        out_shape=shape((total, v.shape[1]), F32),
        in_specs=[SCALAR, WHOLE, WHOLE] + [HBM] * len(after),
        out_specs=WHOLE,
        compiler_params=params(),
        name="meet",
    )(chip, v, r, *after)


class Reduction:
    def __init__(self, chip, parts, n):
        last, orders = orders_out(n)
        self.chip, self.n = chip, n
        self.orders = [part[::-1] for part in orders]
        self.tail = last[::-1]
        self.left = [all_bits(n)[::-1] for _ in range(3)]
        self.pairs = [
            (keep, self.exchange(k, self.orders[k].pop(0), send)) for k, (keep, send) in enumerate(parts)
        ]

    def exchange(self, k, bit, send):
        self.left[k] = [b for b in self.left[k] if b != bit]
        return swap(send, bit, self.n)

    def plan(self):
        chains = [[k] for k in range(len(self.pairs))]
        if len(self.pairs) == 3 and not self.orders[0]:
            chains = [[0, 1, 2]]
            self.orders = [list(self.tail)]
        bits = [self.orders[chain[0]].pop(0) for chain in chains]
        return [
            ([self.pairs[j] for j in chain], bit, list(self.left[chain[0]]))
            for chain, bit in zip(chains, bits)
        ]

    def go(self, jobs, outs):
        self.pairs = [
            (keep, self.exchange(k, bit, send))
            for k, ((_, bit, _), (keep, send)) in enumerate(zip(jobs, outs))
        ]

    def done(self):
        return len(self.pairs) == 1 and not self.orders[0]

    def result(self, *after):
        return finish(*self.pairs[0], after)


def step(sums, *after):
    plans = [s.plan() for s in sums]
    outs = split(sums[0].chip, [job for jobs in plans for job in jobs], after)
    kept = tuple(keep for keep, _ in outs)
    for s, jobs in zip(sums, plans):
        s.go(jobs, outs[: len(jobs)])
        outs = outs[len(jobs) :]
    return kept


def fc2_rows_kernel(side_ref, own_ref, other_ref, out_ref):
    rows = own_ref.shape[0]
    width = out_ref.shape[1]
    for s in range(2):

        @pl.when(side_ref[0] == s)
        def _():
            for half, ref in ((s, own_ref), (1 - s, other_ref)):
                for part in range(2):
                    lo = (2 * half + part) * rows
                    out_ref[lo : lo + rows, :] = ref[:, part * width : (part + 1) * width]


def fc2_rows(side, own, other):
    return pl.pallas_call(
        fc2_rows_kernel,
        out_shape=shape((4 * own.shape[0], own.shape[1] // 2), F32),
        in_specs=[SCALAR, WHOLE, WHOLE],
        out_specs=WHOLE,
        compiler_params=params(),
        name="fc2_rows",
    )(side, own, other)


def attn_rows_kernel(side_ref, own_ref, other_ref, qkv_ref, proj_ref):
    width = proj_ref.shape[1]
    for s in range(2):

        @pl.when(side_ref[0] == s)
        def _():
            low, high = (own_ref, other_ref) if s == 0 else (other_ref, own_ref)
            qkv_ref[:, 0 : 2 * width] = low[...]
            qkv_ref[:, 2 * width :] = high[:, 0:width]
            proj_ref[...] = high[:, width:]


def attn_rows(side, own, other):
    rows, width = own.shape[0], own.shape[1] // 2
    return pl.pallas_call(
        attn_rows_kernel,
        out_shape=(shape((rows, 3 * width), F32), shape((rows, width), F32)),
        in_specs=[SCALAR, WHOLE, WHOLE],
        out_specs=(WHOLE, WHOLE),
        compiler_params=params(),
        name="attn_rows",
    )(side, own, other)


def hold_kernel(*refs):
    pass


def hold(values, *after):
    many = isinstance(values, tuple)
    values = values if many else (values,)
    out = pl.pallas_call(
        hold_kernel,
        out_shape=tuple(shape(v.shape, v.dtype) for v in values),
        in_specs=[HBM] * (len(values) + len(after)),
        out_specs=(HBM,) * len(values),
        input_output_aliases={k: k for k in range(len(values))},
        name="hold",
    )(*values, *after)
    return out if many else out[0]


def attention_kernel(
    side_ref,
    own_ref,
    other_ref,
    normed_ref,
    bqv_ref,
    strip_ref,
    keep_ref,
    x_ref,
    mod_ref,
    bproj_ref,
    qh_ref,
    kh_ref,
    vh_ref,
    mine_ref,
    theirs_ref,
    attended_ref,
    middle_ref,
    normed_two_ref,
    w_out_ref,
    w_ref,
    flat_ref,
    mix_ref,
    sem,
):
    length, width = x_ref.shape
    hd = width // HEADS
    tile = 384
    wait = fetch_halves(side_ref, own_ref, other_ref, w_ref, sem)
    normed = normed_ref[...]

    def project(slot, lo, cols, at, bias_at):
        def body(o):
            y = mm(normed, w_ref[slot, :, pl.ds(lo + o, tile)])
            if bias_at is not None:
                y = y + bqv_ref[:, pl.ds(bias_at + o, tile)]
            flat_ref[:, pl.ds(at + o, tile)] = y.astype(BF)

        strips(cols, tile, body)

    wait(0)
    project(0, 0, width, 0, 0)
    project(0, width, width, width, None)
    wait(1)
    keep_out = pltpu.make_async_copy(w_ref.at[1, :, pl.ds(width, width)], w_out_ref, sem.at[2])
    keep_out.start()
    project(1, 0, width, 2 * width, width)
    for h in range(HEADS):
        qh_ref[h] = flat_ref[:, h * hd : (h + 1) * hd]
        kh_ref[h] = flat_ref[:, width + h * hd : width + (h + 1) * hd]
        vh_ref[h] = flat_ref[:, 2 * width + h * hd : 2 * width + (h + 1) * hd]
    keep = keep_ref[...] > 0.0

    def head(h, carry):
        sc = mm_nt(qh_ref[h], kh_ref[h]) * (hd**-0.5) + bias_of(strip_ref[h])
        sc = jnp.where(keep, sc, -1e30)
        ex = jnp.exp(sc - jnp.max(sc, axis=-1, keepdims=True))
        soft = ex / jnp.sum(ex, axis=-1, keepdims=True)
        mix_ref[h] = mm(soft.astype(BF), vh_ref[h]).astype(BF)
        return carry

    lax.fori_loop(0, HEADS, head, 0)
    for h in range(HEADS):
        flat_ref[:, h * hd : (h + 1) * hd] = mix_ref[h]
    mixed = flat_ref[:, 0:width]
    mine_ref[:, 0:width] = normed
    theirs_ref[:, 0:width] = normed
    for s, (normed_at, mixed_at) in enumerate(((mine_ref, theirs_ref), (theirs_ref, mine_ref))):

        @pl.when(side_ref[0] == s)
        def _():
            normed_at[:, width:] = normed
            mixed_at[:, width:] = mixed

    def out(o):
        y = mm(mixed, w_ref[1, :, pl.ds(width + o, tile)]) + bproj_ref[:, pl.ds(o, tile)]
        attended_ref[:, pl.ds(o, tile)] = y

    strips(width, tile, out)
    middle = x_ref[...] + mod_ref[2:3, :] * attended_ref[...]
    middle_ref[...] = middle
    n2, _ = normal(middle)
    normed_two_ref[...] = (n2 * (1.0 + mod_ref[4:5, :]) + mod_ref[3:4, :]).astype(BF)
    keep_out.wait()


def attention(side, own, other, normed, b_qv, bias, keep, x, mod, b_proj):
    length, width = x.shape
    hd = width // HEADS
    per_head = shape((HEADS, length, hd), BF)
    return pl.pallas_call(
        attention_kernel,
        out_shape=(
            per_head,
            per_head,
            per_head,
            shape((length, 2 * width), BF),
            shape((length, 2 * width), BF),
            shape((length, width), F32),
            shape((length, width), F32),
            shape((length, width), BF),
            shape((width, width), BF),
        ),
        in_specs=[SCALAR, HBM, HBM] + [WHOLE] * 7,
        out_specs=(WHOLE,) * 8 + (HBM,),
        scratch_shapes=[
            pltpu.VMEM((2, width, 2 * width), BF),
            pltpu.VMEM((length, 3 * width), BF),
            pltpu.VMEM((HEADS, length, hd), BF),
            pltpu.SemaphoreType.DMA((3,)),
        ],
        compiler_params=params(),
        cost_estimate=cost(8 * length * width * width + 4 * length * length * width, 24e6),
        name="attention",
    )(side, own, other, normed, b_qv, bias, keep, x, mod, b_proj)


def fc2_tiles(width, half, tile):
    part = tile // 2
    per = width // part
    at = lambda q: (q % per, half // width + q // per)
    return [pl.BlockSpec((part, width), lambda t, k=k: at(2 * t + k)) for k in range(2)]


def mlp_half(normed_two_ref, b_ref, c0_ref, c1_ref, bf1_ref, hid_ref, slope_ref):
    act, slope = gelu_parts(mm(normed_two_ref[...], b_ref[...]) + bf1_ref[...])
    hid = act.astype(BF)
    hid_ref[...] = hid
    slope_ref[...] = slope
    return mm(hid, jnp.concatenate([c0_ref[...], c1_ref[...]], axis=0))


def mlp_first_kernel(normed_two_ref, b_ref, c0_ref, c1_ref, bf1_ref, hid_ref, slope_ref, part_ref):
    total = mlp_half(normed_two_ref, b_ref, c0_ref, c1_ref, bf1_ref, hid_ref, slope_ref)

    @pl.when(pl.program_id(0) == 0)
    def _():
        part_ref[...] = total

    @pl.when(pl.program_id(0) > 0)
    def _():
        part_ref[...] += total


def mlp_last_kernel(
    normed_two_ref,
    b_ref,
    c0_ref,
    c1_ref,
    bf1_ref,
    part_ref,
    bf2_ref,
    middle_ref,
    cot_ref,
    mod_ref,
    place_ref,
    present_ref,
    hid_ref,
    slope_ref,
    g_branch_ref,
    out_ref,
    sums_ref,
    acc_ref,
):
    t = pl.program_id(0)
    total = mlp_half(normed_two_ref, b_ref, c0_ref, c1_ref, bf1_ref, hid_ref, slope_ref)

    @pl.when(t == 0)
    def _():
        acc_ref[...] = part_ref[...] + total

    @pl.when(t > 0)
    def _():
        acc_ref[...] += total

    @pl.when(t == pl.num_programs(0) - 1)
    def _():
        branch = acc_ref[...] + bf2_ref[...]
        cot = cot_ref[...]
        gate = mod_ref[5:6, :]
        result = middle_ref[...] + gate * branch
        out = jnp.where(present_ref[...] > 0.0, result, 0.0).astype(BF)
        out_ref[...] = mm_tn(place_ref[...], out).astype(BF)
        g_branch = (cot * gate).astype(BF)
        g_branch_ref[...] = g_branch
        sums_ref[0:1, :] = jnp.sum(cot * branch, axis=0, keepdims=True)
        sums_ref[1:2, :] = jnp.sum(g_branch.astype(F32), axis=0, keepdims=True)


def mlp(normed_two, weights, bf1, last=None):
    length, width = normed_two.shape
    half = weights.shape[1] // 2
    tile = 2 * width // 3
    fixed = lambda a: pl.BlockSpec(a.shape, lambda t: (0, 0))
    cols = lambda r: pl.BlockSpec((r, tile), lambda t: (0, t))
    rows = fc2_tiles(width, half, tile)
    whole = lambda r: pl.BlockSpec((r, width), lambda t: (0, 0))
    more = last or ()
    outs = [shape((length, half), BF), shape((length, half), F32)]
    if last:
        outs += [shape((length, width), BF), shape((length, width), BF), shape((8, width), F32)]
    else:
        outs += [shape((length, width), F32)]
    return pl.pallas_call(
        mlp_last_kernel if last else mlp_first_kernel,
        grid=(half // tile,),
        out_shape=tuple(outs),
        in_specs=[fixed(normed_two), cols(width)] + rows + [cols(1)] + [fixed(a) for a in more],
        out_specs=tuple([cols(length), cols(length)] + [whole(o.shape[0]) for o in outs[2:]]),
        scratch_shapes=[pltpu.VMEM((length, width), F32)] if last else [],
        compiler_params=params(),
        cost_estimate=cost(4 * length * width * half, 16e6),
        name="mlp",
    )(normed_two, weights, weights, weights, bf1, *more)


def mlp_back_kernel(
    g_branch_ref,
    b0_ref,
    b1_ref,
    c00_ref,
    c01_ref,
    c10_ref,
    c11_ref,
    slope0_ref,
    slope1_ref,
    middle_ref,
    attended_ref,
    cot_ref,
    mod_ref,
    w_out_ref,
    *rest,
):
    pre0_ref, pre1_ref, bsum_ref, g_middle_ref, g_att_ref, g_mixed_ref, sums_ref, acc_ref = rest[-8:]
    t = pl.program_id(0)
    g_branch = g_branch_ref[...]
    total = None
    for i, (b_ref, c_refs, slope_ref, pre_ref) in enumerate(
        (
            (b0_ref, (c00_ref, c01_ref), slope0_ref, pre0_ref),
            (b1_ref, (c10_ref, c11_ref), slope1_ref, pre1_ref),
        )
    ):
        c = jnp.concatenate([ref[...] for ref in c_refs], axis=0)
        pre = (mm_nt(g_branch, c) * slope_ref[...]).astype(BF)
        pre_ref[...] = pre
        bsum_ref[i : i + 1, :] = jnp.sum(pre.astype(F32), axis=0, keepdims=True)
        part = mm_nt(pre, b_ref[...])
        total = part if total is None else total + part

    @pl.when(t == 0)
    def _():
        acc_ref[...] = total

    @pl.when(t > 0)
    def _():
        acc_ref[...] += total

    @pl.when(t == pl.num_programs(0) - 1)
    def _():
        g_n2 = acc_ref[...]
        n2, inv2 = normal(middle_ref[...])
        sums_ref[0:1, :] = jnp.sum(g_n2, axis=0, keepdims=True)
        sums_ref[1:2, :] = jnp.sum(g_n2 * n2, axis=0, keepdims=True)
        g_middle = cot_ref[...] + normal_back(g_n2 * (1.0 + mod_ref[4:5, :]), n2, inv2)
        g_middle_ref[...] = g_middle
        sums_ref[2:3, :] = jnp.sum(g_middle * attended_ref[...], axis=0, keepdims=True)
        g_att = (g_middle * mod_ref[2:3, :]).astype(BF)
        g_att_ref[...] = g_att
        sums_ref[3:4, :] = jnp.sum(g_att.astype(F32), axis=0, keepdims=True)
        g_mixed_ref[...] = mm_nt(g_att, w_out_ref[...]).astype(BF)


def mlp_back(g_branch, weights, slope0, slope1, middle, attended, cot, mod, w_out, after=()):
    length, width = middle.shape
    half = weights[0].shape[1] // 2
    tile = 2 * width // 3
    fixed = lambda a: pl.BlockSpec(a.shape, lambda t: (0, 0))
    cols = lambda r: pl.BlockSpec((r, tile), lambda t: (0, t))
    rows = fc2_tiles(width, half, tile)
    whole = lambda r: pl.BlockSpec((r, width), lambda t: (0, 0))
    return pl.pallas_call(
        mlp_back_kernel,
        grid=(half // tile,),
        out_shape=(
            shape((length, half), BF),
            shape((length, half), BF),
            shape((2, half), F32),
            shape((length, width), F32),
            shape((length, width), BF),
            shape((length, width), BF),
            shape((8, width), F32),
        ),
        in_specs=[
            fixed(g_branch),
            cols(width),
            cols(width),
            *rows,
            *rows,
            cols(length),
            cols(length),
            fixed(middle),
            fixed(attended),
            fixed(cot),
            fixed(mod),
            fixed(w_out),
        ]
        + [HBM] * len(after),
        out_specs=(
            cols(length),
            cols(length),
            cols(2),
            whole(length),
            whole(length),
            whole(length),
            whole(8),
        ),
        scratch_shapes=[pltpu.VMEM((length, width), F32)],
        compiler_params=params(),
        cost_estimate=cost(8 * length * width * half, 32e6),
        name="mlp_back",
    )(
        g_branch,
        *weights,
        weights[0],
        weights[0],
        weights[1],
        weights[1],
        slope0,
        slope1,
        middle,
        attended,
        cot,
        mod,
        w_out,
        *after,
    )


def heads_back(q_ref, k_ref, v_ref, strip_ref, keep, gm_ref, dq_ref, dk_ref, dv_ref, sums_ref, start):
    scale = q_ref.shape[2] ** -0.5
    length = q_ref.shape[1]

    def head(i, carry):
        h = start + i
        q, k, v, gm = q_ref[h], k_ref[h], v_ref[h], gm_ref[i]
        sc = mm_nt(q, k) * scale + bias_of(strip_ref[h])
        sc = jnp.where(keep, sc, -1e30)
        ex = jnp.exp(sc - jnp.max(sc, axis=-1, keepdims=True))
        soft = ex / jnp.sum(ex, axis=-1, keepdims=True)
        dv_ref[i] = mm_tn(soft.astype(BF), gm).astype(BF)
        dp = mm_nt(gm, v)
        ds = (soft * (dp - jnp.sum(dp * soft, axis=-1, keepdims=True))).astype(BF)
        dq_ref[i] = (mm(ds, k) * scale).astype(BF)
        dk_ref[i] = (mm_tn(ds, q) * scale).astype(BF)
        dsf = ds.astype(F32)
        total = jnp.zeros((GRID, sums_ref.shape[2]), F32)
        blank = jnp.zeros((GRID, sums_ref.shape[2] - length), F32)
        for y in range(GRID):
            rows = jnp.concatenate([dsf[y * GRID : (y + 1) * GRID, :], blank], axis=1)
            by = (GRID - 1 - y) * GRID
            total = total + (pltpu.roll(rows, by, 1) if by else rows)
        sums_ref[i] = total
        return carry

    lax.fori_loop(0, dq_ref.shape[0], head, 0, unroll=2)


def first_heads_kernel(qh_ref, kh_ref, vh_ref, strip_ref, keep_ref, g_mixed_ref, *rest):
    dq_ref, dk_ref, dv_ref, sums_ref, gm_ref = rest[-5:]
    hd = qh_ref.shape[2]
    for i in range(HEADS // 2):
        gm_ref[i] = g_mixed_ref[:, i * hd : (i + 1) * hd]
    heads_back(
        qh_ref, kh_ref, vh_ref, strip_ref, keep_ref[...] > 0.0, gm_ref, dq_ref, dk_ref, dv_ref, sums_ref, 0
    )


def first_heads(qh, kh, vh, strip, keep, g_mixed, after=()):
    heads, length, hd = qh.shape
    some = shape((heads // 2, length, hd), BF)
    return pl.pallas_call(
        first_heads_kernel,
        out_shape=(some, some, some, shape((heads // 2,) + strip.shape[1:], F32)),
        in_specs=[WHOLE] * 6 + [HBM] * len(after),
        out_specs=(WHOLE,) * 4,
        scratch_shapes=[pltpu.VMEM((heads // 2, length, hd), BF)],
        compiler_params=params(),
        cost_estimate=cost(5 * length * length * heads * hd, 16e6),
        name="first_heads",
    )(qh, kh, vh, strip, keep, g_mixed, *after)


def last_heads_kernel(
    side_ref,
    qh_ref,
    kh_ref,
    vh_ref,
    strip_ref,
    keep_ref,
    g_mixed_ref,
    g_att_ref,
    fq_ref,
    fk_ref,
    fv_ref,
    fsum_ref,
    *rest,
):
    mine_ref, top_ref, low_ref, lo_ref, hi_ref, sums_ref, both_ref, gm_ref, dq_ref, dk_ref, dv_ref, strips_ref = rest[-12:]
    theirs_ref = both_ref
    width = g_mixed_ref.shape[1]
    hd = qh_ref.shape[2]
    half = HEADS // 2
    for i in range(half):
        gm_ref[i] = g_mixed_ref[:, (half + i) * hd : (half + i + 1) * hd]
    heads_back(
        qh_ref, kh_ref, vh_ref, strip_ref, keep_ref[...] > 0.0, gm_ref, dq_ref, dk_ref, dv_ref, strips_ref, half
    )
    for s, (qk_at, v_at) in enumerate(((mine_ref, theirs_ref), (theirs_ref, mine_ref))):

        @pl.when(side_ref[0] == s)
        def _():
            for h in range(HEADS):
                q, k, v = (fq_ref, fk_ref, fv_ref) if h < half else (dq_ref, dk_ref, dv_ref)
                i = h % half
                qk_at[:, h * hd : (h + 1) * hd] = q[i]
                qk_at[:, width + h * hd : width + (h + 1) * hd] = k[i]
                v_at[:, h * hd : (h + 1) * hd] = v[i]
            v_at[:, width:] = g_att_ref[...]
            sums_ref[0:1, :] = jnp.sum(qk_at[:, 0:width].astype(F32), axis=0, keepdims=True)
            sums_ref[1:2, :] = jnp.sum(v_at[:, 0:width].astype(F32), axis=0, keepdims=True)

    length = both_ref.shape[0]
    top_ref[...] = both_ref[0 : length // 2, :]
    low_ref[...] = both_ref[length // 2 :, :]
    lanes = lo_ref.shape[1]
    for part, ref in enumerate((fsum_ref, strips_ref)):
        lo = jnp.zeros((half, lanes), F32)
        hi = jnp.zeros((half, lanes), F32)
        j = lax.broadcasted_iota(jnp.int32, lo.shape, 1) % GRID
        for i in range(GRID):
            k = GRID - 1 - i
            row = ref[:, i, :]
            a = jnp.where(j < GRID - k, row, 0.0)
            lo = lo + (pltpu.roll(a, k, 1) if k else a)
            if k:
                hi = hi + pltpu.roll(jnp.where(j < GRID - k, 0.0, row), lanes - (GRID - k), 1)
        lo_ref[part * half : (part + 1) * half, :] = lo
        hi_ref[part * half : (part + 1) * half, :] = hi


def last_heads(side, qh, kh, vh, strip, keep, g_mixed, g_att, firsts, after=()):
    length, width = g_mixed.shape
    heads, _, hd = qh.shape
    per_head = pltpu.VMEM((heads // 2, length, hd), BF)
    window = shape((heads, strip.shape[2]), F32)
    return pl.pallas_call(
        last_heads_kernel,
        out_shape=(
            shape((length, 2 * width), BF),
            shape((length // 2, 2 * width), BF),
            shape((length // 2, 2 * width), BF),
            window,
            window,
            shape((8, width), F32),
        ),
        in_specs=[SCALAR] + [WHOLE] * 11 + [HBM] * len(after),
        out_specs=(WHOLE,) * 6,
        scratch_shapes=[pltpu.VMEM((length, 2 * width), BF)]
        + [per_head] * 4 + [pltpu.VMEM((heads // 2,) + strip.shape[1:], F32)],
        compiler_params=params(),
        cost_estimate=cost(5 * length * length * width, 16e6),
        name="last_heads",
    )(side, qh, kh, vh, strip, keep, g_mixed, g_att, *firsts, *after)


def tokens_back_kernel(
    side_ref,
    own_ref,
    other_ref,
    mine_ref,
    top_ref,
    low_ref,
    x_ref,
    g_middle_ref,
    mod_ref,
    place_ref,
    *rest,
):
    out_ref, sums_ref, w_ref, acc_ref, qk_ref, v_ref, sem = rest[-7:]
    length, width = x_ref.shape
    wait = fetch_halves(side_ref, own_ref, other_ref, w_ref, sem)
    half = length // 2

    @pl.when(side_ref[0] == 0)
    def _():
        qk_ref[...] = mine_ref[...]
        v_ref[0:half, :] = top_ref[:, 0:width]
        v_ref[half:, :] = low_ref[:, 0:width]

    @pl.when(side_ref[0] == 1)
    def _():
        qk_ref[0:half, :] = top_ref[...]
        qk_ref[half:, :] = low_ref[...]
        v_ref[...] = mine_ref[:, 0:width]

    wait(0)
    acc_ref[...] = mm_nt(qk_ref[...], w_ref[0])
    wait(1)
    g_n1 = acc_ref[...] + mm_nt(v_ref[...], w_ref[1, :, 0:width])
    n1, inv1 = normal(x_ref[...])
    sums_ref[0:1, :] = jnp.sum(g_n1, axis=0, keepdims=True)
    sums_ref[1:2, :] = jnp.sum(g_n1 * n1, axis=0, keepdims=True)
    g_x = g_middle_ref[...] + normal_back(g_n1 * (1.0 + mod_ref[1:2, :]), n1, inv1)
    out_ref[...] = mm_tn(place_ref[...], g_x.astype(BF)).astype(BF)


def tokens_back(side, own, other, mine, theirs, x, g_middle, mod, place, after=()):
    length, width = x.shape
    return pl.pallas_call(
        tokens_back_kernel,
        out_shape=(shape((length, width), BF), shape((8, width), F32)),
        in_specs=[SCALAR, HBM, HBM] + [WHOLE] * 7 + [HBM] * len(after),
        out_specs=(WHOLE,) * 2,
        scratch_shapes=[
            pltpu.VMEM((2, width, 2 * width), BF),
            pltpu.VMEM((length, width), F32),
            pltpu.VMEM((length, 2 * width), BF),
            pltpu.VMEM((length, width), BF),
            pltpu.SemaphoreType.DMA((2,)),
        ],
        compiler_params=params(),
        cost_estimate=cost(6 * length * width * width, 16e6),
        name="tokens_back",
    )(side, own, other, mine, *theirs, x, g_middle, mod, place, *after)


def local(
    n,
    tokens,
    condition,
    kept_index,
    kept_count,
    cotangent,
    w_ada,
    w_qkv,
    w_proj,
    w_fc1,
    w_fc2,
    b_ada,
    b_qv,
    b_proj,
    b_fc1,
    b_fc2,
    rel_table,
):
    side = lax.axis_index("stream")
    chip = lax.axis_index("dp")
    length, width = tokens.shape[2], tokens.shape[3]
    ff = w_fc1.shape[1]
    rows = width // n
    cut = ff // (2 * n)
    first = side == 0
    side_word = side.astype(jnp.int32).reshape(1)
    chip_word = chip.astype(jnp.int32).reshape(1)

    order_first, order_parts = orders_out(n)
    firsts = tuple(part[-1] for part in order_parts)

    ordinal = jnp.arange(length, dtype=jnp.int32)
    count = jnp.where(first, length, kept_count[0])
    position = jnp.where(first, ordinal, kept_index[0])
    place = ((position[None, :] == ordinal[:, None]) & (ordinal[None, :] < count)).astype(BF)
    present = jnp.sum(place.astype(F32), axis=1)
    keep = present.reshape(1, length)
    present = present.reshape(length, 1)
    x = mm(place, tokens[0, 0])
    cot = mm(place, cotangent[0, 0])
    bias = bias_strip(rel_table)

    cond = condition[0, 0]
    sig = jax.nn.sigmoid(cond)
    cond_act = (cond * sig).astype(BF)
    shard_a = attn_shard(side_word, w_qkv, w_proj)
    all_a = Gathering(chip_word, shard_a, n)
    acts = trade(hold(jnp.broadcast_to(cond_act[None], (n, width)), shard_a))
    acts_part = lax.dynamic_slice_in_dim(acts, chip * rows, rows, axis=1)
    shard_bc = mlp_shard(n, side_word, w_fc1, w_fc2, after=(shard_a,))
    last = all_a.step(shard_bc, bias, x, cot, acts_part)
    all_bc = Gathering(chip_word, hold(shard_bc, *last), n)
    for _ in range(len(order_parts[0]) - 2 + len(order_first) - 1):
        last = all_a.step(*last)
    while all_bc.turn < all_bc.cut_at:
        last = all_bc.step(*last)
    acts_twin = swap_stream(acts_part)
    if {p[-1] for p in order_parts} == {p[0] for p in order_parts}:
        last, result_a, on_bc = merge_steps(all_a, all_bc, acts_twin)
        last = on_bc()
    else:
        last = all_a.step(*last, acts_twin)
        result_a = all_a.result
        last = all_bc.step(*last)
    a_own = result_a(*last)
    a_other = swap_stream(a_own)
    mod_part = trade(hold(mm(acts_part, w_ada), a_own))
    last = (mod_part,)
    while not all_bc.done():
        last = all_bc.step(*last)
    modulation = jnp.sum(mod_part, axis=0) + b_ada
    mod = modulation.reshape(6, width)
    n1, _ = normal(x)
    normed = (n1 * (1.0 + mod[1]) + mod[0]).astype(BF)
    qh, kh, vh, lhs_mine, lhs_theirs, attended, middle, normed_two, w_out = attention(
        side_word,
        a_own,
        a_other,
        normed,
        b_qv.reshape(1, -1),
        bias,
        keep,
        x,
        mod,
        b_proj.reshape(1, -1),
    )

    bf1 = jnp.transpose(b_fc1.reshape(n, 2, 2, cut // 2), (1, 2, 0, 3)).reshape(2, 1, ff // 2)
    bf1_own, bf1_other = jnp.where(first, bf1[0], bf1[1]), jnp.where(first, bf1[1], bf1[0])
    bf2 = b_fc2.reshape(1, -1)
    bc_own = all_bc.result(normed_two, bf1_own, bf1_other, bf2, present, place)
    bc_other = swap_stream(bc_own)
    lhs_twin = swap_stream(lhs_theirs)
    n2_twin = swap_stream(normed_two)
    hid0, slope0, part = mlp(normed_two, bc_own, bf1_own)
    hid1, slope1, g_branch, out_tokens, sums_a = mlp(
        normed_two,
        bc_other,
        bf1_other,
        (part, bf2, middle, cot, mod, place, present),
    )

    parts_c = product(
        chip_word, hid0, swap_stream(hid1), g_branch, swap_stream(g_branch), width, n, firsts
    )
    sum_c = Reduction(chip_word, parts_c, n)
    pre0, pre1, pre_sum, g_middle, g_att, g_mixed, sums_b = mlp_back(
        g_branch,
        (bc_own, bc_other),
        slope0,
        slope1,
        middle,
        attended,
        cot,
        mod,
        w_out,
        after=(parts_c[0][0], lhs_twin, n2_twin),
    )
    kept = step([sum_c], g_mixed)
    pre_twin = swap_stream(pre1)
    one = first_heads(qh, kh, vh, bias, keep, g_mixed, after=kept + (pre_twin,))
    kept = step([sum_c], one[0])
    kept = step([sum_c], *kept)
    parts_b = product(
        chip_word,
        normed_two,
        n2_twin,
        pre0,
        pre_twin,
        width,
        n,
        firsts,
        after=kept,
    )
    sum_b = Reduction(chip_word, parts_b, n)
    g_mine, top, low, lo, hi, sums_c = last_heads(
        side_word, qh, kh, vh, bias, keep, g_mixed, g_att, one, after=(parts_b[0][0],)
    )
    g_theirs = (top, low)
    g_twin = (swap_stream(top), swap_stream(low))
    while not sum_c.done():
        step([sum_c])
    d_c = sum_c.result(g_mine)
    kept = step([sum_b], g_mine) + g_twin
    grad_tokens, sums_d = tokens_back(
        side_word, a_own, a_other, g_mine, g_theirs, x, g_middle, mod, place, after=kept
    )
    sums_a, sums_b, sums_c, lo, hi, pre_sum = hold((sums_a, sums_b, sums_c, lo, hi, pre_sum), sums_d)
    g_mod = jnp.concatenate([sums_d[0], sums_d[1], sums_b[2], sums_b[0], sums_b[1], sums_a[0]])
    g_mod = g_mod.astype(BF).astype(F32).reshape(-1, 128)
    pre_sum = jnp.where(first, pre_sum, jnp.concatenate([pre_sum[1:], pre_sum[:1]]))
    pre_sum = jnp.transpose(pre_sum.reshape(2, 2, n, cut // 2), (2, 0, 1, 3))
    smalls = [
        sums_c[0],
        sums_c[1],
        sums_b[3],
        pre_sum.reshape(-1),
        sums_a[1],
        table_of(lo, hi).reshape(-1),
    ]
    sizes = [t.shape[0] for t in smalls]
    packed = jnp.concatenate(smalls)
    packed = jnp.pad(packed, (0, 128 * SUM_ROWS - packed.shape[0])).reshape(-1, 128)
    mod_rows = g_mod.shape[0]
    pad = -mod_rows % 8
    told = jnp.concatenate([packed, jnp.pad(g_mod, ((0, pad), (0, 0)))], axis=0)
    group = told.shape[0] - SUM_ROWS
    bits = all_bits(n)[::-1]
    kept = (d_c,)
    for b in bits[:2]:
        came = swap(told, b, n)
        if not sum_b.done():
            kept = step([sum_b], told, *kept)
        told = meet(chip_word, told, came, b, group, after=kept)
    while not sum_b.done():
        kept = step([sum_b], *kept)
    came = swap(told, bits[2], n)
    parts_a = product(
        chip_word, lhs_mine, lhs_twin, g_mine, g_twin, width, n, firsts, after=(told,) + kept
    )
    sum_a = Reduction(chip_word, parts_a, n)
    told = meet(chip_word, told, came, bits[2], group, after=(parts_a[0][0],))
    grad_w_fc2 = fc2_rows(side_word, d_c, swap_stream(d_c))
    d_b = sum_b.result(parts_a[0][0])
    grad_w_fc1 = fc1_rows(n, side_word, d_b, swap_stream(d_b))
    for b in bits[3:]:
        told = meet(chip_word, told, swap(told, b, n), b, group)
    kept = step([sum_a], told, grad_w_fc2, grad_w_fc1)
    twin = swap_stream(told)

    def mods_of(t):
        return t[SUM_ROWS:].reshape(n, -1, 128)[:, :mod_rows].reshape(n, -1)

    g_own, g_twin = mods_of(told), mods_of(twin)
    grad_w_ada = mm_tn(acts_part, g_own.astype(BF)) + mm_tn(acts_twin, g_twin.astype(BF))
    grad_b_ada = jnp.sum(g_own, axis=0) + jnp.sum(g_twin, axis=0)
    kept = step([sum_a], *kept, grad_w_ada, grad_b_ada)
    while not sum_a.done():
        kept = step([sum_a], *kept)
    g_acts = trade(hold(mm_nt(g_own.astype(BF), w_ada), *kept)).reshape(width)
    grad_condition = g_acts * sig * (1.0 + cond * (1.0 - sig))
    packed = (told[:SUM_ROWS] + twin[:SUM_ROWS]).reshape(-1)
    parts, at = [], 0
    for size in sizes:
        parts.append(packed[at : at + size])
        at += size

    d_a = sum_a.result(g_acts, *parts)
    grad_w_qkv, grad_w_proj = attn_rows(side_word, d_a, swap_stream(d_a))
    return (
        out_tokens[None, None],
        grad_tokens[None, None],
        grad_condition[None, None],
        grad_w_ada,
        grad_w_qkv,
        grad_w_proj,
        grad_w_fc1,
        grad_w_fc2,
        grad_b_ada,
        jnp.concatenate(parts[:2]),
        parts[2],
        parts[3],
        parts[4],
        parts[5].reshape(rel_table.shape),
    )


def solution(mesh):
    n = mesh.shape["dp"]

    def body(*args):
        return local(n, *args)

    return jax.shard_map(
        body,
        mesh=mesh,
        in_specs=(
            P("stream", "dp", None, None),
            P("stream", "dp", None),
            P("dp", None),
            P("dp"),
            P("stream", "dp", None, None),
            P("dp", None),
            P("dp", None),
            P("dp", None),
            P("dp", None),
            P("dp", None),
            P(),
            P(),
            P(),
            P(),
            P(),
            P(),
        ),
        out_specs=(
            P("stream", "dp", None, None),
            P("stream", "dp", None, None),
            P("stream", "dp", None),
            P("dp", None),
            P("dp", None),
            P("dp", None),
            P("dp", None),
            P("dp", None),
            P(),
            P(),
            P(),
            P(),
            P(),
            P(),
        ),
        check_vma=False,
    )
```

```python
import functools
import math

import jax
import jax.numpy as jnp
from jax import lax
from jax.experimental import pallas as pl
from jax.experimental.pallas import tpu as pltpu
from jax.sharding import PartitionSpec as P

HEADS = 16
GRID = 16
BF = jnp.bfloat16
F32 = jnp.float32


def swap(v, bit, n):
    return lax.ppermute(v, "dp", [(i, i ^ bit) for i in range(n)])


def swap_stream(v):
    return lax.ppermute(v, "stream", [(0, 1), (1, 0)])


def axis_bits(n):
    k = n.bit_length() - 1
    s = k // 3
    xs = [1 << i for i in range(s)]
    ys = [1 << (s + i) for i in range(s)]
    zs = [1 << i for i in range(2 * s, k)]
    return xs, ys, zs


def all_bits(n):
    return [1 << i for i in range(n.bit_length() - 1)]


def orders_out(n):
    xs, ys, zs = axis_bits(n)
    near = zs[:1]
    return zs[1:][::-1], (near + ys + xs, xs + near + ys, ys + xs + near)


def trade(v):
    return lax.all_to_all(v, "dp", 0, 0, tiled=True)


def mm(a, b):
    return lax.dot_general(a, b, (((1,), (0,)), ((), ())), preferred_element_type=F32)


def mm_nt(a, b):
    return lax.dot_general(a, b, (((1,), (1,)), ((), ())), preferred_element_type=F32)


def mm_tn(a, b):
    return lax.dot_general(a, b, (((0,), (0,)), ((), ())), preferred_element_type=F32)


def normal(v):
    center = v - jnp.mean(v, axis=-1, keepdims=True)
    inv = lax.rsqrt(jnp.mean(center * center, axis=-1, keepdims=True) + 1e-06)
    return center * inv, inv


def normal_back(g, n, inv):
    return inv * (g - jnp.mean(g, axis=-1, keepdims=True) - n * jnp.mean(g * n, axis=-1, keepdims=True))


def bias_windows(table):
    w = 2 * GRID - 1
    t = jnp.transpose(table.reshape(w, w, HEADS)[::-1, ::-1], (2, 0, 1))
    t = jnp.pad(t, ((0, 0), (0, 1), (0, 1))).reshape(HEADS, w + 1, 2, GRID)
    return t[:, :, 0].reshape(HEADS, -1), t[:, :, 1].reshape(HEADS, -1)


def table_of(lo, hi):
    w = 2 * GRID - 1
    t = jnp.stack([lo.reshape(HEADS, w + 1, GRID), hi.reshape(HEADS, w + 1, GRID)], axis=2)
    t = t.reshape(HEADS, w + 1, 2 * GRID)[:, :w, :w]
    return jnp.transpose(t, (1, 2, 0))[::-1, ::-1].reshape(w * w, HEADS)


def gelu_parts(x):
    k = math.sqrt(2.0 / math.pi)
    th = jnp.tanh(k * (x + 0.044715 * x * x * x))
    value = 0.5 * x * (1.0 + th)
    slope = 0.5 * (1.0 + th) + 0.5 * x * (1.0 - th * th) * k * (1.0 + 3 * 0.044715 * x * x)
    return value, slope


VMEM_BYTES = 56 * 1024 * 1024
SUM_ROWS = 200
WHOLE = pl.BlockSpec(memory_space=pltpu.VMEM)
HBM = pl.BlockSpec(memory_space=pl.ANY)
SCALAR = pl.BlockSpec(memory_space=pltpu.SMEM)


def shape(dims, dtype):
    return jax.ShapeDtypeStruct(dims, dtype)


def params():
    return pltpu.CompilerParams(vmem_limit_bytes=VMEM_BYTES)


def cost(flops, size):
    return pl.CostEstimate(flops=int(flops), bytes_accessed=int(size), transcendentals=0)


def strips(total, tile, body):
    def step(i, carry):
        body(pl.multiple_of(i * tile, tile))
        return carry

    lax.fori_loop(0, total // tile, step, 0)


def fetch_halves(side_ref, own_ref, other_ref, w_ref, sem):
    side = side_ref[0]
    mine = pltpu.make_async_copy(own_ref, w_ref.at[side], sem.at[side])
    twin = pltpu.make_async_copy(other_ref, w_ref.at[1 - side], sem.at[1 - side])
    mine.start()
    twin.start()

    def wait(slot):
        pltpu.make_async_copy(own_ref, w_ref.at[slot], sem.at[slot]).wait()

    return wait


def pieces(n, rows, cut, s):
    half = cut // 2
    for part in range(2):
        for k in range(n):
            yield (k * 2 + s) * cut + part * half, (part * n + k) * half, half


def fc1_rows_kernel(n, side_ref, own_ref, other_ref, out_ref):
    rows, ff = out_ref.shape
    cut = ff // (2 * n)
    for s in range(2):

        @pl.when(side_ref[0] == s)
        def _():
            for half, ref in ((s, own_ref), (1 - s, other_ref)):
                for src, dst, w in pieces(n, rows, cut, half):
                    out_ref[:, src : src + w] = ref[:, ff // 2 + dst : ff // 2 + dst + w]


def fc1_rows(n, side, own, other):
    return pl.pallas_call(
        functools.partial(fc1_rows_kernel, n),
        out_shape=shape(own.shape, F32),
        in_specs=[SCALAR, WHOLE, WHOLE],
        out_specs=WHOLE,
        compiler_params=params(),
        name="fc1_rows",
    )(side, own, other)


def strip_kernel(lo_ref, hi_ref, out_ref):
    lanes = lo_ref.shape[1]
    lo, hi = lo_ref[...], hi_ref[...]
    j = lax.broadcasted_iota(jnp.int32, lo.shape, 1) % GRID
    for i in range(GRID):
        k = GRID - 1 - i
        a = pltpu.roll(lo, lanes - k, 1) if k else lo
        out_ref[:, i, :] = jnp.where(j < GRID - k, a, pltpu.roll(hi, GRID - k, 1))


def bias_strip(table):
    lo, hi = bias_windows(table)
    return pl.pallas_call(
        strip_kernel,
        out_shape=shape((HEADS, GRID, lo.shape[1]), F32),
        in_specs=[WHOLE, WHOLE],
        out_specs=WHOLE,
        name="bias_strip",
    )(lo, hi)


def bias_of(strip):
    return jnp.concatenate(
        [strip[:, (GRID - 1 - y) * GRID : (2 * GRID - 1 - y) * GRID] for y in range(GRID)], axis=0
    )


def put(i, pos):
    return (i >> pos) << (pos + 1) | (i & ((1 << pos) - 1))


def attn_shard_kernel(side_ref, qkv_ref, proj_ref, out_ref):
    width = proj_ref.shape[1]
    for s in range(2):

        @pl.when(side_ref[0] == s)
        def _():
            if s == 0:
                out_ref[0] = qkv_ref[:, 0 : 2 * width]
            else:
                out_ref[0, :, 0:width] = qkv_ref[:, 2 * width :]
                out_ref[0, :, width:] = proj_ref[...]


def mlp_shard_kernel(n, side_ref, f1_ref, f2_ref, *rest):
    out_ref = rest[-1]
    rows, ff = f1_ref.shape
    width = f2_ref.shape[1]
    cut = ff // (2 * n)
    for s in range(2):

        @pl.when(side_ref[0] == s)
        def _():
            for src, dst, w in pieces(n, rows, cut, s):
                out_ref[0, :, dst : dst + w] = f1_ref[:, src : src + w]
            for part in range(2):
                lo = s * cut + part * rows
                cols = slice(ff // 2 + part * width, ff // 2 + (part + 1) * width)
                out_ref[0, :, cols] = f2_ref[lo : lo + rows, :]


def mlp_shard(n, side, f1, f2, after=()):
    return pl.pallas_call(
        functools.partial(mlp_shard_kernel, n),
        out_shape=shape((1,) + f1.shape, BF),
        in_specs=[SCALAR, WHOLE, WHOLE] + [HBM] * len(after),
        out_specs=WHOLE,
        compiler_params=params(),
        name="mlp_shard",
    )(side, f1, f2, *after)


def attn_shard(side, w_qkv, w_proj):
    rows, width = w_proj.shape
    return pl.pallas_call(
        attn_shard_kernel,
        out_shape=shape((1, rows, 2 * width), BF),
        in_specs=[SCALAR, WHOLE, WHOLE],
        out_specs=WHOLE,
        compiler_params=params(),
        name="attn_shard",
    )(side, w_qkv, w_proj)


def join_kernel(jobs, chip_ref, *refs):
    outs = refs[-sum(len(cols) for _, cols in jobs) :]
    at = 0
    for k, (bit, cols) in enumerate(jobs):
        v_ref, r_ref = refs[2 * k], refs[2 * k + 1]
        m = v_ref.shape[0]
        up = (chip_ref[0] & bit) // bit
        lo = 0
        for c in cols:
            for i in range(m):
                outs[at][up * m + i] = v_ref[i, :, lo : lo + c]
                outs[at][(1 - up) * m + i] = r_ref[i, :, lo : lo + c]
            lo += c
            at += 1


def join(chip, jobs, after=()):
    flat = [t for v, r, _, _ in jobs for t in (v, r)]
    return pl.pallas_call(
        functools.partial(join_kernel, [(bit, cols) for _, _, bit, cols in jobs]),
        out_shape=tuple(
            shape((2 * v.shape[0], v.shape[1], c), v.dtype) for v, _, _, cols in jobs for c in cols
        ),
        in_specs=[SCALAR] + [WHOLE] * len(flat) + [HBM] * len(after),
        out_specs=(WHOLE,) * sum(len(cols) for _, _, _, cols in jobs),
        compiler_params=params(),
        name="join",
    )(chip, *flat, *after)


def assemble_kernel(orders, chip_ref, *refs):
    out_ref = refs[-1]
    lo = 0
    m = out_ref.shape[0] // 2
    for k, bits in enumerate(orders):
        v_ref, r_ref = refs[2 * k], refs[2 * k + 1]
        c = v_ref.shape[2]
        last = bits[-1]
        up = (chip_ref[0] & last) // last
        lead = bits[:-1][::-1]
        for i in range(m):
            base = sum(b for j, b in enumerate(lead) if (i >> (len(lead) - 1 - j)) & 1)
            out_ref[base + up * last, :, lo : lo + c] = v_ref[i]
            out_ref[base + (1 - up) * last, :, lo : lo + c] = r_ref[i]
        lo += c


def assemble(chip, orders, pairs, after=()):
    flat = [t for pair in pairs for t in pair]
    m, rows = 1 << (len(orders[0]) - 1), flat[0].shape[1]
    cols = sum(v.shape[2] for v, _ in pairs)
    out = pl.pallas_call(
        functools.partial(assemble_kernel, orders),
        out_shape=shape((2 * m, rows, cols), BF),
        in_specs=[SCALAR] + [WHOLE] * len(flat) + [HBM] * len(after),
        out_specs=WHOLE,
        compiler_params=params(),
        name="assemble",
    )(chip, *flat, *after)
    return out.reshape(2 * m * rows, cols)


class Gathering:
    def __init__(self, chip, v, n):
        first, parts = orders_out(n)
        self.chip, self.n = chip, n
        self.orders = [first + part for part in parts]
        self.turn, self.cut_at = 0, len(first)
        self.parts = [v]
        self.exchange()

    def exchange(self):
        self.came = [swap(v, self.orders[k][self.turn], self.n) for k, v in enumerate(self.parts)]
        self.turn += 1

    def step(self, *after):
        jobs = []
        for k, (v, r) in enumerate(zip(self.parts, self.came)):
            c = v.shape[2]
            cut = (c // 3,) * 3 if self.turn == self.cut_at else (c,)
            jobs.append((v, r, self.orders[k][self.turn - 1], cut))
        self.parts = list(join(self.chip, jobs, after))
        self.exchange()
        return tuple(self.parts)

    def done(self):
        return self.turn == len(self.orders[0])

    def result(self, *after):
        return assemble(self.chip, self.orders, tuple(zip(self.parts, self.came)), after=after)


def merge_kernel(bits, mates, chip_ref, *refs):
    small, (v_ref, r_ref), outs = refs[:6], refs[6:8], refs[-3:]
    up = lambda bit: (chip_ref[0] & bit) // bit
    m = small[0].shape[0]
    c = small[0].shape[2]
    far = v_ref.shape[0]
    for k in range(3):
        for ref, side in ((small[2 * k], up(bits[k])), (small[2 * k + 1], 1 - up(bits[k]))):
            for i in range(m):
                outs[k][side * m + i] = ref[i]
    for k in range(3):
        out_ref = outs[mates[k]]
        wide = v_ref.shape[2] // 3
        for ref, side in ((v_ref, up(bits[3])), (r_ref, 1 - up(bits[3]))):
            for h in range(wide // c):
                for i in range(far):
                    lo = k * wide + h * c
                    out_ref[2 * m + h * 2 * far + side * far + i] = ref[i, :, lo : lo + c]


def cross_kernel(bits, skip, chip_ref, *refs):
    outs = refs[-3:]
    for k, bit in enumerate(bits):
        v_ref, r_ref, out_ref = refs[2 * k], refs[2 * k + 1], outs[k]
        up = (chip_ref[0] & bit) // bit
        c = v_ref.shape[2]
        m = out_ref.shape[0] // 2
        for ref, side in ((v_ref, up), (r_ref, 1 - up)):
            for h in range(out_ref.shape[2] // c):
                for i in range(m):
                    out_ref[side * m + i, :, h * c : (h + 1) * c] = ref[skip + h * m + i]


def merge_steps(small, large, *after):
    n, turn = small.n, len(small.orders[0]) - 1
    next_small = [order[turn] for order in small.orders]
    next_large = [order[large.cut_at] for order in large.orders]
    mates = [next_small.index(bit) for bit in next_large]
    bits = [order[turn - 1] for order in small.orders] + [large.orders[0][large.cut_at - 1]]
    v, r = large.parts[0], large.came[0]
    _, rows, c = small.parts[0].shape
    m = 2 * small.parts[0].shape[0]
    far = 2 * v.shape[0]
    wide = v.shape[2] // 3
    flat = [t for pair in zip(small.parts, small.came) for t in pair]
    outs = pl.pallas_call(
        functools.partial(merge_kernel, bits, mates),
        out_shape=(shape((m + far * (wide // c), rows, c), BF),) * 3,
        in_specs=[SCALAR] + [WHOLE] * 8 + [HBM] * len(after),
        out_specs=(WHOLE,) * 3,
        compiler_params=params(),
        name="merge",
    )(small.chip, *flat, v, r, *after)
    came = [swap(t, bit, n) for t, bit in zip(outs, next_small)]

    def small_result(*after):
        return assemble(small.chip, small.orders, tuple(zip(outs, came)), after=after)

    def large_on(*after):
        pairs = [t for k in range(3) for t in (outs[mates[k]], came[mates[k]])]
        parts = pl.pallas_call(
            functools.partial(cross_kernel, next_large, m),
            out_shape=(shape((2 * far, rows, wide), BF),) * 3,
            in_specs=[SCALAR] + [WHOLE] * 6 + [HBM] * len(after),
            out_specs=(WHOLE,) * 3,
            compiler_params=params(),
            name="cross",
        )(large.chip, *pairs, *after)
        large.parts = list(parts)
        large.turn = large.cut_at + 1
        large.exchange()
        return tuple(parts)

    return outs, small_result, large_on


def product_kernel(n, firsts, steps, half_step, count, chip_ref, l0_ref, l1_ref, *rest):
    turned_ref = rest[-1]
    r_refs = rest[:count]
    outs = rest[-7:-1]
    t = pl.program_id(0)
    length = l0_ref.shape[0]
    width = turned_ref.shape[1]
    rows = width // n

    @pl.when(t == 0)
    def _():
        for k in range(turned_ref.shape[0]):
            cols = slice(k * width, (k + 1) * width)
            turned_ref[k, :, 0:length] = l0_ref[:, cols].T
            turned_ref[k, :, length:] = l1_ref[:, cols].T

    slot = jnp.where(t >= half_step, turned_ref.shape[0] - 1, 0)
    value, at = 0.0, 0
    for r_ref in r_refs:
        rows_here = r_ref.shape[0]
        value = value + mm(turned_ref[slot, :, at : at + rows_here], r_ref[...])
        at += rows_here
    for part, (bit, (lo, hi)) in enumerate(zip(firsts, steps)):
        pos = bit.bit_length() - 1
        for up in range(2):

            @pl.when((t >= lo) & (t < hi) & ((chip_ref[0] & bit) // bit == up))
            def _():
                for i in range(n // 2):
                    at = put(i, pos)
                    for goes, ref in ((up, outs[2 * part]), (1 - up, outs[2 * part + 1])):
                        k = at + goes * bit
                        ref[i] = value[k * rows : (k + 1) * rows].astype(BF)


def product(chip, l0, l1, r0, r1, width, n, firsts, after=()):
    length = l0.shape[0]
    tile = width // 3
    per = width // tile
    rights = (r0,) + (r1 if isinstance(r1, tuple) else (r1,))
    two_l, two_r = l0.shape[1] > width, r0.shape[1] > width
    cols = (2 * width // 3,) * 3
    steps = []
    for c in cols:
        lo = steps[-1][1] if steps else 0
        steps.append((lo, lo + c // tile))
    left = pl.BlockSpec(l0.shape, lambda t: (0, 0))
    right = [pl.BlockSpec((r.shape[0], tile), lambda t: (0, t if two_r else t % per)) for r in rights]
    spec = lambda lo, hi: pl.BlockSpec(
        (n // 2, width // n, tile), lambda t: (0, 0, jnp.clip(t - lo, 0, hi - lo - 1))
    )
    out = pl.pallas_call(
        functools.partial(product_kernel, n, firsts, steps, per, len(rights)),
        grid=(2 * per,),
        out_shape=tuple(shape((n // 2, width // n, c), BF) for c in cols for _ in range(2)),
        in_specs=[SCALAR, left, left] + right + [HBM] * len(after),
        out_specs=tuple(spec(*s) for s in steps for _ in range(2)),
        scratch_shapes=[pltpu.VMEM((1 + two_l, width, 2 * length), BF)],
        compiler_params=params(),
        cost_estimate=cost(8 * length * width * width, 12e6),
        name="product",
    )(chip, l0, l1, *rights, *after)
    return tuple((out[2 * k], out[2 * k + 1]) for k in range(3))


def split_kernel(jobs, chip_ref, *refs):
    outs = refs[-2 * len(jobs) :]
    at = 0
    for k, (bit, pos, count) in enumerate(jobs):
        keep_ref, send_ref = outs[2 * k], outs[2 * k + 1]
        up = (chip_ref[0] & bit) // bit
        lo = 0
        for _ in range(count):
            v_ref, r_ref = refs[at], refs[at + 1]
            at += 2
            c = v_ref.shape[2]
            for i in range(keep_ref.shape[0]):
                for out_ref, goes in ((send_ref, 1 - up), (keep_ref, up)):
                    j = put(i, pos) + goes * (1 << pos)
                    total = v_ref[j].astype(F32) + r_ref[j].astype(F32)
                    out_ref[i, :, lo : lo + c] = total.astype(BF)
            lo += c


def split(chip, jobs, after=()):
    flat = [t for pairs, _, _ in jobs for pair in pairs for t in pair]
    outs, plan = [], []
    for pairs, bit, left in jobs:
        m, rows, _ = pairs[0][0].shape
        cols = sum(v.shape[2] for v, _ in pairs)
        outs += [shape((m // 2, rows, cols), BF)] * 2
        plan.append((bit, len(left) - 1 - left.index(bit), len(pairs)))
    out = pl.pallas_call(
        functools.partial(split_kernel, plan),
        out_shape=tuple(outs),
        in_specs=[SCALAR] + [WHOLE] * len(flat) + [HBM] * len(after),
        out_specs=(WHOLE,) * len(outs),
        compiler_params=params(),
        name="split",
    )(chip, *flat, *after)
    return [(out[2 * k], out[2 * k + 1]) for k in range(len(jobs))]


def finish_kernel(v_ref, r_ref, *rest):
    rest[-1][...] = v_ref[0].astype(F32) + r_ref[0].astype(F32)


def finish(v, r, after=()):
    return pl.pallas_call(
        finish_kernel,
        out_shape=shape(v.shape[1:], F32),
        in_specs=[WHOLE] * 2 + [HBM] * len(after),
        out_specs=WHOLE,
        compiler_params=params(),
        name="finish",
    )(v, r, *after)


def pack_kernel(side_ref, a_ref, b_ref, c_ref, d_ref, lo_ref, hi_ref, pre_ref, *rest):
    out_ref = rest[-1]
    lanes = out_ref.shape[1]
    per = a_ref.shape[1] // lanes

    def row(at, ref, i, rounded=False):
        for k in range(ref.shape[1] // lanes):
            value = ref[i : i + 1, k * lanes : (k + 1) * lanes]
            out_ref[at + k : at + k + 1, :] = value.astype(BF).astype(F32) if rounded else value

    for k, (ref, i) in enumerate(((c_ref, 0), (c_ref, 1), (b_ref, 3), (a_ref, 1))):
        row(k * per, ref, i)
    many = pre_ref.shape[1] // lanes
    for s in range(2):

        @pl.when(side_ref[0] == s)
        def _():
            for i in range(2):
                row(4 * per + (s ^ i) * many, pre_ref, i)

    at = 4 * per + 2 * many
    for ref in (lo_ref, hi_ref):
        for k in range(ref.shape[1] // lanes):
            out_ref[at : at + HEADS, :] = ref[:, k * lanes : (k + 1) * lanes]
            at += HEADS
    out_ref[at:, :] = jnp.zeros((out_ref.shape[0] - at, lanes), F32)
    parts = ((d_ref, 0), (d_ref, 1), (b_ref, 2), (b_ref, 0), (b_ref, 1), (a_ref, 0))
    for k, (ref, i) in enumerate(parts):
        row(at + k * per, ref, i, True)


def pack(side, arrays, rows, after=()):
    return pl.pallas_call(
        pack_kernel,
        out_shape=shape((rows, 128), F32),
        in_specs=[SCALAR] + [WHOLE] * len(arrays) + [HBM] * len(after),
        out_specs=WHOLE,
        compiler_params=params(),
        name="pack",
    )(side, *arrays, *after)


def meet_kernel(bit, rows, chip_ref, v_ref, r_ref, *rest):
    out_ref = rest[-1]
    out_ref[0:SUM_ROWS, :] = v_ref[0:SUM_ROWS, :] + r_ref[0:SUM_ROWS, :]
    up = (chip_ref[0] & bit) // bit
    for i in range((v_ref.shape[0] - SUM_ROWS) // rows):
        src = slice(SUM_ROWS + i * rows, SUM_ROWS + (i + 1) * rows)
        for ref, side in ((v_ref, up), (r_ref, 1 - up)):
            at = pl.multiple_of(SUM_ROWS + (2 * i + side) * rows, 8)
            out_ref[pl.ds(at, rows), :] = ref[src, :]


def meet(chip, v, r, bit, rows, after=()):
    total = 2 * v.shape[0] - SUM_ROWS
    return pl.pallas_call(
        functools.partial(meet_kernel, bit, rows),
        out_shape=shape((total, v.shape[1]), F32),
        in_specs=[SCALAR, WHOLE, WHOLE] + [HBM] * len(after),
        out_specs=WHOLE,
        compiler_params=params(),
        name="meet",
    )(chip, v, r, *after)


class Reduction:
    def __init__(self, chip, parts, n):
        last, orders = orders_out(n)
        self.chip, self.n = chip, n
        self.orders = [part[::-1] for part in orders]
        self.tail = last[::-1]
        self.left = [all_bits(n)[::-1] for _ in range(3)]
        self.pairs = [
            (keep, self.exchange(k, self.orders[k].pop(0), send)) for k, (keep, send) in enumerate(parts)
        ]

    def exchange(self, k, bit, send):
        self.left[k] = [b for b in self.left[k] if b != bit]
        return swap(send, bit, self.n)

    def plan(self):
        chains = [[k] for k in range(len(self.pairs))]
        if len(self.pairs) > 1 and not self.orders[0]:
            chains = [list(range(len(self.pairs)))]
            self.orders = [list(self.tail)]
        bits = [self.orders[chain[0]].pop(0) for chain in chains]
        return [
            ([self.pairs[j] for j in chain], bit, list(self.left[chain[0]]))
            for chain, bit in zip(chains, bits)
        ]

    def parted(self):
        return len(self.pairs) > 1 and not self.orders[0]

    def take(self, other):
        self.pairs = other.pairs + self.pairs

    def go(self, jobs, outs):
        self.pairs = [
            (keep, self.exchange(k, bit, send))
            for k, ((_, bit, _), (keep, send)) in enumerate(zip(jobs, outs))
        ]

    def done(self):
        return len(self.pairs) == 1 and not self.orders[0]

    def result(self, *after):
        return finish(*self.pairs[0], after)


def step(sums, *after):
    plans = [s.plan() for s in sums]
    outs = split(sums[0].chip, [job for jobs in plans for job in jobs], after)
    kept = tuple(keep for keep, _ in outs)
    for s, jobs in zip(sums, plans):
        s.go(jobs, outs[: len(jobs)])
        outs = outs[len(jobs) :]
    return kept


def fc2_rows_kernel(side_ref, own_ref, other_ref, out_ref):
    rows = own_ref.shape[0]
    width = out_ref.shape[1]
    for s in range(2):

        @pl.when(side_ref[0] == s)
        def _():
            for half, ref in ((s, own_ref), (1 - s, other_ref)):
                for part in range(2):
                    lo = (2 * half + part) * rows
                    out_ref[lo : lo + rows, :] = ref[:, part * width : (part + 1) * width]


def fc2_rows(side, own, other):
    return pl.pallas_call(
        fc2_rows_kernel,
        out_shape=shape((4 * own.shape[0], own.shape[1] // 4), F32),
        in_specs=[SCALAR, WHOLE, WHOLE],
        out_specs=WHOLE,
        compiler_params=params(),
        name="fc2_rows",
    )(side, own, other)


def attn_rows_kernel(side_ref, own_ref, other_ref, qkv_ref, proj_ref):
    width = proj_ref.shape[1]
    for s in range(2):

        @pl.when(side_ref[0] == s)
        def _():
            low, high = (own_ref, other_ref) if s == 0 else (other_ref, own_ref)
            qkv_ref[:, 0 : 2 * width] = low[...]
            qkv_ref[:, 2 * width :] = high[:, 0:width]
            proj_ref[...] = high[:, width:]


def attn_rows(side, own, other):
    rows, width = own.shape[0], own.shape[1] // 2
    return pl.pallas_call(
        attn_rows_kernel,
        out_shape=(shape((rows, 3 * width), F32), shape((rows, width), F32)),
        in_specs=[SCALAR, WHOLE, WHOLE],
        out_specs=(WHOLE, WHOLE),
        compiler_params=params(),
        name="attn_rows",
    )(side, own, other)


def hold_kernel(*refs):
    pass


def hold(values, *after):
    many = isinstance(values, tuple)
    values = values if many else (values,)
    out = pl.pallas_call(
        hold_kernel,
        out_shape=tuple(shape(v.shape, v.dtype) for v in values),
        in_specs=[HBM] * (len(values) + len(after)),
        out_specs=(HBM,) * len(values),
        input_output_aliases={k: k for k in range(len(values))},
        name="hold",
    )(*values, *after)
    return out if many else out[0]


def attention_kernel(
    side_ref,
    own_ref,
    other_ref,
    normed_ref,
    bqv_ref,
    strip_ref,
    keep_ref,
    x_ref,
    mod_ref,
    bproj_ref,
    qh_ref,
    kh_ref,
    vh_ref,
    mine_ref,
    theirs_ref,
    attended_ref,
    middle_ref,
    normed_two_ref,
    w_out_ref,
    w_ref,
    flat_ref,
    mix_ref,
    sem,
):
    length, width = x_ref.shape
    hd = width // HEADS
    tile = 384
    wait = fetch_halves(side_ref, own_ref, other_ref, w_ref, sem)
    normed = normed_ref[...]

    def project(slot, lo, cols, at, bias_at):
        def body(o):
            y = mm(normed, w_ref[slot, :, pl.ds(lo + o, tile)])
            if bias_at is not None:
                y = y + bqv_ref[:, pl.ds(bias_at + o, tile)]
            flat_ref[:, pl.ds(at + o, tile)] = y.astype(BF)

        strips(cols, tile, body)

    wait(0)
    project(0, 0, width, 0, 0)
    project(0, width, width, width, None)
    wait(1)
    keep_out = pltpu.make_async_copy(w_ref.at[1, :, pl.ds(width, width)], w_out_ref, sem.at[2])
    keep_out.start()
    project(1, 0, width, 2 * width, width)
    for h in range(HEADS):
        qh_ref[h] = flat_ref[:, h * hd : (h + 1) * hd]
        kh_ref[h] = flat_ref[:, width + h * hd : width + (h + 1) * hd]
        vh_ref[h] = flat_ref[:, 2 * width + h * hd : 2 * width + (h + 1) * hd]
    keep = keep_ref[...] > 0.0

    def head(h, carry):
        sc = mm_nt(qh_ref[h], kh_ref[h]) * (hd**-0.5) + bias_of(strip_ref[h])
        sc = jnp.where(keep, sc, -1e30)
        ex = jnp.exp(sc - jnp.max(sc, axis=-1, keepdims=True))
        soft = ex / jnp.sum(ex, axis=-1, keepdims=True)
        mix_ref[h] = mm(soft.astype(BF), vh_ref[h]).astype(BF)
        return carry

    lax.fori_loop(0, HEADS, head, 0)
    for h in range(HEADS):
        flat_ref[:, h * hd : (h + 1) * hd] = mix_ref[h]
    mixed = flat_ref[:, 0:width]
    mine_ref[:, 0:width] = normed
    theirs_ref[:, 0:width] = normed
    for s, (normed_at, mixed_at) in enumerate(((mine_ref, theirs_ref), (theirs_ref, mine_ref))):

        @pl.when(side_ref[0] == s)
        def _():
            normed_at[:, width:] = normed
            mixed_at[:, width:] = mixed

    def out(o):
        y = mm(mixed, w_ref[1, :, pl.ds(width + o, tile)]) + bproj_ref[:, pl.ds(o, tile)]
        attended_ref[:, pl.ds(o, tile)] = y

    strips(width, tile, out)
    middle = x_ref[...] + mod_ref[2:3, :] * attended_ref[...]
    middle_ref[...] = middle
    n2, _ = normal(middle)
    normed_two_ref[...] = (n2 * (1.0 + mod_ref[4:5, :]) + mod_ref[3:4, :]).astype(BF)
    keep_out.wait()


def attention(side, own, other, normed, b_qv, bias, keep, x, mod, b_proj):
    length, width = x.shape
    hd = width // HEADS
    per_head = shape((HEADS, length, hd), BF)
    return pl.pallas_call(
        attention_kernel,
        out_shape=(
            per_head,
            per_head,
            per_head,
            shape((length, 2 * width), BF),
            shape((length, 2 * width), BF),
            shape((length, width), F32),
            shape((length, width), F32),
            shape((length, width), BF),
            shape((width, width), BF),
        ),
        in_specs=[SCALAR, HBM, HBM] + [WHOLE] * 7,
        out_specs=(WHOLE,) * 8 + (HBM,),
        scratch_shapes=[
            pltpu.VMEM((2, width, 2 * width), BF),
            pltpu.VMEM((length, 3 * width), BF),
            pltpu.VMEM((HEADS, length, hd), BF),
            pltpu.SemaphoreType.DMA((3,)),
        ],
        compiler_params=params(),
        cost_estimate=cost(8 * length * width * width + 4 * length * length * width, 24e6),
        name="attention",
    )(side, own, other, normed, b_qv, bias, keep, x, mod, b_proj)


def fc2_tiles(width, half, tile):
    part = tile // 2
    per = width // part
    at = lambda q: (q % per, half // width + q // per)
    return [pl.BlockSpec((part, width), lambda t, k=k: at(2 * t + k)) for k in range(2)]


def mlp_half(normed_two_ref, b_ref, c0_ref, c1_ref, bf1_ref, hid_ref, slope_ref):
    act, slope = gelu_parts(mm(normed_two_ref[...], b_ref[...]) + bf1_ref[...])
    hid = act.astype(BF)
    hid_ref[...] = hid
    slope_ref[...] = slope
    return mm(hid, jnp.concatenate([c0_ref[...], c1_ref[...]], axis=0))


def mlp_first_kernel(normed_two_ref, b_ref, c0_ref, c1_ref, bf1_ref, hid_ref, slope_ref, part_ref):
    total = mlp_half(normed_two_ref, b_ref, c0_ref, c1_ref, bf1_ref, hid_ref, slope_ref)

    @pl.when(pl.program_id(0) == 0)
    def _():
        part_ref[...] = total

    @pl.when(pl.program_id(0) > 0)
    def _():
        part_ref[...] += total


def mlp_last_kernel(
    normed_two_ref,
    b_ref,
    c0_ref,
    c1_ref,
    bf1_ref,
    part_ref,
    bf2_ref,
    middle_ref,
    cot_ref,
    mod_ref,
    place_ref,
    present_ref,
    hid_ref,
    slope_ref,
    g_branch_ref,
    out_ref,
    sums_ref,
    acc_ref,
):
    t = pl.program_id(0)
    total = mlp_half(normed_two_ref, b_ref, c0_ref, c1_ref, bf1_ref, hid_ref, slope_ref)

    @pl.when(t == 0)
    def _():
        acc_ref[...] = part_ref[...] + total

    @pl.when(t > 0)
    def _():
        acc_ref[...] += total

    @pl.when(t == pl.num_programs(0) - 1)
    def _():
        branch = acc_ref[...] + bf2_ref[...]
        cot = cot_ref[...]
        gate = mod_ref[5:6, :]
        result = middle_ref[...] + gate * branch
        out = jnp.where(present_ref[...] > 0.0, result, 0.0).astype(BF)
        out_ref[...] = mm_tn(place_ref[...], out).astype(BF)
        g_branch = (cot * gate).astype(BF)
        g_branch_ref[...] = g_branch
        sums_ref[0:1, :] = jnp.sum(cot * branch, axis=0, keepdims=True)
        sums_ref[1:2, :] = jnp.sum(g_branch.astype(F32), axis=0, keepdims=True)


def mlp(normed_two, weights, bf1, last=None):
    length, width = normed_two.shape
    half = weights.shape[1] // 2
    tile = 2 * width // 3
    fixed = lambda a: pl.BlockSpec(a.shape, lambda t: (0, 0))
    cols = lambda r: pl.BlockSpec((r, tile), lambda t: (0, t))
    rows = fc2_tiles(width, half, tile)
    whole = lambda r: pl.BlockSpec((r, width), lambda t: (0, 0))
    more = last or ()
    outs = [shape((length, half), BF), shape((length, half), F32)]
    if last:
        outs += [shape((length, width), BF), shape((length, width), BF), shape((8, width), F32)]
    else:
        outs += [shape((length, width), F32)]
    return pl.pallas_call(
        mlp_last_kernel if last else mlp_first_kernel,
        grid=(half // tile,),
        out_shape=tuple(outs),
        in_specs=[fixed(normed_two), cols(width)] + rows + [cols(1)] + [fixed(a) for a in more],
        out_specs=tuple([cols(length), cols(length)] + [whole(o.shape[0]) for o in outs[2:]]),
        scratch_shapes=[pltpu.VMEM((length, width), F32)] if last else [],
        compiler_params=params(),
        cost_estimate=cost(4 * length * width * half, 16e6),
        name="mlp",
    )(normed_two, weights, weights, weights, bf1, *more)


def mlp_back_kernel(
    g_branch_ref,
    b0_ref,
    b1_ref,
    c00_ref,
    c01_ref,
    c10_ref,
    c11_ref,
    slope0_ref,
    slope1_ref,
    middle_ref,
    attended_ref,
    cot_ref,
    mod_ref,
    w_out_ref,
    *rest,
):
    pre0_ref, pre1_ref, bsum_ref, g_middle_ref, g_att_ref, g_mixed_ref, sums_ref, acc_ref = rest[-8:]
    t = pl.program_id(0)
    g_branch = g_branch_ref[...]
    total = None
    for i, (b_ref, c_refs, slope_ref, pre_ref) in enumerate(
        (
            (b0_ref, (c00_ref, c01_ref), slope0_ref, pre0_ref),
            (b1_ref, (c10_ref, c11_ref), slope1_ref, pre1_ref),
        )
    ):
        c = jnp.concatenate([ref[...] for ref in c_refs], axis=0)
        pre = (mm_nt(g_branch, c) * slope_ref[...]).astype(BF)
        pre_ref[...] = pre
        bsum_ref[i : i + 1, :] = jnp.sum(pre.astype(F32), axis=0, keepdims=True)
        part = mm_nt(pre, b_ref[...])
        total = part if total is None else total + part

    @pl.when(t == 0)
    def _():
        acc_ref[...] = total

    @pl.when(t > 0)
    def _():
        acc_ref[...] += total

    @pl.when(t == pl.num_programs(0) - 1)
    def _():
        g_n2 = acc_ref[...]
        n2, inv2 = normal(middle_ref[...])
        sums_ref[0:1, :] = jnp.sum(g_n2, axis=0, keepdims=True)
        sums_ref[1:2, :] = jnp.sum(g_n2 * n2, axis=0, keepdims=True)
        g_middle = cot_ref[...] + normal_back(g_n2 * (1.0 + mod_ref[4:5, :]), n2, inv2)
        g_middle_ref[...] = g_middle
        sums_ref[2:3, :] = jnp.sum(g_middle * attended_ref[...], axis=0, keepdims=True)
        g_att = (g_middle * mod_ref[2:3, :]).astype(BF)
        g_att_ref[...] = g_att
        sums_ref[3:4, :] = jnp.sum(g_att.astype(F32), axis=0, keepdims=True)
        g_mixed_ref[...] = mm_nt(g_att, w_out_ref[...]).astype(BF)


def mlp_back(g_branch, weights, slope0, slope1, middle, attended, cot, mod, w_out, after=()):
    length, width = middle.shape
    half = weights[0].shape[1] // 2
    tile = 2 * width // 3
    fixed = lambda a: pl.BlockSpec(a.shape, lambda t: (0, 0))
    cols = lambda r: pl.BlockSpec((r, tile), lambda t: (0, t))
    rows = fc2_tiles(width, half, tile)
    whole = lambda r: pl.BlockSpec((r, width), lambda t: (0, 0))
    return pl.pallas_call(
        mlp_back_kernel,
        grid=(half // tile,),
        out_shape=(
            shape((length, half), BF),
            shape((length, half), BF),
            shape((2, half), F32),
            shape((length, width), F32),
            shape((length, width), BF),
            shape((length, width), BF),
            shape((8, width), F32),
        ),
        in_specs=[
            fixed(g_branch),
            cols(width),
            cols(width),
            *rows,
            *rows,
            cols(length),
            cols(length),
            fixed(middle),
            fixed(attended),
            fixed(cot),
            fixed(mod),
            fixed(w_out),
        ]
        + [HBM] * len(after),
        out_specs=(
            cols(length),
            cols(length),
            cols(2),
            whole(length),
            whole(length),
            whole(length),
            whole(8),
        ),
        scratch_shapes=[pltpu.VMEM((length, width), F32)],
        compiler_params=params(),
        cost_estimate=cost(8 * length * width * half, 32e6),
        name="mlp_back",
    )(
        g_branch,
        *weights,
        weights[0],
        weights[0],
        weights[1],
        weights[1],
        slope0,
        slope1,
        middle,
        attended,
        cot,
        mod,
        w_out,
        *after,
    )


def heads_back(q_ref, k_ref, v_ref, strip_ref, keep, gm_ref, dq_ref, dk_ref, dv_ref, sums_ref, start):
    scale = q_ref.shape[2] ** -0.5
    length = q_ref.shape[1]

    def head(i, carry):
        h = start + i
        q, k, v, gm = q_ref[h], k_ref[h], v_ref[h], gm_ref[i]
        sc = mm_nt(q, k) * scale + bias_of(strip_ref[h])
        sc = jnp.where(keep, sc, -1e30)
        ex = jnp.exp(sc - jnp.max(sc, axis=-1, keepdims=True))
        soft = ex / jnp.sum(ex, axis=-1, keepdims=True)
        dv_ref[i] = mm_tn(soft.astype(BF), gm).astype(BF)
        dp = mm_nt(gm, v)
        ds = (soft * (dp - jnp.sum(dp * soft, axis=-1, keepdims=True))).astype(BF)
        dq_ref[i] = (mm(ds, k) * scale).astype(BF)
        dk_ref[i] = (mm_tn(ds, q) * scale).astype(BF)
        dsf = ds.astype(F32)
        total = jnp.zeros((GRID, sums_ref.shape[2]), F32)
        blank = jnp.zeros((GRID, sums_ref.shape[2] - length), F32)
        for y in range(GRID):
            rows = jnp.concatenate([dsf[y * GRID : (y + 1) * GRID, :], blank], axis=1)
            by = (GRID - 1 - y) * GRID
            total = total + (pltpu.roll(rows, by, 1) if by else rows)
        sums_ref[i] = total
        return carry

    lax.fori_loop(0, dq_ref.shape[0], head, 0, unroll=2)


def first_heads_kernel(qh_ref, kh_ref, vh_ref, strip_ref, keep_ref, g_mixed_ref, *rest):
    dq_ref, dk_ref, dv_ref, sums_ref, gm_ref = rest[-5:]
    hd = qh_ref.shape[2]
    for i in range(HEADS // 2):
        gm_ref[i] = g_mixed_ref[:, i * hd : (i + 1) * hd]
    heads_back(
        qh_ref, kh_ref, vh_ref, strip_ref, keep_ref[...] > 0.0, gm_ref, dq_ref, dk_ref, dv_ref, sums_ref, 0
    )


def first_heads(qh, kh, vh, strip, keep, g_mixed, after=()):
    heads, length, hd = qh.shape
    some = shape((heads // 2, length, hd), BF)
    return pl.pallas_call(
        first_heads_kernel,
        out_shape=(some, some, some, shape((heads // 2,) + strip.shape[1:], F32)),
        in_specs=[WHOLE] * 6 + [HBM] * len(after),
        out_specs=(WHOLE,) * 4,
        scratch_shapes=[pltpu.VMEM((heads // 2, length, hd), BF)],
        compiler_params=params(),
        cost_estimate=cost(5 * length * length * heads * hd, 16e6),
        name="first_heads",
    )(qh, kh, vh, strip, keep, g_mixed, *after)


def last_heads_kernel(
    side_ref,
    qh_ref,
    kh_ref,
    vh_ref,
    strip_ref,
    keep_ref,
    g_mixed_ref,
    g_att_ref,
    fq_ref,
    fk_ref,
    fv_ref,
    fsum_ref,
    *rest,
):
    mine_ref, top_ref, low_ref, lo_ref, hi_ref, sums_ref, both_ref, gm_ref, dq_ref, dk_ref, dv_ref, strips_ref = rest[-12:]
    theirs_ref = both_ref
    width = g_mixed_ref.shape[1]
    hd = qh_ref.shape[2]
    half = HEADS // 2
    for i in range(half):
        gm_ref[i] = g_mixed_ref[:, (half + i) * hd : (half + i + 1) * hd]
    heads_back(
        qh_ref, kh_ref, vh_ref, strip_ref, keep_ref[...] > 0.0, gm_ref, dq_ref, dk_ref, dv_ref, strips_ref, half
    )
    for s, (qk_at, v_at) in enumerate(((mine_ref, theirs_ref), (theirs_ref, mine_ref))):

        @pl.when(side_ref[0] == s)
        def _():
            for h in range(HEADS):
                q, k, v = (fq_ref, fk_ref, fv_ref) if h < half else (dq_ref, dk_ref, dv_ref)
                i = h % half
                qk_at[:, h * hd : (h + 1) * hd] = q[i]
                qk_at[:, width + h * hd : width + (h + 1) * hd] = k[i]
                v_at[:, h * hd : (h + 1) * hd] = v[i]
            v_at[:, width:] = g_att_ref[...]
            sums_ref[0:1, :] = jnp.sum(qk_at[:, 0:width].astype(F32), axis=0, keepdims=True)
            sums_ref[1:2, :] = jnp.sum(v_at[:, 0:width].astype(F32), axis=0, keepdims=True)

    length = both_ref.shape[0]
    top_ref[...] = both_ref[0 : length // 2, :]
    low_ref[...] = both_ref[length // 2 :, :]
    lanes = lo_ref.shape[1]
    for part, ref in enumerate((fsum_ref, strips_ref)):
        lo = jnp.zeros((half, lanes), F32)
        hi = jnp.zeros((half, lanes), F32)
        j = lax.broadcasted_iota(jnp.int32, lo.shape, 1) % GRID
        for i in range(GRID):
            k = GRID - 1 - i
            row = ref[:, i, :]
            a = jnp.where(j < GRID - k, row, 0.0)
            lo = lo + (pltpu.roll(a, k, 1) if k else a)
            if k:
                hi = hi + pltpu.roll(jnp.where(j < GRID - k, 0.0, row), lanes - (GRID - k), 1)
        lo_ref[part * half : (part + 1) * half, :] = lo
        hi_ref[part * half : (part + 1) * half, :] = hi


def last_heads(side, qh, kh, vh, strip, keep, g_mixed, g_att, firsts, after=()):
    length, width = g_mixed.shape
    heads, _, hd = qh.shape
    per_head = pltpu.VMEM((heads // 2, length, hd), BF)
    window = shape((heads, strip.shape[2]), F32)
    return pl.pallas_call(
        last_heads_kernel,
        out_shape=(
            shape((length, 2 * width), BF),
            shape((length // 2, 2 * width), BF),
            shape((length // 2, 2 * width), BF),
            window,
            window,
            shape((8, width), F32),
        ),
        in_specs=[SCALAR] + [WHOLE] * 11 + [HBM] * len(after),
        out_specs=(WHOLE,) * 6,
        scratch_shapes=[pltpu.VMEM((length, 2 * width), BF)]
        + [per_head] * 4 + [pltpu.VMEM((heads // 2,) + strip.shape[1:], F32)],
        compiler_params=params(),
        cost_estimate=cost(5 * length * length * width, 16e6),
        name="last_heads",
    )(side, qh, kh, vh, strip, keep, g_mixed, g_att, *firsts, *after)


def tokens_back_kernel(
    side_ref,
    own_ref,
    other_ref,
    mine_ref,
    top_ref,
    low_ref,
    x_ref,
    g_middle_ref,
    mod_ref,
    place_ref,
    *rest,
):
    out_ref, sums_ref, w_ref, acc_ref, qk_ref, v_ref, sem = rest[-7:]
    length, width = x_ref.shape
    wait = fetch_halves(side_ref, own_ref, other_ref, w_ref, sem)
    half = length // 2

    @pl.when(side_ref[0] == 0)
    def _():
        qk_ref[...] = mine_ref[...]
        v_ref[0:half, :] = top_ref[:, 0:width]
        v_ref[half:, :] = low_ref[:, 0:width]

    @pl.when(side_ref[0] == 1)
    def _():
        qk_ref[0:half, :] = top_ref[...]
        qk_ref[half:, :] = low_ref[...]
        v_ref[...] = mine_ref[:, 0:width]

    wait(0)
    acc_ref[...] = mm_nt(qk_ref[...], w_ref[0])
    wait(1)
    g_n1 = acc_ref[...] + mm_nt(v_ref[...], w_ref[1, :, 0:width])
    n1, inv1 = normal(x_ref[...])
    sums_ref[0:1, :] = jnp.sum(g_n1, axis=0, keepdims=True)
    sums_ref[1:2, :] = jnp.sum(g_n1 * n1, axis=0, keepdims=True)
    g_x = g_middle_ref[...] + normal_back(g_n1 * (1.0 + mod_ref[1:2, :]), n1, inv1)
    out_ref[...] = mm_tn(place_ref[...], g_x.astype(BF)).astype(BF)


def tokens_back(side, own, other, mine, theirs, x, g_middle, mod, place, after=()):
    length, width = x.shape
    return pl.pallas_call(
        tokens_back_kernel,
        out_shape=(shape((length, width), BF), shape((8, width), F32)),
        in_specs=[SCALAR, HBM, HBM] + [WHOLE] * 7 + [HBM] * len(after),
        out_specs=(WHOLE,) * 2,
        scratch_shapes=[
            pltpu.VMEM((2, width, 2 * width), BF),
            pltpu.VMEM((length, width), F32),
            pltpu.VMEM((length, 2 * width), BF),
            pltpu.VMEM((length, width), BF),
            pltpu.SemaphoreType.DMA((2,)),
        ],
        compiler_params=params(),
        cost_estimate=cost(6 * length * width * width, 16e6),
        name="tokens_back",
    )(side, own, other, mine, *theirs, x, g_middle, mod, place, *after)


def local(
    n,
    tokens,
    condition,
    kept_index,
    kept_count,
    cotangent,
    w_ada,
    w_qkv,
    w_proj,
    w_fc1,
    w_fc2,
    b_ada,
    b_qv,
    b_proj,
    b_fc1,
    b_fc2,
    rel_table,
):
    side = lax.axis_index("stream")
    chip = lax.axis_index("dp")
    length, width = tokens.shape[2], tokens.shape[3]
    ff = w_fc1.shape[1]
    rows = width // n
    cut = ff // (2 * n)
    first = side == 0
    side_word = side.astype(jnp.int32).reshape(1)
    chip_word = chip.astype(jnp.int32).reshape(1)

    order_first, order_parts = orders_out(n)
    firsts = tuple(part[-1] for part in order_parts)

    ordinal = jnp.arange(length, dtype=jnp.int32)
    count = jnp.where(first, length, kept_count[0])
    position = jnp.where(first, ordinal, kept_index[0])
    place = ((position[None, :] == ordinal[:, None]) & (ordinal[None, :] < count)).astype(BF)
    present = jnp.sum(place.astype(F32), axis=1)
    keep = present.reshape(1, length)
    present = present.reshape(length, 1)
    x = mm(place, tokens[0, 0])
    cot = mm(place, cotangent[0, 0])
    bias = bias_strip(rel_table)

    cond = condition[0, 0]
    sig = jax.nn.sigmoid(cond)
    cond_act = (cond * sig).astype(BF)
    shard_a = attn_shard(side_word, w_qkv, w_proj)
    all_a = Gathering(chip_word, shard_a, n)
    acts = trade(hold(jnp.broadcast_to(cond_act[None], (n, width)), shard_a))
    acts_part = lax.dynamic_slice_in_dim(acts, chip * rows, rows, axis=1)
    shard_bc = mlp_shard(n, side_word, w_fc1, w_fc2, after=(shard_a,))
    last = all_a.step(shard_bc, bias, x, cot, acts_part)
    all_bc = Gathering(chip_word, hold(shard_bc, *last), n)
    for _ in range(len(order_parts[0]) - 2 + len(order_first) - 1):
        last = all_a.step(*last)
    while all_bc.turn < all_bc.cut_at:
        last = all_bc.step(*last)
    acts_twin = swap_stream(acts_part)
    if {p[-1] for p in order_parts} == {p[0] for p in order_parts}:
        last, result_a, on_bc = merge_steps(all_a, all_bc, acts_twin)
        last = on_bc()
    else:
        last = all_a.step(*last, acts_twin)
        result_a = all_a.result
        last = all_bc.step(*last)
    a_own = result_a(*last)
    a_other = swap_stream(a_own)
    mod_part = trade(hold(mm(acts_part, w_ada), a_own))
    last = (mod_part,)
    while not all_bc.done():
        last = all_bc.step(*last)
    modulation = jnp.sum(mod_part, axis=0) + b_ada
    mod = modulation.reshape(6, width)
    n1, _ = normal(x)
    normed = (n1 * (1.0 + mod[1]) + mod[0]).astype(BF)
    qh, kh, vh, lhs_mine, lhs_theirs, attended, middle, normed_two, w_out = attention(
        side_word,
        a_own,
        a_other,
        normed,
        b_qv.reshape(1, -1),
        bias,
        keep,
        x,
        mod,
        b_proj.reshape(1, -1),
    )

    bf1 = jnp.transpose(b_fc1.reshape(n, 2, 2, cut // 2), (1, 2, 0, 3)).reshape(2, 1, ff // 2)
    bf1_own, bf1_other = jnp.where(first, bf1[0], bf1[1]), jnp.where(first, bf1[1], bf1[0])
    bf2 = b_fc2.reshape(1, -1)
    bc_own = all_bc.result(normed_two, bf1_own, bf1_other, bf2, present, place)
    bc_other = swap_stream(bc_own)
    lhs_twin = swap_stream(lhs_theirs)
    n2_twin = swap_stream(normed_two)
    hid0, slope0, part = mlp(normed_two, bc_own, bf1_own)
    hid1, slope1, g_branch, out_tokens, sums_a = mlp(
        normed_two,
        bc_other,
        bf1_other,
        (part, bf2, middle, cot, mod, place, present),
    )

    parts_c = product(
        chip_word, hid0, swap_stream(hid1), g_branch, swap_stream(g_branch), width, n, firsts
    )
    sum_c = Reduction(chip_word, parts_c, n)
    pre0, pre1, pre_sum, g_middle, g_att, g_mixed, sums_b = mlp_back(
        g_branch,
        (bc_own, bc_other),
        slope0,
        slope1,
        middle,
        attended,
        cot,
        mod,
        w_out,
        after=(parts_c[0][0], lhs_twin, n2_twin),
    )
    kept = step([sum_c], g_mixed)
    pre_twin = swap_stream(pre1)
    one = first_heads(qh, kh, vh, bias, keep, g_mixed, after=kept + (pre_twin,))
    kept = step([sum_c], one[0])
    while not sum_c.parted():
        kept = step([sum_c], *kept)
    parts_b = product(chip_word, normed_two, n2_twin, pre0, pre_twin, width, n, firsts, after=kept)
    sum_b = Reduction(chip_word, parts_b, n)
    g_mine, top, low, lo, hi, sums_c = last_heads(
        side_word, qh, kh, vh, bias, keep, g_mixed, g_att, one, after=(parts_b[0][0],)
    )
    g_theirs = (top, low)
    g_twin = (swap_stream(top), swap_stream(low))
    kept = step([sum_b], g_mine) + g_twin
    grad_tokens, sums_d = tokens_back(
        side_word, a_own, a_other, g_mine, g_theirs, x, g_middle, mod, place, after=kept
    )

    kept = (sums_d,)
    while not sum_b.parted():
        kept = step([sum_b], *kept)
    mod_rows = 6 * width // 128
    group = -(-mod_rows // 8) * 8
    told = pack(
        side_word, (sums_a, sums_b, sums_c, sums_d, lo, hi, pre_sum), SUM_ROWS + group, after=kept
    )
    bits = all_bits(n)[::-1]
    came = swap(told, bits[0], n)
    sum_b.take(sum_c)
    kept = (told,)
    while not sum_b.done():
        kept = step([sum_b], *kept)
    told = meet(chip_word, told, came, bits[0], group, after=kept)
    told = meet(chip_word, told, swap(told, bits[1], n), bits[1], group)
    came = swap(told, bits[2], n)
    parts_a = product(
        chip_word, lhs_mine, lhs_twin, g_mine, g_twin, width, n, firsts, after=(told,) + kept
    )
    told = meet(chip_word, told, came, bits[2], group, after=(parts_a[0][0],))
    sum_a = Reduction(chip_word, parts_a, n)
    for b in bits[3:]:
        told = meet(chip_word, told, swap(told, b, n), b, group)
    d_cb = sum_b.result()
    kept = step([sum_a], told, d_cb)
    d_cb_twin = swap_stream(d_cb)
    grad_w_fc2 = fc2_rows(side_word, d_cb, d_cb_twin)
    grad_w_fc1 = fc1_rows(n, side_word, d_cb, d_cb_twin)
    kept = step([sum_a], told, grad_w_fc2)
    twin = swap_stream(told)

    def mods_of(t):
        return t[SUM_ROWS:].reshape(n, -1, 128)[:, :mod_rows].reshape(n, -1)

    g_own, g_twin = mods_of(told), mods_of(twin)
    grad_w_ada = mm_tn(acts_part, g_own.astype(BF)) + mm_tn(acts_twin, g_twin.astype(BF))
    grad_b_ada = jnp.sum(g_own, axis=0) + jnp.sum(g_twin, axis=0)
    kept = step([sum_a], *kept, grad_w_ada, grad_b_ada)
    while not sum_a.done():
        kept = step([sum_a], *kept)
    g_acts = trade(hold(mm_nt(g_own.astype(BF), w_ada), *kept)).reshape(width)
    grad_condition = g_acts * sig * (1.0 + cond * (1.0 - sig))
    sums = told[:SUM_ROWS] + twin[:SUM_ROWS]
    per = width // 128
    at = 4 * per + ff // 128
    grad_b_fc1 = jnp.transpose(sums[4 * per : at].reshape(2, 2, n, cut // 2), (2, 0, 1, 3)).reshape(-1)
    windows = jnp.transpose(sums[at:].reshape(2, -1, HEADS, 128), (0, 2, 1, 3)).reshape(2, HEADS, -1)
    parts = (
        sums[: 2 * per].reshape(-1),
        sums[2 * per : 3 * per].reshape(-1),
        grad_b_fc1,
        sums[3 * per : 4 * per].reshape(-1),
        table_of(windows[0], windows[1]),
    )
    d_a = sum_a.result(g_acts, grad_w_fc1, *parts)
    grad_w_qkv, grad_w_proj = attn_rows(side_word, d_a, swap_stream(d_a))
    return (
        out_tokens[None, None],
        grad_tokens[None, None],
        grad_condition[None, None],
        grad_w_ada,
        grad_w_qkv,
        grad_w_proj,
        grad_w_fc1,
        grad_w_fc2,
        grad_b_ada,
        *parts,
    )


def solution(mesh):
    n = mesh.shape["dp"]

    def body(*args):
        return local(n, *args)

    return jax.shard_map(
        body,
        mesh=mesh,
        in_specs=(
            P("stream", "dp", None, None),
            P("stream", "dp", None),
            P("dp", None),
            P("dp"),
            P("stream", "dp", None, None),
            P("dp", None),
            P("dp", None),
            P("dp", None),
            P("dp", None),
            P("dp", None),
            P(),
            P(),
            P(),
            P(),
            P(),
            P(),
        ),
        out_specs=(
            P("stream", "dp", None, None),
            P("stream", "dp", None, None),
            P("stream", "dp", None),
            P("dp", None),
            P("dp", None),
            P("dp", None),
            P("dp", None),
            P("dp", None),
            P(),
            P(),
            P(),
            P(),
            P(),
            P(),
        ),
        check_vma=False,
    )
```

```python
import functools
import math

import jax
import jax.numpy as jnp
from jax import lax
from jax.experimental import pallas as pl
from jax.experimental.pallas import tpu as pltpu
from jax.sharding import PartitionSpec as P

HEADS = 16
GRID = 16
BF = jnp.bfloat16
F32 = jnp.float32


def swap(v, bit, n):
    return lax.ppermute(v, "dp", [(i, i ^ bit) for i in range(n)])


def swap_stream(v):
    return lax.ppermute(v, "stream", [(0, 1), (1, 0)])


def axis_bits(n):
    k = n.bit_length() - 1
    s = k // 3
    xs = [1 << i for i in range(s)]
    ys = [1 << (s + i) for i in range(s)]
    zs = [1 << i for i in range(2 * s, k)]
    return xs, ys, zs


def all_bits(n):
    return [1 << i for i in range(n.bit_length() - 1)]


def orders_out(n):
    xs, ys, zs = axis_bits(n)
    near = zs[:1]
    return zs[1:][::-1], (near + ys + xs, xs + near + ys, ys + xs + near)


def trade(v):
    return lax.all_to_all(v, "dp", 0, 0, tiled=True)


def mm(a, b):
    return lax.dot_general(a, b, (((1,), (0,)), ((), ())), preferred_element_type=F32)


def mm_nt(a, b):
    return lax.dot_general(a, b, (((1,), (1,)), ((), ())), preferred_element_type=F32)


def mm_tn(a, b):
    return lax.dot_general(a, b, (((0,), (0,)), ((), ())), preferred_element_type=F32)


def normal(v):
    center = v - jnp.mean(v, axis=-1, keepdims=True)
    inv = lax.rsqrt(jnp.mean(center * center, axis=-1, keepdims=True) + 1e-06)
    return center * inv, inv


def normal_back(g, n, inv):
    return inv * (g - jnp.mean(g, axis=-1, keepdims=True) - n * jnp.mean(g * n, axis=-1, keepdims=True))


def bias_windows(table):
    w = 2 * GRID - 1
    t = jnp.transpose(table.reshape(w, w, HEADS)[::-1, ::-1], (2, 0, 1))
    t = jnp.pad(t, ((0, 0), (0, 1), (0, 1))).reshape(HEADS, w + 1, 2, GRID)
    return t[:, :, 0].reshape(HEADS, -1), t[:, :, 1].reshape(HEADS, -1)


def table_of(lo, hi):
    w = 2 * GRID - 1
    t = jnp.stack([lo.reshape(HEADS, w + 1, GRID), hi.reshape(HEADS, w + 1, GRID)], axis=2)
    t = t.reshape(HEADS, w + 1, 2 * GRID)[:, :w, :w]
    return jnp.transpose(t, (1, 2, 0))[::-1, ::-1].reshape(w * w, HEADS)


def gelu_parts(x):
    k = math.sqrt(2.0 / math.pi)
    th = jnp.tanh(k * (x + 0.044715 * x * x * x))
    value = 0.5 * x * (1.0 + th)
    slope = 0.5 * (1.0 + th) + 0.5 * x * (1.0 - th * th) * k * (1.0 + 3 * 0.044715 * x * x)
    return value, slope


VMEM_BYTES = 56 * 1024 * 1024
SUM_ROWS = 200
WHOLE = pl.BlockSpec(memory_space=pltpu.VMEM)
HBM = pl.BlockSpec(memory_space=pl.ANY)
SCALAR = pl.BlockSpec(memory_space=pltpu.SMEM)


def shape(dims, dtype):
    return jax.ShapeDtypeStruct(dims, dtype)


def params():
    return pltpu.CompilerParams(vmem_limit_bytes=VMEM_BYTES)


def cost(flops, size):
    return pl.CostEstimate(flops=int(flops), bytes_accessed=int(size), transcendentals=0)


def strips(total, tile, body):
    def step(i, carry):
        body(pl.multiple_of(i * tile, tile))
        return carry

    lax.fori_loop(0, total // tile, step, 0)


def fetch_halves(side_ref, own_ref, other_ref, w_ref, sem):
    side = side_ref[0]
    mine = pltpu.make_async_copy(own_ref, w_ref.at[side], sem.at[side])
    twin = pltpu.make_async_copy(other_ref, w_ref.at[1 - side], sem.at[1 - side])
    mine.start()
    twin.start()

    def wait(slot):
        pltpu.make_async_copy(own_ref, w_ref.at[slot], sem.at[slot]).wait()

    return wait


def pieces(n, rows, cut, s):
    half = cut // 2
    for part in range(2):
        for k in range(n):
            yield (k * 2 + s) * cut + part * half, (part * n + k) * half, half


def fc1_rows_kernel(n, side_ref, own_ref, other_ref, out_ref):
    rows, ff = out_ref.shape
    cut = ff // (2 * n)
    for s in range(2):

        @pl.when(side_ref[0] == s)
        def _():
            for half, ref in ((s, own_ref), (1 - s, other_ref)):
                for src, dst, w in pieces(n, rows, cut, half):
                    out_ref[:, src : src + w] = ref[:, ff // 2 + dst : ff // 2 + dst + w]


def fc1_rows(n, side, own, other):
    return pl.pallas_call(
        functools.partial(fc1_rows_kernel, n),
        out_shape=shape(own.shape, F32),
        in_specs=[SCALAR, WHOLE, WHOLE],
        out_specs=WHOLE,
        compiler_params=params(),
        name="fc1_rows",
    )(side, own, other)


def strip_kernel(lo_ref, hi_ref, out_ref):
    lanes = lo_ref.shape[1]
    lo, hi = lo_ref[...], hi_ref[...]
    j = lax.broadcasted_iota(jnp.int32, lo.shape, 1) % GRID
    for i in range(GRID):
        k = GRID - 1 - i
        a = pltpu.roll(lo, lanes - k, 1) if k else lo
        out_ref[:, i, :] = jnp.where(j < GRID - k, a, pltpu.roll(hi, GRID - k, 1))


def bias_strip(table):
    lo, hi = bias_windows(table)
    return pl.pallas_call(
        strip_kernel,
        out_shape=shape((HEADS, GRID, lo.shape[1]), F32),
        in_specs=[WHOLE, WHOLE],
        out_specs=WHOLE,
        name="bias_strip",
    )(lo, hi)


def bias_of(strip):
    return jnp.concatenate(
        [strip[:, (GRID - 1 - y) * GRID : (2 * GRID - 1 - y) * GRID] for y in range(GRID)], axis=0
    )


def put(i, pos):
    return (i >> pos) << (pos + 1) | (i & ((1 << pos) - 1))


def attn_shard_kernel(side_ref, qkv_ref, proj_ref, out_ref):
    width = proj_ref.shape[1]
    for s in range(2):

        @pl.when(side_ref[0] == s)
        def _():
            if s == 0:
                out_ref[0] = qkv_ref[:, 0 : 2 * width]
            else:
                out_ref[0, :, 0:width] = qkv_ref[:, 2 * width :]
                out_ref[0, :, width:] = proj_ref[...]


def mlp_shard_kernel(n, side_ref, f1_ref, f2_ref, *rest):
    out_ref = rest[-1]
    rows, ff = f1_ref.shape
    width = f2_ref.shape[1]
    cut = ff // (2 * n)
    for s in range(2):

        @pl.when(side_ref[0] == s)
        def _():
            for src, dst, w in pieces(n, rows, cut, s):
                out_ref[0, :, dst : dst + w] = f1_ref[:, src : src + w]
            for part in range(2):
                lo = s * cut + part * rows
                cols = slice(ff // 2 + part * width, ff // 2 + (part + 1) * width)
                out_ref[0, :, cols] = f2_ref[lo : lo + rows, :]


def mlp_shard(n, side, f1, f2, after=()):
    return pl.pallas_call(
        functools.partial(mlp_shard_kernel, n),
        out_shape=shape((1,) + f1.shape, BF),
        in_specs=[SCALAR, WHOLE, WHOLE] + [HBM] * len(after),
        out_specs=WHOLE,
        compiler_params=params(),
        name="mlp_shard",
    )(side, f1, f2, *after)


def attn_shard(side, w_qkv, w_proj):
    rows, width = w_proj.shape
    return pl.pallas_call(
        attn_shard_kernel,
        out_shape=shape((1, rows, 2 * width), BF),
        in_specs=[SCALAR, WHOLE, WHOLE],
        out_specs=WHOLE,
        compiler_params=params(),
        name="attn_shard",
    )(side, w_qkv, w_proj)


def join_kernel(jobs, chip_ref, *refs):
    outs = refs[-sum(len(cols) for _, cols in jobs) :]
    at = 0
    for k, (bit, cols) in enumerate(jobs):
        v_ref, r_ref = refs[2 * k], refs[2 * k + 1]
        m = v_ref.shape[0]
        up = (chip_ref[0] & bit) // bit
        lo = 0
        for c in cols:
            for i in range(m):
                outs[at][up * m + i] = v_ref[i, :, lo : lo + c]
                outs[at][(1 - up) * m + i] = r_ref[i, :, lo : lo + c]
            lo += c
            at += 1


def join(chip, jobs, after=()):
    flat = [t for v, r, _, _ in jobs for t in (v, r)]
    return pl.pallas_call(
        functools.partial(join_kernel, [(bit, cols) for _, _, bit, cols in jobs]),
        out_shape=tuple(
            shape((2 * v.shape[0], v.shape[1], c), v.dtype) for v, _, _, cols in jobs for c in cols
        ),
        in_specs=[SCALAR] + [WHOLE] * len(flat) + [HBM] * len(after),
        out_specs=(WHOLE,) * sum(len(cols) for _, _, _, cols in jobs),
        compiler_params=params(),
        name="join",
    )(chip, *flat, *after)


def assemble_kernel(orders, chip_ref, *refs):
    out_ref = refs[-1]
    lo = 0
    m = out_ref.shape[0] // 2
    for k, bits in enumerate(orders):
        v_ref, r_ref = refs[2 * k], refs[2 * k + 1]
        c = v_ref.shape[2]
        last = bits[-1]
        up = (chip_ref[0] & last) // last
        lead = bits[:-1][::-1]
        for i in range(m):
            base = sum(b for j, b in enumerate(lead) if (i >> (len(lead) - 1 - j)) & 1)
            out_ref[base + up * last, :, lo : lo + c] = v_ref[i]
            out_ref[base + (1 - up) * last, :, lo : lo + c] = r_ref[i]
        lo += c


def assemble(chip, orders, pairs, after=()):
    flat = [t for pair in pairs for t in pair]
    m, rows = 1 << (len(orders[0]) - 1), flat[0].shape[1]
    cols = sum(v.shape[2] for v, _ in pairs)
    out = pl.pallas_call(
        functools.partial(assemble_kernel, orders),
        out_shape=shape((2 * m, rows, cols), BF),
        in_specs=[SCALAR] + [WHOLE] * len(flat) + [HBM] * len(after),
        out_specs=WHOLE,
        compiler_params=params(),
        name="assemble",
    )(chip, *flat, *after)
    return out.reshape(2 * m * rows, cols)


class Gathering:
    def __init__(self, chip, v, n):
        first, parts = orders_out(n)
        self.chip, self.n = chip, n
        self.orders = [first + part for part in parts]
        self.turn, self.cut_at = 0, len(first)
        self.parts = [v]
        self.exchange()

    def exchange(self):
        self.came = [swap(v, self.orders[k][self.turn], self.n) for k, v in enumerate(self.parts)]
        self.turn += 1

    def step(self, *after):
        jobs = []
        for k, (v, r) in enumerate(zip(self.parts, self.came)):
            c = v.shape[2]
            cut = (c // 3,) * 3 if self.turn == self.cut_at else (c,)
            jobs.append((v, r, self.orders[k][self.turn - 1], cut))
        self.parts = list(join(self.chip, jobs, after))
        self.exchange()
        return tuple(self.parts)

    def done(self):
        return self.turn == len(self.orders[0])

    def result(self, *after):
        return assemble(self.chip, self.orders, tuple(zip(self.parts, self.came)), after=after)


def merge_kernel(bits, mates, chip_ref, *refs):
    small, (v_ref, r_ref), outs = refs[:6], refs[6:8], refs[-3:]
    up = lambda bit: (chip_ref[0] & bit) // bit
    m = small[0].shape[0]
    c = small[0].shape[2]
    far = v_ref.shape[0]
    for k in range(3):
        for ref, side in ((small[2 * k], up(bits[k])), (small[2 * k + 1], 1 - up(bits[k]))):
            for i in range(m):
                outs[k][side * m + i] = ref[i]
    for k in range(3):
        out_ref = outs[mates[k]]
        wide = v_ref.shape[2] // 3
        for ref, side in ((v_ref, up(bits[3])), (r_ref, 1 - up(bits[3]))):
            for h in range(wide // c):
                for i in range(far):
                    lo = k * wide + h * c
                    out_ref[2 * m + h * 2 * far + side * far + i] = ref[i, :, lo : lo + c]


def cross_kernel(bits, skip, chip_ref, *refs):
    outs = refs[-3:]
    for k, bit in enumerate(bits):
        v_ref, r_ref, out_ref = refs[2 * k], refs[2 * k + 1], outs[k]
        up = (chip_ref[0] & bit) // bit
        c = v_ref.shape[2]
        m = out_ref.shape[0] // 2
        for ref, side in ((v_ref, up), (r_ref, 1 - up)):
            for h in range(out_ref.shape[2] // c):
                for i in range(m):
                    out_ref[side * m + i, :, h * c : (h + 1) * c] = ref[skip + h * m + i]


def merge_steps(small, large, *after):
    n, turn = small.n, len(small.orders[0]) - 1
    next_small = [order[turn] for order in small.orders]
    next_large = [order[large.cut_at] for order in large.orders]
    mates = [next_small.index(bit) for bit in next_large]
    bits = [order[turn - 1] for order in small.orders] + [large.orders[0][large.cut_at - 1]]
    v, r = large.parts[0], large.came[0]
    _, rows, c = small.parts[0].shape
    m = 2 * small.parts[0].shape[0]
    far = 2 * v.shape[0]
    wide = v.shape[2] // 3
    flat = [t for pair in zip(small.parts, small.came) for t in pair]
    outs = pl.pallas_call(
        functools.partial(merge_kernel, bits, mates),
        out_shape=(shape((m + far * (wide // c), rows, c), BF),) * 3,
        in_specs=[SCALAR] + [WHOLE] * 8 + [HBM] * len(after),
        out_specs=(WHOLE,) * 3,
        compiler_params=params(),
        name="merge",
    )(small.chip, *flat, v, r, *after)
    came = [swap(t, bit, n) for t, bit in zip(outs, next_small)]

    def small_result(*after):
        return assemble(small.chip, small.orders, tuple(zip(outs, came)), after=after)

    def large_on(*after):
        pairs = [t for k in range(3) for t in (outs[mates[k]], came[mates[k]])]
        parts = pl.pallas_call(
            functools.partial(cross_kernel, next_large, m),
            out_shape=(shape((2 * far, rows, wide), BF),) * 3,
            in_specs=[SCALAR] + [WHOLE] * 6 + [HBM] * len(after),
            out_specs=(WHOLE,) * 3,
            compiler_params=params(),
            name="cross",
        )(large.chip, *pairs, *after)
        large.parts = list(parts)
        large.turn = large.cut_at + 1
        large.exchange()
        return tuple(parts)

    return outs, small_result, large_on


def product_kernel(n, firsts, two_l, two_r, count, chip_ref, l0_ref, l1_ref, *rest):
    r_refs, outs, (turned_ref, buf_ref, sem) = rest[:count], rest[-9:-3], rest[-3:]
    length = l0_ref.shape[0]
    width = turned_ref.shape[1]
    rows = width // n
    tile = width // 3
    for k in range(turned_ref.shape[0]):
        cols = slice(k * width, (k + 1) * width)
        turned_ref[k, :, 0:length] = l0_ref[:, cols].T
        turned_ref[k, :, length:] = l1_ref[:, cols].T

    def times(slot, lo, w):
        total, at = None, 0
        for r_ref in r_refs:
            m = r_ref.shape[0]
            term = mm(turned_ref[slot, :, at : at + m], r_ref[:, lo : lo + w])
            total = term if total is None else total + term
            at += m
        return total

    copies = []
    for t, bit in enumerate(firsts):
        (s0, c0), (s1, c1) = (
            (q // 3 if two_l else 0, (q if two_r else q % 3) * tile) for q in (2 * t, 2 * t + 1)
        )
        if s0 == s1 and c1 == c0 + tile:
            value = times(s0, c0, 2 * tile)
        else:
            value = jnp.concatenate([times(s0, c0, tile), times(s1, c1, tile)], axis=1)
        up = (chip_ref[0] & bit) // bit
        for k in range(n):
            at = (k // (2 * bit)) * bit + k % bit
            goes = 1 - up if k & bit else up
            buf_ref[t, goes, at] = value[k * rows : (k + 1) * rows].astype(BF)
        for goes in range(2):
            copy = pltpu.make_async_copy(buf_ref.at[t, goes], outs[2 * t + goes], sem.at[2 * t + goes])
            copy.start()
            copies.append(copy)
    for copy in copies:
        copy.wait()


def product(chip, l0, l1, r0, r1, width, n, firsts, after=()):
    length = l0.shape[0]
    rights = (r0,) + (r1 if isinstance(r1, tuple) else (r1,))
    two_l, two_r = l0.shape[1] > width, r0.shape[1] > width
    block = (n // 2, width // n, 2 * width // 3)
    out = pl.pallas_call(
        functools.partial(product_kernel, n, firsts, two_l, two_r, len(rights)),
        out_shape=(shape(block, BF),) * 6,
        in_specs=[SCALAR] + [WHOLE] * (2 + len(rights)) + [HBM] * len(after),
        out_specs=(HBM,) * 6,
        scratch_shapes=[
            pltpu.VMEM((1 + two_l, width, 2 * length), BF),
            pltpu.VMEM((3, 2) + block, BF),
            pltpu.SemaphoreType.DMA((6,)),
        ],
        compiler_params=params(),
        cost_estimate=cost(8 * length * width * width, 12e6),
        name="product",
    )(chip, l0, l1, *rights, *after)
    return tuple((out[2 * k], out[2 * k + 1]) for k in range(3))


def split_kernel(jobs, chip_ref, *refs):
    outs = refs[-2 * len(jobs) :]
    at = 0
    for k, (bit, pos, count) in enumerate(jobs):
        keep_ref, send_ref = outs[2 * k], outs[2 * k + 1]
        up = (chip_ref[0] & bit) // bit
        lo = 0
        for _ in range(count):
            v_ref, r_ref = refs[at], refs[at + 1]
            at += 2
            c = v_ref.shape[2]
            for i in range(keep_ref.shape[0]):
                for out_ref, goes in ((send_ref, 1 - up), (keep_ref, up)):
                    j = put(i, pos) + goes * (1 << pos)
                    total = v_ref[j].astype(F32) + r_ref[j].astype(F32)
                    out_ref[i, :, lo : lo + c] = total.astype(BF)
            lo += c


def split(chip, jobs, after=()):
    flat = [t for pairs, _, _ in jobs for pair in pairs for t in pair]
    outs, plan = [], []
    for pairs, bit, left in jobs:
        m, rows, _ = pairs[0][0].shape
        cols = sum(v.shape[2] for v, _ in pairs)
        outs += [shape((m // 2, rows, cols), BF)] * 2
        plan.append((bit, len(left) - 1 - left.index(bit), len(pairs)))
    out = pl.pallas_call(
        functools.partial(split_kernel, plan),
        out_shape=tuple(outs),
        in_specs=[SCALAR] + [WHOLE] * len(flat) + [HBM] * len(after),
        out_specs=(WHOLE,) * len(outs),
        compiler_params=params(),
        name="split",
    )(chip, *flat, *after)
    return [(out[2 * k], out[2 * k + 1]) for k in range(len(jobs))]


def finish_kernel(v_ref, r_ref, *rest):
    rest[-1][...] = v_ref[0].astype(F32) + r_ref[0].astype(F32)


def finish(v, r, after=()):
    return pl.pallas_call(
        finish_kernel,
        out_shape=shape(v.shape[1:], F32),
        in_specs=[WHOLE] * 2 + [HBM] * len(after),
        out_specs=WHOLE,
        compiler_params=params(),
        name="finish",
    )(v, r, *after)


def pack_kernel(side_ref, a_ref, b_ref, c_ref, d_ref, lo_ref, hi_ref, pre_ref, *rest):
    out_ref = rest[-1]
    lanes = out_ref.shape[1]
    per = a_ref.shape[1] // lanes

    def row(at, ref, i, rounded=False):
        for k in range(ref.shape[1] // lanes):
            value = ref[i : i + 1, k * lanes : (k + 1) * lanes]
            out_ref[at + k : at + k + 1, :] = value.astype(BF).astype(F32) if rounded else value

    for k, (ref, i) in enumerate(((c_ref, 0), (c_ref, 1), (b_ref, 3), (a_ref, 1))):
        row(k * per, ref, i)
    many = pre_ref.shape[1] // lanes
    for s in range(2):

        @pl.when(side_ref[0] == s)
        def _():
            for i in range(2):
                row(4 * per + (s ^ i) * many, pre_ref, i)

    at = 4 * per + 2 * many
    for ref in (lo_ref, hi_ref):
        for k in range(ref.shape[1] // lanes):
            out_ref[at : at + HEADS, :] = ref[:, k * lanes : (k + 1) * lanes]
            at += HEADS
    out_ref[at:, :] = jnp.zeros((out_ref.shape[0] - at, lanes), F32)
    parts = ((d_ref, 0), (d_ref, 1), (b_ref, 2), (b_ref, 0), (b_ref, 1), (a_ref, 0))
    for k, (ref, i) in enumerate(parts):
        row(at + k * per, ref, i, True)


def pack(side, arrays, rows, after=()):
    return pl.pallas_call(
        pack_kernel,
        out_shape=shape((rows, 128), F32),
        in_specs=[SCALAR] + [WHOLE] * len(arrays) + [HBM] * len(after),
        out_specs=WHOLE,
        compiler_params=params(),
        name="pack",
    )(side, *arrays, *after)


def meet_kernel(bit, rows, chip_ref, v_ref, r_ref, *rest):
    out_ref = rest[-1]
    out_ref[0:SUM_ROWS, :] = v_ref[0:SUM_ROWS, :] + r_ref[0:SUM_ROWS, :]
    up = (chip_ref[0] & bit) // bit
    for i in range((v_ref.shape[0] - SUM_ROWS) // rows):
        src = slice(SUM_ROWS + i * rows, SUM_ROWS + (i + 1) * rows)
        for ref, side in ((v_ref, up), (r_ref, 1 - up)):
            at = pl.multiple_of(SUM_ROWS + (2 * i + side) * rows, 8)
            out_ref[pl.ds(at, rows), :] = ref[src, :]


def meet(chip, v, r, bit, rows, after=()):
    total = 2 * v.shape[0] - SUM_ROWS
    return pl.pallas_call(
        functools.partial(meet_kernel, bit, rows),
        out_shape=shape((total, v.shape[1]), F32),
        in_specs=[SCALAR, WHOLE, WHOLE] + [HBM] * len(after),
        out_specs=WHOLE,
        compiler_params=params(),
        name="meet",
    )(chip, v, r, *after)


class Reduction:
    def __init__(self, chip, parts, n):
        last, orders = orders_out(n)
        self.chip, self.n = chip, n
        self.orders = [part[::-1] for part in orders]
        self.tail = last[::-1]
        self.left = [all_bits(n)[::-1] for _ in range(3)]
        self.pairs = [
            (keep, self.exchange(k, self.orders[k].pop(0), send)) for k, (keep, send) in enumerate(parts)
        ]

    def exchange(self, k, bit, send):
        self.left[k] = [b for b in self.left[k] if b != bit]
        return swap(send, bit, self.n)

    def plan(self):
        chains = [[k] for k in range(len(self.pairs))]
        if len(self.pairs) > 1 and not self.orders[0]:
            chains = [list(range(len(self.pairs)))]
            self.orders = [list(self.tail)]
        bits = [self.orders[chain[0]].pop(0) for chain in chains]
        return [
            ([self.pairs[j] for j in chain], bit, list(self.left[chain[0]]))
            for chain, bit in zip(chains, bits)
        ]

    def parted(self):
        return len(self.pairs) > 1 and not self.orders[0]

    def take(self, other):
        self.pairs = other.pairs + self.pairs

    def go(self, jobs, outs):
        self.pairs = [
            (keep, self.exchange(k, bit, send))
            for k, ((_, bit, _), (keep, send)) in enumerate(zip(jobs, outs))
        ]

    def done(self):
        return len(self.pairs) == 1 and not self.orders[0]

    def result(self, *after):
        return finish(*self.pairs[0], after)


def step(sums, *after):
    plans = [s.plan() for s in sums]
    outs = split(sums[0].chip, [job for jobs in plans for job in jobs], after)
    kept = tuple(keep for keep, _ in outs)
    for s, jobs in zip(sums, plans):
        s.go(jobs, outs[: len(jobs)])
        outs = outs[len(jobs) :]
    return kept


def fc2_rows_kernel(side_ref, own_ref, other_ref, out_ref):
    rows = own_ref.shape[0]
    width = out_ref.shape[1]
    for s in range(2):

        @pl.when(side_ref[0] == s)
        def _():
            for half, ref in ((s, own_ref), (1 - s, other_ref)):
                for part in range(2):
                    lo = (2 * half + part) * rows
                    out_ref[lo : lo + rows, :] = ref[:, part * width : (part + 1) * width]


def fc2_rows(side, own, other):
    return pl.pallas_call(
        fc2_rows_kernel,
        out_shape=shape((4 * own.shape[0], own.shape[1] // 4), F32),
        in_specs=[SCALAR, WHOLE, WHOLE],
        out_specs=WHOLE,
        compiler_params=params(),
        name="fc2_rows",
    )(side, own, other)


def attn_rows_kernel(side_ref, own_ref, other_ref, qkv_ref, proj_ref):
    width = proj_ref.shape[1]
    for s in range(2):

        @pl.when(side_ref[0] == s)
        def _():
            low, high = (own_ref, other_ref) if s == 0 else (other_ref, own_ref)
            qkv_ref[:, 0 : 2 * width] = low[...]
            qkv_ref[:, 2 * width :] = high[:, 0:width]
            proj_ref[...] = high[:, width:]


def attn_rows(side, own, other):
    rows, width = own.shape[0], own.shape[1] // 2
    return pl.pallas_call(
        attn_rows_kernel,
        out_shape=(shape((rows, 3 * width), F32), shape((rows, width), F32)),
        in_specs=[SCALAR, WHOLE, WHOLE],
        out_specs=(WHOLE, WHOLE),
        compiler_params=params(),
        name="attn_rows",
    )(side, own, other)


def hold_kernel(*refs):
    pass


def hold(values, *after):
    many = isinstance(values, tuple)
    values = values if many else (values,)
    out = pl.pallas_call(
        hold_kernel,
        out_shape=tuple(shape(v.shape, v.dtype) for v in values),
        in_specs=[HBM] * (len(values) + len(after)),
        out_specs=(HBM,) * len(values),
        input_output_aliases={k: k for k in range(len(values))},
        name="hold",
    )(*values, *after)
    return out if many else out[0]


def attention_kernel(
    side_ref,
    own_ref,
    other_ref,
    normed_ref,
    bqv_ref,
    strip_ref,
    keep_ref,
    x_ref,
    mod_ref,
    bproj_ref,
    qh_ref,
    kh_ref,
    vh_ref,
    mine_ref,
    theirs_ref,
    attended_ref,
    middle_ref,
    normed_two_ref,
    w_out_ref,
    w_ref,
    flat_ref,
    mix_ref,
    sem,
):
    length, width = x_ref.shape
    hd = width // HEADS
    tile = 384
    wait = fetch_halves(side_ref, own_ref, other_ref, w_ref, sem)
    normed = normed_ref[...]

    def project(slot, lo, cols, at, bias_at):
        def body(o):
            y = mm(normed, w_ref[slot, :, pl.ds(lo + o, tile)])
            if bias_at is not None:
                y = y + bqv_ref[:, pl.ds(bias_at + o, tile)]
            flat_ref[:, pl.ds(at + o, tile)] = y.astype(BF)

        strips(cols, tile, body)

    wait(0)
    project(0, 0, width, 0, 0)
    project(0, width, width, width, None)
    wait(1)
    keep_out = pltpu.make_async_copy(w_ref.at[1, :, pl.ds(width, width)], w_out_ref, sem.at[2])
    keep_out.start()
    project(1, 0, width, 2 * width, width)
    for h in range(HEADS):
        qh_ref[h] = flat_ref[:, h * hd : (h + 1) * hd]
        kh_ref[h] = flat_ref[:, width + h * hd : width + (h + 1) * hd]
        vh_ref[h] = flat_ref[:, 2 * width + h * hd : 2 * width + (h + 1) * hd]
    keep = keep_ref[...] > 0.0

    def head(h, carry):
        sc = mm_nt(qh_ref[h], kh_ref[h]) * (hd**-0.5) + bias_of(strip_ref[h])
        sc = jnp.where(keep, sc, -1e30)
        ex = jnp.exp(sc - jnp.max(sc, axis=-1, keepdims=True))
        soft = ex / jnp.sum(ex, axis=-1, keepdims=True)
        mix_ref[h] = mm(soft.astype(BF), vh_ref[h]).astype(BF)
        return carry

    lax.fori_loop(0, HEADS, head, 0)
    for h in range(HEADS):
        flat_ref[:, h * hd : (h + 1) * hd] = mix_ref[h]
    mixed = flat_ref[:, 0:width]
    mine_ref[:, 0:width] = normed
    theirs_ref[:, 0:width] = normed
    for s, (normed_at, mixed_at) in enumerate(((mine_ref, theirs_ref), (theirs_ref, mine_ref))):

        @pl.when(side_ref[0] == s)
        def _():
            normed_at[:, width:] = normed
            mixed_at[:, width:] = mixed

    def out(o):
        y = mm(mixed, w_ref[1, :, pl.ds(width + o, tile)]) + bproj_ref[:, pl.ds(o, tile)]
        attended_ref[:, pl.ds(o, tile)] = y

    strips(width, tile, out)
    middle = x_ref[...] + mod_ref[2:3, :] * attended_ref[...]
    middle_ref[...] = middle
    n2, _ = normal(middle)
    normed_two_ref[...] = (n2 * (1.0 + mod_ref[4:5, :]) + mod_ref[3:4, :]).astype(BF)
    keep_out.wait()


def attention(side, own, other, normed, b_qv, bias, keep, x, mod, b_proj):
    length, width = x.shape
    hd = width // HEADS
    per_head = shape((HEADS, length, hd), BF)
    return pl.pallas_call(
        attention_kernel,
        out_shape=(
            per_head,
            per_head,
            per_head,
            shape((length, 2 * width), BF),
            shape((length, 2 * width), BF),
            shape((length, width), F32),
            shape((length, width), F32),
            shape((length, width), BF),
            shape((width, width), BF),
        ),
        in_specs=[SCALAR, HBM, HBM] + [WHOLE] * 7,
        out_specs=(WHOLE,) * 8 + (HBM,),
        scratch_shapes=[
            pltpu.VMEM((2, width, 2 * width), BF),
            pltpu.VMEM((length, 3 * width), BF),
            pltpu.VMEM((HEADS, length, hd), BF),
            pltpu.SemaphoreType.DMA((3,)),
        ],
        compiler_params=params(),
        cost_estimate=cost(8 * length * width * width + 4 * length * length * width, 24e6),
        name="attention",
    )(side, own, other, normed, b_qv, bias, keep, x, mod, b_proj)


def fc2_tiles(width, half, tile):
    part = tile // 2
    per = width // part
    at = lambda q: (q % per, half // width + q // per)
    return [pl.BlockSpec((part, width), lambda t, k=k: at(2 * t + k)) for k in range(2)]


def mlp_half(normed_two_ref, b_ref, c0_ref, c1_ref, bf1_ref, hid_ref, slope_ref):
    act, slope = gelu_parts(mm(normed_two_ref[...], b_ref[...]) + bf1_ref[...])
    hid = act.astype(BF)
    hid_ref[...] = hid
    slope_ref[...] = slope
    return mm(hid, jnp.concatenate([c0_ref[...], c1_ref[...]], axis=0))


def mlp_first_kernel(normed_two_ref, b_ref, c0_ref, c1_ref, bf1_ref, hid_ref, slope_ref, part_ref):
    total = mlp_half(normed_two_ref, b_ref, c0_ref, c1_ref, bf1_ref, hid_ref, slope_ref)

    @pl.when(pl.program_id(0) == 0)
    def _():
        part_ref[...] = total

    @pl.when(pl.program_id(0) > 0)
    def _():
        part_ref[...] += total


def mlp_last_kernel(
    normed_two_ref,
    b_ref,
    c0_ref,
    c1_ref,
    bf1_ref,
    part_ref,
    bf2_ref,
    middle_ref,
    cot_ref,
    mod_ref,
    place_ref,
    present_ref,
    hid_ref,
    slope_ref,
    g_branch_ref,
    out_ref,
    sums_ref,
    acc_ref,
):
    t = pl.program_id(0)
    total = mlp_half(normed_two_ref, b_ref, c0_ref, c1_ref, bf1_ref, hid_ref, slope_ref)

    @pl.when(t == 0)
    def _():
        acc_ref[...] = part_ref[...] + total

    @pl.when(t > 0)
    def _():
        acc_ref[...] += total

    @pl.when(t == pl.num_programs(0) - 1)
    def _():
        branch = acc_ref[...] + bf2_ref[...]
        cot = cot_ref[...]
        gate = mod_ref[5:6, :]
        result = middle_ref[...] + gate * branch
        out = jnp.where(present_ref[...] > 0.0, result, 0.0).astype(BF)
        out_ref[...] = mm_tn(place_ref[...], out).astype(BF)
        g_branch = (cot * gate).astype(BF)
        g_branch_ref[...] = g_branch
        sums_ref[0:1, :] = jnp.sum(cot * branch, axis=0, keepdims=True)
        sums_ref[1:2, :] = jnp.sum(g_branch.astype(F32), axis=0, keepdims=True)


def mlp(normed_two, weights, bf1, last=None):
    length, width = normed_two.shape
    half = weights.shape[1] // 2
    tile = 2 * width // 3
    fixed = lambda a: pl.BlockSpec(a.shape, lambda t: (0, 0))
    cols = lambda r: pl.BlockSpec((r, tile), lambda t: (0, t))
    rows = fc2_tiles(width, half, tile)
    whole = lambda r: pl.BlockSpec((r, width), lambda t: (0, 0))
    more = last or ()
    outs = [shape((length, half), BF), shape((length, half), F32)]
    if last:
        outs += [shape((length, width), BF), shape((length, width), BF), shape((8, width), F32)]
    else:
        outs += [shape((length, width), F32)]
    return pl.pallas_call(
        mlp_last_kernel if last else mlp_first_kernel,
        grid=(half // tile,),
        out_shape=tuple(outs),
        in_specs=[fixed(normed_two), cols(width)] + rows + [cols(1)] + [fixed(a) for a in more],
        out_specs=tuple([cols(length), cols(length)] + [whole(o.shape[0]) for o in outs[2:]]),
        scratch_shapes=[pltpu.VMEM((length, width), F32)] if last else [],
        compiler_params=params(),
        cost_estimate=cost(4 * length * width * half, 16e6),
        name="mlp",
    )(normed_two, weights, weights, weights, bf1, *more)


def mlp_back_kernel(
    g_branch_ref,
    b0_ref,
    b1_ref,
    c00_ref,
    c01_ref,
    c10_ref,
    c11_ref,
    slope0_ref,
    slope1_ref,
    middle_ref,
    attended_ref,
    cot_ref,
    mod_ref,
    w_out_ref,
    *rest,
):
    pre0_ref, pre1_ref, bsum_ref, g_middle_ref, g_att_ref, g_mixed_ref, sums_ref, acc_ref = rest[-8:]
    t = pl.program_id(0)
    g_branch = g_branch_ref[...]
    total = None
    for i, (b_ref, c_refs, slope_ref, pre_ref) in enumerate(
        (
            (b0_ref, (c00_ref, c01_ref), slope0_ref, pre0_ref),
            (b1_ref, (c10_ref, c11_ref), slope1_ref, pre1_ref),
        )
    ):
        c = jnp.concatenate([ref[...] for ref in c_refs], axis=0)
        pre = (mm_nt(g_branch, c) * slope_ref[...]).astype(BF)
        pre_ref[...] = pre
        bsum_ref[i : i + 1, :] = jnp.sum(pre.astype(F32), axis=0, keepdims=True)
        part = mm_nt(pre, b_ref[...])
        total = part if total is None else total + part

    @pl.when(t == 0)
    def _():
        acc_ref[...] = total

    @pl.when(t > 0)
    def _():
        acc_ref[...] += total

    @pl.when(t == pl.num_programs(0) - 1)
    def _():
        g_n2 = acc_ref[...]
        n2, inv2 = normal(middle_ref[...])
        sums_ref[0:1, :] = jnp.sum(g_n2, axis=0, keepdims=True)
        sums_ref[1:2, :] = jnp.sum(g_n2 * n2, axis=0, keepdims=True)
        g_middle = cot_ref[...] + normal_back(g_n2 * (1.0 + mod_ref[4:5, :]), n2, inv2)
        g_middle_ref[...] = g_middle
        sums_ref[2:3, :] = jnp.sum(g_middle * attended_ref[...], axis=0, keepdims=True)
        g_att = (g_middle * mod_ref[2:3, :]).astype(BF)
        g_att_ref[...] = g_att
        sums_ref[3:4, :] = jnp.sum(g_att.astype(F32), axis=0, keepdims=True)
        g_mixed_ref[...] = mm_nt(g_att, w_out_ref[...]).astype(BF)


def mlp_back(g_branch, weights, slope0, slope1, middle, attended, cot, mod, w_out, after=()):
    length, width = middle.shape
    half = weights[0].shape[1] // 2
    tile = 2 * width // 3
    fixed = lambda a: pl.BlockSpec(a.shape, lambda t: (0, 0))
    cols = lambda r: pl.BlockSpec((r, tile), lambda t: (0, t))
    rows = fc2_tiles(width, half, tile)
    whole = lambda r: pl.BlockSpec((r, width), lambda t: (0, 0))
    return pl.pallas_call(
        mlp_back_kernel,
        grid=(half // tile,),
        out_shape=(
            shape((length, half), BF),
            shape((length, half), BF),
            shape((2, half), F32),
            shape((length, width), F32),
            shape((length, width), BF),
            shape((length, width), BF),
            shape((8, width), F32),
        ),
        in_specs=[
            fixed(g_branch),
            cols(width),
            cols(width),
            *rows,
            *rows,
            cols(length),
            cols(length),
            fixed(middle),
            fixed(attended),
            fixed(cot),
            fixed(mod),
            fixed(w_out),
        ]
        + [HBM] * len(after),
        out_specs=(
            cols(length),
            cols(length),
            cols(2),
            whole(length),
            whole(length),
            whole(length),
            whole(8),
        ),
        scratch_shapes=[pltpu.VMEM((length, width), F32)],
        compiler_params=params(),
        cost_estimate=cost(8 * length * width * half, 32e6),
        name="mlp_back",
    )(
        g_branch,
        *weights,
        weights[0],
        weights[0],
        weights[1],
        weights[1],
        slope0,
        slope1,
        middle,
        attended,
        cot,
        mod,
        w_out,
        *after,
    )


def heads_back(q_ref, k_ref, v_ref, strip_ref, keep, gm_ref, dq_ref, dk_ref, dv_ref, sums_ref, start):
    scale = q_ref.shape[2] ** -0.5
    length = q_ref.shape[1]

    def head(i, carry):
        h = start + i
        q, k, v, gm = q_ref[h], k_ref[h], v_ref[h], gm_ref[i]
        sc = mm_nt(q, k) * scale + bias_of(strip_ref[h])
        sc = jnp.where(keep, sc, -1e30)
        ex = jnp.exp(sc - jnp.max(sc, axis=-1, keepdims=True))
        soft = ex / jnp.sum(ex, axis=-1, keepdims=True)
        dv_ref[i] = mm_tn(soft.astype(BF), gm).astype(BF)
        dp = mm_nt(gm, v)
        ds = (soft * (dp - jnp.sum(dp * soft, axis=-1, keepdims=True))).astype(BF)
        dq_ref[i] = (mm(ds, k) * scale).astype(BF)
        dk_ref[i] = (mm_tn(ds, q) * scale).astype(BF)
        dsf = ds.astype(F32)
        total = jnp.zeros((GRID, sums_ref.shape[2]), F32)
        blank = jnp.zeros((GRID, sums_ref.shape[2] - length), F32)
        for y in range(GRID):
            rows = jnp.concatenate([dsf[y * GRID : (y + 1) * GRID, :], blank], axis=1)
            by = (GRID - 1 - y) * GRID
            total = total + (pltpu.roll(rows, by, 1) if by else rows)
        sums_ref[i] = total
        return carry

    lax.fori_loop(0, dq_ref.shape[0], head, 0, unroll=2)


def first_heads_kernel(qh_ref, kh_ref, vh_ref, strip_ref, keep_ref, g_mixed_ref, *rest):
    dq_ref, dk_ref, dv_ref, sums_ref, gm_ref = rest[-5:]
    hd = qh_ref.shape[2]
    for i in range(HEADS // 2):
        gm_ref[i] = g_mixed_ref[:, i * hd : (i + 1) * hd]
    heads_back(
        qh_ref, kh_ref, vh_ref, strip_ref, keep_ref[...] > 0.0, gm_ref, dq_ref, dk_ref, dv_ref, sums_ref, 0
    )


def first_heads(qh, kh, vh, strip, keep, g_mixed, after=()):
    heads, length, hd = qh.shape
    some = shape((heads // 2, length, hd), BF)
    return pl.pallas_call(
        first_heads_kernel,
        out_shape=(some, some, some, shape((heads // 2,) + strip.shape[1:], F32)),
        in_specs=[WHOLE] * 6 + [HBM] * len(after),
        out_specs=(WHOLE,) * 4,
        scratch_shapes=[pltpu.VMEM((heads // 2, length, hd), BF)],
        compiler_params=params(),
        cost_estimate=cost(5 * length * length * heads * hd, 16e6),
        name="first_heads",
    )(qh, kh, vh, strip, keep, g_mixed, *after)


def last_heads_kernel(
    side_ref,
    qh_ref,
    kh_ref,
    vh_ref,
    strip_ref,
    keep_ref,
    g_mixed_ref,
    g_att_ref,
    fq_ref,
    fk_ref,
    fv_ref,
    fsum_ref,
    *rest,
):
    mine_ref, top_ref, low_ref, lo_ref, hi_ref, sums_ref, both_ref, gm_ref, dq_ref, dk_ref, dv_ref, strips_ref = rest[-12:]
    theirs_ref = both_ref
    width = g_mixed_ref.shape[1]
    hd = qh_ref.shape[2]
    half = HEADS // 2
    for i in range(half):
        gm_ref[i] = g_mixed_ref[:, (half + i) * hd : (half + i + 1) * hd]
    heads_back(
        qh_ref, kh_ref, vh_ref, strip_ref, keep_ref[...] > 0.0, gm_ref, dq_ref, dk_ref, dv_ref, strips_ref, half
    )
    for s, (qk_at, v_at) in enumerate(((mine_ref, theirs_ref), (theirs_ref, mine_ref))):

        @pl.when(side_ref[0] == s)
        def _():
            for h in range(HEADS):
                q, k, v = (fq_ref, fk_ref, fv_ref) if h < half else (dq_ref, dk_ref, dv_ref)
                i = h % half
                qk_at[:, h * hd : (h + 1) * hd] = q[i]
                qk_at[:, width + h * hd : width + (h + 1) * hd] = k[i]
                v_at[:, h * hd : (h + 1) * hd] = v[i]
            v_at[:, width:] = g_att_ref[...]
            sums_ref[0:1, :] = jnp.sum(qk_at[:, 0:width].astype(F32), axis=0, keepdims=True)
            sums_ref[1:2, :] = jnp.sum(v_at[:, 0:width].astype(F32), axis=0, keepdims=True)

    length = both_ref.shape[0]
    top_ref[...] = both_ref[0 : length // 2, :]
    low_ref[...] = both_ref[length // 2 :, :]
    lanes = lo_ref.shape[1]
    for part, ref in enumerate((fsum_ref, strips_ref)):
        lo = jnp.zeros((half, lanes), F32)
        hi = jnp.zeros((half, lanes), F32)
        j = lax.broadcasted_iota(jnp.int32, lo.shape, 1) % GRID
        for i in range(GRID):
            k = GRID - 1 - i
            row = ref[:, i, :]
            a = jnp.where(j < GRID - k, row, 0.0)
            lo = lo + (pltpu.roll(a, k, 1) if k else a)
            if k:
                hi = hi + pltpu.roll(jnp.where(j < GRID - k, 0.0, row), lanes - (GRID - k), 1)
        lo_ref[part * half : (part + 1) * half, :] = lo
        hi_ref[part * half : (part + 1) * half, :] = hi


def last_heads(side, qh, kh, vh, strip, keep, g_mixed, g_att, firsts, after=()):
    length, width = g_mixed.shape
    heads, _, hd = qh.shape
    per_head = pltpu.VMEM((heads // 2, length, hd), BF)
    window = shape((heads, strip.shape[2]), F32)
    return pl.pallas_call(
        last_heads_kernel,
        out_shape=(
            shape((length, 2 * width), BF),
            shape((length // 2, 2 * width), BF),
            shape((length // 2, 2 * width), BF),
            window,
            window,
            shape((8, width), F32),
        ),
        in_specs=[SCALAR] + [WHOLE] * 11 + [HBM] * len(after),
        out_specs=(WHOLE,) * 6,
        scratch_shapes=[pltpu.VMEM((length, 2 * width), BF)]
        + [per_head] * 4 + [pltpu.VMEM((heads // 2,) + strip.shape[1:], F32)],
        compiler_params=params(),
        cost_estimate=cost(5 * length * length * width, 16e6),
        name="last_heads",
    )(side, qh, kh, vh, strip, keep, g_mixed, g_att, *firsts, *after)


def tokens_back_kernel(
    side_ref,
    own_ref,
    other_ref,
    mine_ref,
    top_ref,
    low_ref,
    x_ref,
    g_middle_ref,
    mod_ref,
    place_ref,
    *rest,
):
    out_ref, sums_ref, w_ref, acc_ref, qk_ref, v_ref, sem = rest[-7:]
    length, width = x_ref.shape
    wait = fetch_halves(side_ref, own_ref, other_ref, w_ref, sem)
    half = length // 2

    @pl.when(side_ref[0] == 0)
    def _():
        qk_ref[...] = mine_ref[...]
        v_ref[0:half, :] = top_ref[:, 0:width]
        v_ref[half:, :] = low_ref[:, 0:width]

    @pl.when(side_ref[0] == 1)
    def _():
        qk_ref[0:half, :] = top_ref[...]
        qk_ref[half:, :] = low_ref[...]
        v_ref[...] = mine_ref[:, 0:width]

    wait(0)
    acc_ref[...] = mm_nt(qk_ref[...], w_ref[0])
    wait(1)
    g_n1 = acc_ref[...] + mm_nt(v_ref[...], w_ref[1, :, 0:width])
    n1, inv1 = normal(x_ref[...])
    sums_ref[0:1, :] = jnp.sum(g_n1, axis=0, keepdims=True)
    sums_ref[1:2, :] = jnp.sum(g_n1 * n1, axis=0, keepdims=True)
    g_x = g_middle_ref[...] + normal_back(g_n1 * (1.0 + mod_ref[1:2, :]), n1, inv1)
    out_ref[...] = mm_tn(place_ref[...], g_x.astype(BF)).astype(BF)


def tokens_back(side, own, other, mine, theirs, x, g_middle, mod, place, after=()):
    length, width = x.shape
    return pl.pallas_call(
        tokens_back_kernel,
        out_shape=(shape((length, width), BF), shape((8, width), F32)),
        in_specs=[SCALAR, HBM, HBM] + [WHOLE] * 7 + [HBM] * len(after),
        out_specs=(WHOLE,) * 2,
        scratch_shapes=[
            pltpu.VMEM((2, width, 2 * width), BF),
            pltpu.VMEM((length, width), F32),
            pltpu.VMEM((length, 2 * width), BF),
            pltpu.VMEM((length, width), BF),
            pltpu.SemaphoreType.DMA((2,)),
        ],
        compiler_params=params(),
        cost_estimate=cost(6 * length * width * width, 16e6),
        name="tokens_back",
    )(side, own, other, mine, *theirs, x, g_middle, mod, place, *after)


def local(
    n,
    tokens,
    condition,
    kept_index,
    kept_count,
    cotangent,
    w_ada,
    w_qkv,
    w_proj,
    w_fc1,
    w_fc2,
    b_ada,
    b_qv,
    b_proj,
    b_fc1,
    b_fc2,
    rel_table,
):
    side = lax.axis_index("stream")
    chip = lax.axis_index("dp")
    length, width = tokens.shape[2], tokens.shape[3]
    ff = w_fc1.shape[1]
    rows = width // n
    cut = ff // (2 * n)
    first = side == 0
    side_word = side.astype(jnp.int32).reshape(1)
    chip_word = chip.astype(jnp.int32).reshape(1)

    order_first, order_parts = orders_out(n)
    firsts = tuple(part[-1] for part in order_parts)

    ordinal = jnp.arange(length, dtype=jnp.int32)
    count = jnp.where(first, length, kept_count[0])
    position = jnp.where(first, ordinal, kept_index[0])
    place = ((position[None, :] == ordinal[:, None]) & (ordinal[None, :] < count)).astype(BF)
    present = jnp.sum(place.astype(F32), axis=1)
    keep = present.reshape(1, length)
    present = present.reshape(length, 1)
    x = mm(place, tokens[0, 0])
    cot = mm(place, cotangent[0, 0])
    bias = bias_strip(rel_table)

    cond = condition[0, 0]
    sig = jax.nn.sigmoid(cond)
    cond_act = (cond * sig).astype(BF)
    shard_a = attn_shard(side_word, w_qkv, w_proj)
    all_a = Gathering(chip_word, shard_a, n)
    acts = trade(hold(jnp.broadcast_to(cond_act[None], (n, width)), shard_a))
    acts_part = lax.dynamic_slice_in_dim(acts, chip * rows, rows, axis=1)
    shard_bc = mlp_shard(n, side_word, w_fc1, w_fc2, after=(shard_a,))
    last = all_a.step(shard_bc, bias, x, cot, acts_part)
    all_bc = Gathering(chip_word, hold(shard_bc, *last), n)
    for _ in range(len(order_parts[0]) - 2 + len(order_first) - 1):
        last = all_a.step(*last)
    while all_bc.turn < all_bc.cut_at:
        last = all_bc.step(*last)
    acts_twin = swap_stream(acts_part)
    if {p[-1] for p in order_parts} == {p[0] for p in order_parts}:
        last, result_a, on_bc = merge_steps(all_a, all_bc, acts_twin)
        last = on_bc()
    else:
        last = all_a.step(*last, acts_twin)
        result_a = all_a.result
        last = all_bc.step(*last)
    a_own = result_a(*last)
    a_other = swap_stream(a_own)
    mod_part = trade(hold(mm(acts_part, w_ada), a_own))
    last = (mod_part,)
    while not all_bc.done():
        last = all_bc.step(*last)
    modulation = jnp.sum(mod_part, axis=0) + b_ada
    mod = modulation.reshape(6, width)
    n1, _ = normal(x)
    normed = (n1 * (1.0 + mod[1]) + mod[0]).astype(BF)
    qh, kh, vh, lhs_mine, lhs_theirs, attended, middle, normed_two, w_out = attention(
        side_word,
        a_own,
        a_other,
        normed,
        b_qv.reshape(1, -1),
        bias,
        keep,
        x,
        mod,
        b_proj.reshape(1, -1),
    )

    bf1 = jnp.transpose(b_fc1.reshape(n, 2, 2, cut // 2), (1, 2, 0, 3)).reshape(2, 1, ff // 2)
    bf1_own, bf1_other = jnp.where(first, bf1[0], bf1[1]), jnp.where(first, bf1[1], bf1[0])
    bf2 = b_fc2.reshape(1, -1)
    bc_own = all_bc.result(normed_two, bf1_own, bf1_other, bf2, present, place)
    bc_other = swap_stream(bc_own)
    lhs_twin = swap_stream(lhs_theirs)
    n2_twin = swap_stream(normed_two)
    hid0, slope0, part = mlp(normed_two, bc_own, bf1_own)
    hid1, slope1, g_branch, out_tokens, sums_a = mlp(
        normed_two,
        bc_other,
        bf1_other,
        (part, bf2, middle, cot, mod, place, present),
    )

    parts_c = product(
        chip_word, hid0, swap_stream(hid1), g_branch, swap_stream(g_branch), width, n, firsts
    )
    sum_c = Reduction(chip_word, parts_c, n)
    pre0, pre1, pre_sum, g_middle, g_att, g_mixed, sums_b = mlp_back(
        g_branch,
        (bc_own, bc_other),
        slope0,
        slope1,
        middle,
        attended,
        cot,
        mod,
        w_out,
        after=(parts_c[0][0], lhs_twin, n2_twin),
    )
    kept = step([sum_c], g_mixed)
    pre_twin = swap_stream(pre1)
    one = first_heads(qh, kh, vh, bias, keep, g_mixed, after=kept + (pre_twin,))
    kept = step([sum_c], one[0])
    while not sum_c.parted():
        kept = step([sum_c], *kept)
    parts_b = product(chip_word, normed_two, n2_twin, pre0, pre_twin, width, n, firsts, after=kept)
    sum_b = Reduction(chip_word, parts_b, n)
    g_mine, top, low, lo, hi, sums_c = last_heads(
        side_word, qh, kh, vh, bias, keep, g_mixed, g_att, one, after=(parts_b[0][0],)
    )
    g_theirs = (top, low)
    g_twin = (swap_stream(top), swap_stream(low))
    kept = step([sum_b], g_mine) + g_twin
    grad_tokens, sums_d = tokens_back(
        side_word, a_own, a_other, g_mine, g_theirs, x, g_middle, mod, place, after=kept
    )

    kept = (sums_d,)
    while not sum_b.parted():
        kept = step([sum_b], *kept)
    mod_rows = 6 * width // 128
    group = -(-mod_rows // 8) * 8
    told = pack(
        side_word, (sums_a, sums_b, sums_c, sums_d, lo, hi, pre_sum), SUM_ROWS + group, after=kept
    )
    bits = all_bits(n)[::-1]
    came = swap(told, bits[0], n)
    sum_b.take(sum_c)
    kept = (told,)
    while not sum_b.done():
        kept = step([sum_b], *kept)
    told = meet(chip_word, told, came, bits[0], group, after=kept)
    told = meet(chip_word, told, swap(told, bits[1], n), bits[1], group)
    came = swap(told, bits[2], n)
    parts_a = product(
        chip_word, lhs_mine, lhs_twin, g_mine, g_twin, width, n, firsts, after=(told,) + kept
    )
    told = meet(chip_word, told, came, bits[2], group, after=(parts_a[0][0],))
    sum_a = Reduction(chip_word, parts_a, n)
    for b in bits[3:]:
        told = meet(chip_word, told, swap(told, b, n), b, group)
    d_cb = sum_b.result()
    kept = step([sum_a], told, d_cb)
    d_cb_twin = swap_stream(d_cb)
    grad_w_fc2 = fc2_rows(side_word, d_cb, d_cb_twin)
    grad_w_fc1 = fc1_rows(n, side_word, d_cb, d_cb_twin)
    kept = step([sum_a], told, grad_w_fc2)
    twin = swap_stream(told)

    def mods_of(t):
        return t[SUM_ROWS:].reshape(n, -1, 128)[:, :mod_rows].reshape(n, -1)

    g_own, g_twin = mods_of(told), mods_of(twin)
    grad_w_ada = mm_tn(acts_part, g_own.astype(BF)) + mm_tn(acts_twin, g_twin.astype(BF))
    grad_b_ada = jnp.sum(g_own, axis=0) + jnp.sum(g_twin, axis=0)
    kept = step([sum_a], *kept, grad_w_ada, grad_b_ada)
    while not sum_a.done():
        kept = step([sum_a], *kept)
    g_acts = trade(hold(mm_nt(g_own.astype(BF), w_ada), *kept)).reshape(width)
    grad_condition = g_acts * sig * (1.0 + cond * (1.0 - sig))
    sums = told[:SUM_ROWS] + twin[:SUM_ROWS]
    per = width // 128
    at = 4 * per + ff // 128
    grad_b_fc1 = jnp.transpose(sums[4 * per : at].reshape(2, 2, n, cut // 2), (2, 0, 1, 3)).reshape(-1)
    windows = jnp.transpose(sums[at:].reshape(2, -1, HEADS, 128), (0, 2, 1, 3)).reshape(2, HEADS, -1)
    parts = (
        sums[: 2 * per].reshape(-1),
        sums[2 * per : 3 * per].reshape(-1),
        grad_b_fc1,
        sums[3 * per : 4 * per].reshape(-1),
        table_of(windows[0], windows[1]),
    )
    d_a = sum_a.result(g_acts, grad_w_fc1, *parts)
    grad_w_qkv, grad_w_proj = attn_rows(side_word, d_a, swap_stream(d_a))
    return (
        out_tokens[None, None],
        grad_tokens[None, None],
        grad_condition[None, None],
        grad_w_ada,
        grad_w_qkv,
        grad_w_proj,
        grad_w_fc1,
        grad_w_fc2,
        grad_b_ada,
        *parts,
    )


def solution(mesh):
    n = mesh.shape["dp"]

    def body(*args):
        return local(n, *args)

    return jax.shard_map(
        body,
        mesh=mesh,
        in_specs=(
            P("stream", "dp", None, None),
            P("stream", "dp", None),
            P("dp", None),
            P("dp"),
            P("stream", "dp", None, None),
            P("dp", None),
            P("dp", None),
            P("dp", None),
            P("dp", None),
            P("dp", None),
            P(),
            P(),
            P(),
            P(),
            P(),
            P(),
        ),
        out_specs=(
            P("stream", "dp", None, None),
            P("stream", "dp", None, None),
            P("stream", "dp", None),
            P("dp", None),
            P("dp", None),
            P("dp", None),
            P("dp", None),
            P("dp", None),
            P(),
            P(),
            P(),
            P(),
            P(),
            P(),
        ),
        check_vma=False,
    )
```

```python
import functools
import math

import jax
import jax.numpy as jnp
from jax import lax
from jax.experimental import pallas as pl
from jax.experimental.pallas import tpu as pltpu
from jax.sharding import PartitionSpec as P

HEADS = 16
GRID = 16
BF = jnp.bfloat16
F32 = jnp.float32


def swap(v, bit, n):
    return lax.ppermute(v, "dp", [(i, i ^ bit) for i in range(n)])


def swap_stream(v):
    return lax.ppermute(v, "stream", [(0, 1), (1, 0)])


def axis_bits(n):
    k = n.bit_length() - 1
    s = k // 3
    xs = [1 << i for i in range(s)]
    ys = [1 << (s + i) for i in range(s)]
    zs = [1 << i for i in range(2 * s, k)]
    return xs, ys, zs


def all_bits(n):
    return [1 << i for i in range(n.bit_length() - 1)]


def orders_out(n):
    xs, ys, zs = axis_bits(n)
    near = zs[:1]
    return zs[1:][::-1], (near + ys + xs, xs + near + ys, ys + xs + near)


def trade(v):
    return lax.all_to_all(v, "dp", 0, 0, tiled=True)


def mm(a, b):
    return lax.dot_general(a, b, (((1,), (0,)), ((), ())), preferred_element_type=F32)


def mm_nt(a, b):
    return lax.dot_general(a, b, (((1,), (1,)), ((), ())), preferred_element_type=F32)


def mm_tn(a, b):
    return lax.dot_general(a, b, (((0,), (0,)), ((), ())), preferred_element_type=F32)


def normal(v):
    center = v - jnp.mean(v, axis=-1, keepdims=True)
    inv = lax.rsqrt(jnp.mean(center * center, axis=-1, keepdims=True) + 1e-06)
    return center * inv, inv


def normal_back(g, n, inv):
    return inv * (g - jnp.mean(g, axis=-1, keepdims=True) - n * jnp.mean(g * n, axis=-1, keepdims=True))


def bias_windows(table):
    w = 2 * GRID - 1
    t = jnp.transpose(table.reshape(w, w, HEADS)[::-1, ::-1], (2, 0, 1))
    t = jnp.pad(t, ((0, 0), (0, 1), (0, 1))).reshape(HEADS, w + 1, 2, GRID)
    return t[:, :, 0].reshape(HEADS, -1), t[:, :, 1].reshape(HEADS, -1)


def table_of(lo, hi):
    w = 2 * GRID - 1
    t = jnp.stack([lo.reshape(HEADS, w + 1, GRID), hi.reshape(HEADS, w + 1, GRID)], axis=2)
    t = t.reshape(HEADS, w + 1, 2 * GRID)[:, :w, :w]
    return jnp.transpose(t, (1, 2, 0))[::-1, ::-1].reshape(w * w, HEADS)


def gelu_parts(x):
    k = math.sqrt(2.0 / math.pi)
    th = jnp.tanh(k * (x + 0.044715 * x * x * x))
    value = 0.5 * x * (1.0 + th)
    slope = 0.5 * (1.0 + th) + 0.5 * x * (1.0 - th * th) * k * (1.0 + 3 * 0.044715 * x * x)
    return value, slope


VMEM_BYTES = 56 * 1024 * 1024
SUM_ROWS = 200
WHOLE = pl.BlockSpec(memory_space=pltpu.VMEM)
HBM = pl.BlockSpec(memory_space=pl.ANY)
SCALAR = pl.BlockSpec(memory_space=pltpu.SMEM)


def shape(dims, dtype):
    return jax.ShapeDtypeStruct(dims, dtype)


def params():
    return pltpu.CompilerParams(vmem_limit_bytes=VMEM_BYTES)


def cost(flops, size):
    return pl.CostEstimate(flops=int(flops), bytes_accessed=int(size), transcendentals=0)


def strips(total, tile, body):
    def step(i, carry):
        body(pl.multiple_of(i * tile, tile))
        return carry

    lax.fori_loop(0, total // tile, step, 0)


def fetch_halves(side_ref, own_ref, other_ref, w_ref, sem):
    side = side_ref[0]
    mine = pltpu.make_async_copy(own_ref, w_ref.at[side], sem.at[side])
    twin = pltpu.make_async_copy(other_ref, w_ref.at[1 - side], sem.at[1 - side])
    mine.start()
    twin.start()

    def wait(slot):
        pltpu.make_async_copy(own_ref, w_ref.at[slot], sem.at[slot]).wait()

    return wait


def pieces(n, rows, cut, s):
    half = cut // 2
    for part in range(2):
        for k in range(n):
            yield (k * 2 + s) * cut + part * half, (part * n + k) * half, half


def fc1_rows_kernel(n, side_ref, own_ref, other_ref, out_ref):
    rows, ff = out_ref.shape
    cut = ff // (2 * n)
    for s in range(2):

        @pl.when(side_ref[0] == s)
        def _():
            for half, ref in ((s, own_ref), (1 - s, other_ref)):
                for src, dst, w in pieces(n, rows, cut, half):
                    out_ref[:, src : src + w] = ref[:, ff // 2 + dst : ff // 2 + dst + w]


def fc1_rows(n, side, own, other):
    return pl.pallas_call(
        functools.partial(fc1_rows_kernel, n),
        out_shape=shape(own.shape, F32),
        in_specs=[SCALAR, WHOLE, WHOLE],
        out_specs=WHOLE,
        compiler_params=params(),
        name="fc1_rows",
    )(side, own, other)


def strip_kernel(lo_ref, hi_ref, out_ref):
    lanes = lo_ref.shape[1]
    lo, hi = lo_ref[...], hi_ref[...]
    j = lax.broadcasted_iota(jnp.int32, lo.shape, 1) % GRID
    for i in range(GRID):
        k = GRID - 1 - i
        a = pltpu.roll(lo, lanes - k, 1) if k else lo
        out_ref[:, i, :] = jnp.where(j < GRID - k, a, pltpu.roll(hi, GRID - k, 1))


def bias_strip(table):
    lo, hi = bias_windows(table)
    return pl.pallas_call(
        strip_kernel,
        out_shape=shape((HEADS, GRID, lo.shape[1]), F32),
        in_specs=[WHOLE, WHOLE],
        out_specs=WHOLE,
        name="bias_strip",
    )(lo, hi)


def bias_of(strip):
    return jnp.concatenate(
        [strip[:, (GRID - 1 - y) * GRID : (2 * GRID - 1 - y) * GRID] for y in range(GRID)], axis=0
    )


def put(i, pos):
    return (i >> pos) << (pos + 1) | (i & ((1 << pos) - 1))


def attn_shard_kernel(side_ref, qkv_ref, proj_ref, out_ref):
    width = proj_ref.shape[1]
    for s in range(2):

        @pl.when(side_ref[0] == s)
        def _():
            if s == 0:
                out_ref[0] = qkv_ref[:, 0 : 2 * width]
            else:
                out_ref[0, :, 0:width] = qkv_ref[:, 2 * width :]
                out_ref[0, :, width:] = proj_ref[...]


def mlp_shard_kernel(n, side_ref, f1_ref, f2_ref, *rest):
    out_ref = rest[-1]
    rows, ff = f1_ref.shape
    width = f2_ref.shape[1]
    cut = ff // (2 * n)
    for s in range(2):

        @pl.when(side_ref[0] == s)
        def _():
            for src, dst, w in pieces(n, rows, cut, s):
                out_ref[0, :, dst : dst + w] = f1_ref[:, src : src + w]
            for part in range(2):
                lo = s * cut + part * rows
                cols = slice(ff // 2 + part * width, ff // 2 + (part + 1) * width)
                out_ref[0, :, cols] = f2_ref[lo : lo + rows, :]


def mlp_shard(n, side, f1, f2, after=()):
    return pl.pallas_call(
        functools.partial(mlp_shard_kernel, n),
        out_shape=shape((1,) + f1.shape, BF),
        in_specs=[SCALAR, WHOLE, WHOLE] + [HBM] * len(after),
        out_specs=WHOLE,
        compiler_params=params(),
        name="mlp_shard",
    )(side, f1, f2, *after)


def attn_shard(side, w_qkv, w_proj):
    rows, width = w_proj.shape
    return pl.pallas_call(
        attn_shard_kernel,
        out_shape=shape((1, rows, 2 * width), BF),
        in_specs=[SCALAR, WHOLE, WHOLE],
        out_specs=WHOLE,
        compiler_params=params(),
        name="attn_shard",
    )(side, w_qkv, w_proj)


def join_kernel(jobs, chip_ref, *refs):
    outs = refs[-sum(len(cols) for _, cols in jobs) :]
    at = 0
    for k, (bit, cols) in enumerate(jobs):
        v_ref, r_ref = refs[2 * k], refs[2 * k + 1]
        m = v_ref.shape[0]
        up = (chip_ref[0] & bit) // bit
        lo = 0
        for c in cols:
            for i in range(m):
                outs[at][up * m + i] = v_ref[i, :, lo : lo + c]
                outs[at][(1 - up) * m + i] = r_ref[i, :, lo : lo + c]
            lo += c
            at += 1


def join(chip, jobs, after=()):
    flat = [t for v, r, _, _ in jobs for t in (v, r)]
    return pl.pallas_call(
        functools.partial(join_kernel, [(bit, cols) for _, _, bit, cols in jobs]),
        out_shape=tuple(
            shape((2 * v.shape[0], v.shape[1], c), v.dtype) for v, _, _, cols in jobs for c in cols
        ),
        in_specs=[SCALAR] + [WHOLE] * len(flat) + [HBM] * len(after),
        out_specs=(WHOLE,) * sum(len(cols) for _, _, _, cols in jobs),
        compiler_params=params(),
        name="join",
    )(chip, *flat, *after)


def assemble_kernel(orders, chip_ref, *refs):
    out_ref = refs[-1]
    lo = 0
    m = out_ref.shape[0] // 2
    for k, bits in enumerate(orders):
        v_ref, r_ref = refs[2 * k], refs[2 * k + 1]
        c = v_ref.shape[2]
        last = bits[-1]
        up = (chip_ref[0] & last) // last
        lead = bits[:-1][::-1]
        for i in range(m):
            base = sum(b for j, b in enumerate(lead) if (i >> (len(lead) - 1 - j)) & 1)
            out_ref[base + up * last, :, lo : lo + c] = v_ref[i]
            out_ref[base + (1 - up) * last, :, lo : lo + c] = r_ref[i]
        lo += c


def assemble(chip, orders, pairs, after=()):
    flat = [t for pair in pairs for t in pair]
    m, rows = 1 << (len(orders[0]) - 1), flat[0].shape[1]
    cols = sum(v.shape[2] for v, _ in pairs)
    out = pl.pallas_call(
        functools.partial(assemble_kernel, orders),
        out_shape=shape((2 * m, rows, cols), BF),
        in_specs=[SCALAR] + [WHOLE] * len(flat) + [HBM] * len(after),
        out_specs=WHOLE,
        compiler_params=params(),
        name="assemble",
    )(chip, *flat, *after)
    return out.reshape(2 * m * rows, cols)


class Gathering:
    def __init__(self, chip, v, n):
        first, parts = orders_out(n)
        self.chip, self.n = chip, n
        self.orders = [first + part for part in parts]
        self.turn, self.cut_at = 0, len(first)
        self.parts = [v]
        self.exchange()

    def exchange(self):
        self.came = [swap(v, self.orders[k][self.turn], self.n) for k, v in enumerate(self.parts)]
        self.turn += 1

    def step(self, *after):
        jobs = []
        for k, (v, r) in enumerate(zip(self.parts, self.came)):
            c = v.shape[2]
            cut = (c // 3,) * 3 if self.turn == self.cut_at else (c,)
            jobs.append((v, r, self.orders[k][self.turn - 1], cut))
        self.parts = list(join(self.chip, jobs, after))
        self.exchange()
        return tuple(self.parts)

    def done(self):
        return self.turn == len(self.orders[0])

    def result(self, *after):
        return assemble(self.chip, self.orders, tuple(zip(self.parts, self.came)), after=after)


def merge_kernel(bits, mates, chip_ref, *refs):
    small, (v_ref, r_ref), outs = refs[:6], refs[6:8], refs[-3:]
    up = lambda bit: (chip_ref[0] & bit) // bit
    m = small[0].shape[0]
    c = small[0].shape[2]
    far = v_ref.shape[0]
    for k in range(3):
        for ref, side in ((small[2 * k], up(bits[k])), (small[2 * k + 1], 1 - up(bits[k]))):
            for i in range(m):
                outs[k][side * m + i] = ref[i]
    for k in range(3):
        out_ref = outs[mates[k]]
        wide = v_ref.shape[2] // 3
        for ref, side in ((v_ref, up(bits[3])), (r_ref, 1 - up(bits[3]))):
            for h in range(wide // c):
                for i in range(far):
                    lo = k * wide + h * c
                    out_ref[2 * m + h * 2 * far + side * far + i] = ref[i, :, lo : lo + c]


def cross_kernel(bits, skip, chip_ref, *refs):
    outs = refs[-3:]
    for k, bit in enumerate(bits):
        v_ref, r_ref, out_ref = refs[2 * k], refs[2 * k + 1], outs[k]
        up = (chip_ref[0] & bit) // bit
        c = v_ref.shape[2]
        m = out_ref.shape[0] // 2
        for ref, side in ((v_ref, up), (r_ref, 1 - up)):
            for h in range(out_ref.shape[2] // c):
                for i in range(m):
                    out_ref[side * m + i, :, h * c : (h + 1) * c] = ref[skip + h * m + i]


def merge_steps(small, large, *after):
    n, turn = small.n, len(small.orders[0]) - 1
    next_small = [order[turn] for order in small.orders]
    next_large = [order[large.cut_at] for order in large.orders]
    mates = [next_small.index(bit) for bit in next_large]
    bits = [order[turn - 1] for order in small.orders] + [large.orders[0][large.cut_at - 1]]
    v, r = large.parts[0], large.came[0]
    _, rows, c = small.parts[0].shape
    m = 2 * small.parts[0].shape[0]
    far = 2 * v.shape[0]
    wide = v.shape[2] // 3
    flat = [t for pair in zip(small.parts, small.came) for t in pair]
    outs = pl.pallas_call(
        functools.partial(merge_kernel, bits, mates),
        out_shape=(shape((m + far * (wide // c), rows, c), BF),) * 3,
        in_specs=[SCALAR] + [WHOLE] * 8 + [HBM] * len(after),
        out_specs=(WHOLE,) * 3,
        compiler_params=params(),
        name="merge",
    )(small.chip, *flat, v, r, *after)
    came = [swap(t, bit, n) for t, bit in zip(outs, next_small)]

    def small_result(*after):
        return assemble(small.chip, small.orders, tuple(zip(outs, came)), after=after)

    def large_on(*after):
        pairs = [t for k in range(3) for t in (outs[mates[k]], came[mates[k]])]
        parts = pl.pallas_call(
            functools.partial(cross_kernel, next_large, m),
            out_shape=(shape((2 * far, rows, wide), BF),) * 3,
            in_specs=[SCALAR] + [WHOLE] * 6 + [HBM] * len(after),
            out_specs=(WHOLE,) * 3,
            compiler_params=params(),
            name="cross",
        )(large.chip, *pairs, *after)
        large.parts = list(parts)
        large.turn = large.cut_at + 1
        large.exchange()
        return tuple(parts)

    return outs, small_result, large_on


def product_kernel(n, firsts, two_l, two_r, count, chip_ref, l0_ref, l1_ref, *rest):
    r_refs, outs, (turned_ref, buf_ref, sem) = rest[:count], rest[-9:-3], rest[-3:]
    length = l0_ref.shape[0]
    width = turned_ref.shape[1]
    rows = width // n
    tile = width // 3
    for k in range(turned_ref.shape[0]):
        cols = slice(k * width, (k + 1) * width)
        turned_ref[k, :, 0:length] = l0_ref[:, cols].T
        turned_ref[k, :, length:] = l1_ref[:, cols].T

    def times(slot, lo, w):
        total, at = None, 0
        for r_ref in r_refs:
            m = r_ref.shape[0]
            term = mm(turned_ref[slot, :, at : at + m], r_ref[:, lo : lo + w])
            total = term if total is None else total + term
            at += m
        return total

    copies = []
    for t, bit in enumerate(firsts):
        (s0, c0), (s1, c1) = (
            (q // 3 if two_l else 0, (q if two_r else q % 3) * tile) for q in (2 * t, 2 * t + 1)
        )
        if s0 == s1 and c1 == c0 + tile:
            value = times(s0, c0, 2 * tile)
        else:
            value = jnp.concatenate([times(s0, c0, tile), times(s1, c1, tile)], axis=1)
        up = (chip_ref[0] & bit) // bit
        for k in range(n):
            at = (k // (2 * bit)) * bit + k % bit
            goes = 1 - up if k & bit else up
            buf_ref[t, goes, at] = value[k * rows : (k + 1) * rows].astype(BF)
        for goes in range(2):
            copy = pltpu.make_async_copy(buf_ref.at[t, goes], outs[2 * t + goes], sem.at[2 * t + goes])
            copy.start()
            copies.append(copy)
    for copy in copies:
        copy.wait()


def product(chip, l0, l1, r0, r1, width, n, firsts, after=()):
    length = l0.shape[0]
    rights = (r0,) + (r1 if isinstance(r1, tuple) else (r1,))
    two_l, two_r = l0.shape[1] > width, r0.shape[1] > width
    block = (n // 2, width // n, 2 * width // 3)
    out = pl.pallas_call(
        functools.partial(product_kernel, n, firsts, two_l, two_r, len(rights)),
        out_shape=(shape(block, BF),) * 6,
        in_specs=[SCALAR] + [WHOLE] * (2 + len(rights)) + [HBM] * len(after),
        out_specs=(HBM,) * 6,
        scratch_shapes=[
            pltpu.VMEM((1 + two_l, width, 2 * length), BF),
            pltpu.VMEM((3, 2) + block, BF),
            pltpu.SemaphoreType.DMA((6,)),
        ],
        compiler_params=params(),
        cost_estimate=cost(8 * length * width * width, 12e6),
        name="product",
    )(chip, l0, l1, *rights, *after)
    return tuple((out[2 * k], out[2 * k + 1]) for k in range(3))


def split_kernel(jobs, chip_ref, *refs):
    outs = refs[-2 * len(jobs) :]
    at = 0
    for k, (bit, pos, count) in enumerate(jobs):
        keep_ref, send_ref = outs[2 * k], outs[2 * k + 1]
        up = (chip_ref[0] & bit) // bit
        lo = 0
        for _ in range(count):
            v_ref, r_ref = refs[at], refs[at + 1]
            at += 2
            c = v_ref.shape[2]
            for i in range(keep_ref.shape[0]):
                for out_ref, goes in ((send_ref, 1 - up), (keep_ref, up)):
                    j = put(i, pos) + goes * (1 << pos)
                    total = v_ref[j].astype(F32) + r_ref[j].astype(F32)
                    out_ref[i, :, lo : lo + c] = total.astype(BF)
            lo += c


def split(chip, jobs, after=()):
    flat = [t for pairs, _, _ in jobs for pair in pairs for t in pair]
    outs, plan = [], []
    for pairs, bit, left in jobs:
        m, rows, _ = pairs[0][0].shape
        cols = sum(v.shape[2] for v, _ in pairs)
        outs += [shape((m // 2, rows, cols), BF)] * 2
        plan.append((bit, len(left) - 1 - left.index(bit), len(pairs)))
    out = pl.pallas_call(
        functools.partial(split_kernel, plan),
        out_shape=tuple(outs),
        in_specs=[SCALAR] + [WHOLE] * len(flat) + [HBM] * len(after),
        out_specs=(WHOLE,) * len(outs),
        compiler_params=params(),
        name="split",
    )(chip, *flat, *after)
    return [(out[2 * k], out[2 * k + 1]) for k in range(len(jobs))]


def finish_kernel(v_ref, r_ref, *rest):
    rest[-1][...] = v_ref[0].astype(F32) + r_ref[0].astype(F32)


def finish(v, r, after=()):
    return pl.pallas_call(
        finish_kernel,
        out_shape=shape(v.shape[1:], F32),
        in_specs=[WHOLE] * 2 + [HBM] * len(after),
        out_specs=WHOLE,
        compiler_params=params(),
        name="finish",
    )(v, r, *after)


def pack_kernel(side_ref, a_ref, b_ref, c_ref, d_ref, lo_ref, hi_ref, pre_ref, *rest):
    out_ref = rest[-1]
    lanes = out_ref.shape[1]
    per = a_ref.shape[1] // lanes

    def row(at, ref, i, rounded=False):
        for k in range(ref.shape[1] // lanes):
            value = ref[i : i + 1, k * lanes : (k + 1) * lanes]
            out_ref[at + k : at + k + 1, :] = value.astype(BF).astype(F32) if rounded else value

    for k, (ref, i) in enumerate(((c_ref, 0), (c_ref, 1), (b_ref, 3), (a_ref, 1))):
        row(k * per, ref, i)
    many = pre_ref.shape[1] // lanes
    for s in range(2):

        @pl.when(side_ref[0] == s)
        def _():
            for i in range(2):
                row(4 * per + (s ^ i) * many, pre_ref, i)

    at = 4 * per + 2 * many
    for ref in (lo_ref, hi_ref):
        for k in range(ref.shape[1] // lanes):
            out_ref[at : at + HEADS, :] = ref[:, k * lanes : (k + 1) * lanes]
            at += HEADS
    out_ref[at:, :] = jnp.zeros((out_ref.shape[0] - at, lanes), F32)
    parts = ((d_ref, 0), (d_ref, 1), (b_ref, 2), (b_ref, 0), (b_ref, 1), (a_ref, 0))
    for k, (ref, i) in enumerate(parts):
        row(at + k * per, ref, i, True)


def pack(side, arrays, rows, after=()):
    return pl.pallas_call(
        pack_kernel,
        out_shape=shape((rows, 128), F32),
        in_specs=[SCALAR] + [WHOLE] * len(arrays) + [HBM] * len(after),
        out_specs=WHOLE,
        compiler_params=params(),
        name="pack",
    )(side, *arrays, *after)


def meet_kernel(bit, rows, chip_ref, v_ref, r_ref, *rest):
    out_ref = rest[-1]
    out_ref[0:SUM_ROWS, :] = v_ref[0:SUM_ROWS, :] + r_ref[0:SUM_ROWS, :]
    up = (chip_ref[0] & bit) // bit
    for i in range((v_ref.shape[0] - SUM_ROWS) // rows):
        src = slice(SUM_ROWS + i * rows, SUM_ROWS + (i + 1) * rows)
        for ref, side in ((v_ref, up), (r_ref, 1 - up)):
            at = pl.multiple_of(SUM_ROWS + (2 * i + side) * rows, 8)
            out_ref[pl.ds(at, rows), :] = ref[src, :]


def meet(chip, v, r, bit, rows, after=()):
    total = 2 * v.shape[0] - SUM_ROWS
    return pl.pallas_call(
        functools.partial(meet_kernel, bit, rows),
        out_shape=shape((total, v.shape[1]), F32),
        in_specs=[SCALAR, WHOLE, WHOLE] + [HBM] * len(after),
        out_specs=WHOLE,
        compiler_params=params(),
        name="meet",
    )(chip, v, r, *after)


class Reduction:
    def __init__(self, chip, parts, n):
        last, orders = orders_out(n)
        self.chip, self.n = chip, n
        self.orders = [part[::-1] for part in orders]
        self.tail = last[::-1]
        self.left = [all_bits(n)[::-1] for _ in range(3)]
        self.pairs = [
            (keep, self.exchange(k, self.orders[k].pop(0), send)) for k, (keep, send) in enumerate(parts)
        ]

    def exchange(self, k, bit, send):
        self.left[k] = [b for b in self.left[k] if b != bit]
        return swap(send, bit, self.n)

    def plan(self):
        chains = [[k] for k in range(len(self.pairs))]
        if len(self.pairs) > 1 and not self.orders[0]:
            chains = [list(range(len(self.pairs)))]
            self.orders = [list(self.tail)]
        bits = [self.orders[chain[0]].pop(0) for chain in chains]
        return [
            ([self.pairs[j] for j in chain], bit, list(self.left[chain[0]]))
            for chain, bit in zip(chains, bits)
        ]

    def parted(self):
        return len(self.pairs) > 1 and not self.orders[0]

    def take(self, other):
        self.pairs = other.pairs + self.pairs

    def go(self, jobs, outs):
        self.pairs = [
            (keep, self.exchange(k, bit, send))
            for k, ((_, bit, _), (keep, send)) in enumerate(zip(jobs, outs))
        ]

    def done(self):
        return len(self.pairs) == 1 and not self.orders[0]

    def result(self, *after):
        return finish(*self.pairs[0], after)


def step(sums, *after):
    plans = [s.plan() for s in sums]
    outs = split(sums[0].chip, [job for jobs in plans for job in jobs], after)
    kept = tuple(keep for keep, _ in outs)
    for s, jobs in zip(sums, plans):
        s.go(jobs, outs[: len(jobs)])
        outs = outs[len(jobs) :]
    return kept


def fc2_rows_kernel(side_ref, own_ref, other_ref, out_ref):
    rows = own_ref.shape[0]
    width = out_ref.shape[1]
    for s in range(2):

        @pl.when(side_ref[0] == s)
        def _():
            for half, ref in ((s, own_ref), (1 - s, other_ref)):
                for part in range(2):
                    lo = (2 * half + part) * rows
                    out_ref[lo : lo + rows, :] = ref[:, part * width : (part + 1) * width]


def fc2_rows(side, own, other):
    return pl.pallas_call(
        fc2_rows_kernel,
        out_shape=shape((4 * own.shape[0], own.shape[1] // 4), F32),
        in_specs=[SCALAR, WHOLE, WHOLE],
        out_specs=WHOLE,
        compiler_params=params(),
        name="fc2_rows",
    )(side, own, other)


def attn_rows_kernel(side_ref, keep_ref, came_ref, keep_twin_ref, came_twin_ref, *rest):
    qkv_ref, proj_ref = rest[-2:]
    width = proj_ref.shape[1]
    own = keep_ref[0].astype(F32) + came_ref[0].astype(F32)
    other = keep_twin_ref[0].astype(F32) + came_twin_ref[0].astype(F32)
    for s in range(2):

        @pl.when(side_ref[0] == s)
        def _():
            low, high = (own, other) if s == 0 else (other, own)
            qkv_ref[:, 0 : 2 * width] = low
            qkv_ref[:, 2 * width :] = high[:, 0:width]
            proj_ref[...] = high[:, width:]


def attn_rows(side, keep, came, keep_twin, came_twin, after=()):
    _, rows, cols = keep.shape
    width = cols // 2
    return pl.pallas_call(
        attn_rows_kernel,
        out_shape=(shape((rows, 3 * width), F32), shape((rows, width), F32)),
        in_specs=[SCALAR] + [WHOLE] * 4 + [HBM] * len(after),
        out_specs=(WHOLE, WHOLE),
        compiler_params=params(),
        name="attn_rows",
    )(side, keep, came, keep_twin, came_twin, *after)


def hold_kernel(*refs):
    pass


def hold(values, *after):
    many = isinstance(values, tuple)
    values = values if many else (values,)
    out = pl.pallas_call(
        hold_kernel,
        out_shape=tuple(shape(v.shape, v.dtype) for v in values),
        in_specs=[HBM] * (len(values) + len(after)),
        out_specs=(HBM,) * len(values),
        input_output_aliases={k: k for k in range(len(values))},
        name="hold",
    )(*values, *after)
    return out if many else out[0]


def attention_kernel(
    side_ref,
    own_ref,
    other_ref,
    normed_ref,
    bqv_ref,
    strip_ref,
    keep_ref,
    x_ref,
    mod_ref,
    bproj_ref,
    qh_ref,
    kh_ref,
    vh_ref,
    mine_ref,
    theirs_ref,
    attended_ref,
    middle_ref,
    normed_two_ref,
    w_out_ref,
    w_ref,
    flat_ref,
    mix_ref,
    sem,
):
    length, width = x_ref.shape
    hd = width // HEADS
    tile = 384
    wait = fetch_halves(side_ref, own_ref, other_ref, w_ref, sem)
    normed = normed_ref[...]

    def project(slot, lo, cols, at, bias_at):
        def body(o):
            y = mm(normed, w_ref[slot, :, pl.ds(lo + o, tile)])
            if bias_at is not None:
                y = y + bqv_ref[:, pl.ds(bias_at + o, tile)]
            flat_ref[:, pl.ds(at + o, tile)] = y.astype(BF)

        strips(cols, tile, body)

    wait(0)
    project(0, 0, width, 0, 0)
    project(0, width, width, width, None)
    wait(1)
    keep_out = pltpu.make_async_copy(w_ref.at[1, :, pl.ds(width, width)], w_out_ref, sem.at[2])
    keep_out.start()
    project(1, 0, width, 2 * width, width)
    for h in range(HEADS):
        qh_ref[h] = flat_ref[:, h * hd : (h + 1) * hd]
        kh_ref[h] = flat_ref[:, width + h * hd : width + (h + 1) * hd]
        vh_ref[h] = flat_ref[:, 2 * width + h * hd : 2 * width + (h + 1) * hd]
    keep = keep_ref[...] > 0.0

    def head(h, carry):
        sc = mm_nt(qh_ref[h], kh_ref[h]) * (hd**-0.5) + bias_of(strip_ref[h])
        sc = jnp.where(keep, sc, -1e30)
        ex = jnp.exp(sc - jnp.max(sc, axis=-1, keepdims=True))
        soft = ex / jnp.sum(ex, axis=-1, keepdims=True)
        mix_ref[h] = mm(soft.astype(BF), vh_ref[h]).astype(BF)
        return carry

    lax.fori_loop(0, HEADS, head, 0)
    for h in range(HEADS):
        flat_ref[:, h * hd : (h + 1) * hd] = mix_ref[h]
    mixed = flat_ref[:, 0:width]
    mine_ref[:, 0:width] = normed
    theirs_ref[:, 0:width] = normed
    for s, (normed_at, mixed_at) in enumerate(((mine_ref, theirs_ref), (theirs_ref, mine_ref))):

        @pl.when(side_ref[0] == s)
        def _():
            normed_at[:, width:] = normed
            mixed_at[:, width:] = mixed

    def out(o):
        y = mm(mixed, w_ref[1, :, pl.ds(width + o, tile)]) + bproj_ref[:, pl.ds(o, tile)]
        attended_ref[:, pl.ds(o, tile)] = y

    strips(width, tile, out)
    middle = x_ref[...] + mod_ref[2:3, :] * attended_ref[...]
    middle_ref[...] = middle
    n2, _ = normal(middle)
    normed_two_ref[...] = (n2 * (1.0 + mod_ref[4:5, :]) + mod_ref[3:4, :]).astype(BF)
    keep_out.wait()


def attention(side, own, other, normed, b_qv, bias, keep, x, mod, b_proj):
    length, width = x.shape
    hd = width // HEADS
    per_head = shape((HEADS, length, hd), BF)
    return pl.pallas_call(
        attention_kernel,
        out_shape=(
            per_head,
            per_head,
            per_head,
            shape((length, 2 * width), BF),
            shape((length, 2 * width), BF),
            shape((length, width), F32),
            shape((length, width), F32),
            shape((length, width), BF),
            shape((width, width), BF),
        ),
        in_specs=[SCALAR, HBM, HBM] + [WHOLE] * 7,
        out_specs=(WHOLE,) * 8 + (HBM,),
        scratch_shapes=[
            pltpu.VMEM((2, width, 2 * width), BF),
            pltpu.VMEM((length, 3 * width), BF),
            pltpu.VMEM((HEADS, length, hd), BF),
            pltpu.SemaphoreType.DMA((3,)),
        ],
        compiler_params=params(),
        cost_estimate=cost(8 * length * width * width + 4 * length * length * width, 24e6),
        name="attention",
    )(side, own, other, normed, b_qv, bias, keep, x, mod, b_proj)


def fc2_tiles(width, half, tile):
    part = tile // 2
    per = width // part
    at = lambda q: (q % per, half // width + q // per)
    return [pl.BlockSpec((part, width), lambda t, k=k: at(2 * t + k)) for k in range(2)]


def mlp_half(normed_two_ref, b_ref, c0_ref, c1_ref, bf1_ref, hid_ref, slope_ref):
    act, slope = gelu_parts(mm(normed_two_ref[...], b_ref[...]) + bf1_ref[...])
    hid = act.astype(BF)
    hid_ref[...] = hid
    slope_ref[...] = slope
    return mm(hid, jnp.concatenate([c0_ref[...], c1_ref[...]], axis=0))


def mlp_first_kernel(normed_two_ref, b_ref, c0_ref, c1_ref, bf1_ref, hid_ref, slope_ref, part_ref):
    total = mlp_half(normed_two_ref, b_ref, c0_ref, c1_ref, bf1_ref, hid_ref, slope_ref)

    @pl.when(pl.program_id(0) == 0)
    def _():
        part_ref[...] = total

    @pl.when(pl.program_id(0) > 0)
    def _():
        part_ref[...] += total


def mlp_last_kernel(
    normed_two_ref,
    b_ref,
    c0_ref,
    c1_ref,
    bf1_ref,
    part_ref,
    bf2_ref,
    middle_ref,
    cot_ref,
    mod_ref,
    place_ref,
    present_ref,
    hid_ref,
    slope_ref,
    g_branch_ref,
    out_ref,
    sums_ref,
    acc_ref,
):
    t = pl.program_id(0)
    total = mlp_half(normed_two_ref, b_ref, c0_ref, c1_ref, bf1_ref, hid_ref, slope_ref)

    @pl.when(t == 0)
    def _():
        acc_ref[...] = part_ref[...] + total

    @pl.when(t > 0)
    def _():
        acc_ref[...] += total

    @pl.when(t == pl.num_programs(0) - 1)
    def _():
        branch = acc_ref[...] + bf2_ref[...]
        cot = cot_ref[...]
        gate = mod_ref[5:6, :]
        result = middle_ref[...] + gate * branch
        out = jnp.where(present_ref[...] > 0.0, result, 0.0).astype(BF)
        out_ref[...] = mm_tn(place_ref[...], out).astype(BF)
        g_branch = (cot * gate).astype(BF)
        g_branch_ref[...] = g_branch
        sums_ref[0:1, :] = jnp.sum(cot * branch, axis=0, keepdims=True)
        sums_ref[1:2, :] = jnp.sum(g_branch.astype(F32), axis=0, keepdims=True)


def mlp(normed_two, weights, bf1, last=None):
    length, width = normed_two.shape
    half = weights.shape[1] // 2
    tile = 2 * width // 3
    fixed = lambda a: pl.BlockSpec(a.shape, lambda t: (0, 0))
    cols = lambda r: pl.BlockSpec((r, tile), lambda t: (0, t))
    rows = fc2_tiles(width, half, tile)
    whole = lambda r: pl.BlockSpec((r, width), lambda t: (0, 0))
    more = last or ()
    outs = [shape((length, half), BF), shape((length, half), F32)]
    if last:
        outs += [shape((length, width), BF), shape((length, width), BF), shape((8, width), F32)]
    else:
        outs += [shape((length, width), F32)]
    return pl.pallas_call(
        mlp_last_kernel if last else mlp_first_kernel,
        grid=(half // tile,),
        out_shape=tuple(outs),
        in_specs=[fixed(normed_two), cols(width)] + rows + [cols(1)] + [fixed(a) for a in more],
        out_specs=tuple([cols(length), cols(length)] + [whole(o.shape[0]) for o in outs[2:]]),
        scratch_shapes=[pltpu.VMEM((length, width), F32)] if last else [],
        compiler_params=params(),
        cost_estimate=cost(4 * length * width * half, 16e6),
        name="mlp",
    )(normed_two, weights, weights, weights, bf1, *more)


def mlp_back_kernel(
    g_branch_ref,
    b0_ref,
    b1_ref,
    c00_ref,
    c01_ref,
    c10_ref,
    c11_ref,
    slope0_ref,
    slope1_ref,
    middle_ref,
    attended_ref,
    cot_ref,
    mod_ref,
    w_out_ref,
    *rest,
):
    pre0_ref, pre1_ref, bsum_ref, g_middle_ref, g_att_ref, g_mixed_ref, sums_ref, acc_ref = rest[-8:]
    t = pl.program_id(0)
    g_branch = g_branch_ref[...]
    total = None
    for i, (b_ref, c_refs, slope_ref, pre_ref) in enumerate(
        (
            (b0_ref, (c00_ref, c01_ref), slope0_ref, pre0_ref),
            (b1_ref, (c10_ref, c11_ref), slope1_ref, pre1_ref),
        )
    ):
        c = jnp.concatenate([ref[...] for ref in c_refs], axis=0)
        pre = (mm_nt(g_branch, c) * slope_ref[...]).astype(BF)
        pre_ref[...] = pre
        bsum_ref[i : i + 1, :] = jnp.sum(pre.astype(F32), axis=0, keepdims=True)
        part = mm_nt(pre, b_ref[...])
        total = part if total is None else total + part

    @pl.when(t == 0)
    def _():
        acc_ref[...] = total

    @pl.when(t > 0)
    def _():
        acc_ref[...] += total

    @pl.when(t == pl.num_programs(0) - 1)
    def _():
        g_n2 = acc_ref[...]
        n2, inv2 = normal(middle_ref[...])
        sums_ref[0:1, :] = jnp.sum(g_n2, axis=0, keepdims=True)
        sums_ref[1:2, :] = jnp.sum(g_n2 * n2, axis=0, keepdims=True)
        g_middle = cot_ref[...] + normal_back(g_n2 * (1.0 + mod_ref[4:5, :]), n2, inv2)
        g_middle_ref[...] = g_middle
        sums_ref[2:3, :] = jnp.sum(g_middle * attended_ref[...], axis=0, keepdims=True)
        g_att = (g_middle * mod_ref[2:3, :]).astype(BF)
        g_att_ref[...] = g_att
        sums_ref[3:4, :] = jnp.sum(g_att.astype(F32), axis=0, keepdims=True)
        g_mixed_ref[...] = mm_nt(g_att, w_out_ref[...]).astype(BF)


def mlp_back(g_branch, weights, slope0, slope1, middle, attended, cot, mod, w_out, after=()):
    length, width = middle.shape
    half = weights[0].shape[1] // 2
    tile = 2 * width // 3
    fixed = lambda a: pl.BlockSpec(a.shape, lambda t: (0, 0))
    cols = lambda r: pl.BlockSpec((r, tile), lambda t: (0, t))
    rows = fc2_tiles(width, half, tile)
    whole = lambda r: pl.BlockSpec((r, width), lambda t: (0, 0))
    return pl.pallas_call(
        mlp_back_kernel,
        grid=(half // tile,),
        out_shape=(
            shape((length, half), BF),
            shape((length, half), BF),
            shape((2, half), F32),
            shape((length, width), F32),
            shape((length, width), BF),
            shape((length, width), BF),
            shape((8, width), F32),
        ),
        in_specs=[
            fixed(g_branch),
            cols(width),
            cols(width),
            *rows,
            *rows,
            cols(length),
            cols(length),
            fixed(middle),
            fixed(attended),
            fixed(cot),
            fixed(mod),
            fixed(w_out),
        ]
        + [HBM] * len(after),
        out_specs=(
            cols(length),
            cols(length),
            cols(2),
            whole(length),
            whole(length),
            whole(length),
            whole(8),
        ),
        scratch_shapes=[pltpu.VMEM((length, width), F32)],
        compiler_params=params(),
        cost_estimate=cost(8 * length * width * half, 32e6),
        name="mlp_back",
    )(
        g_branch,
        *weights,
        weights[0],
        weights[0],
        weights[1],
        weights[1],
        slope0,
        slope1,
        middle,
        attended,
        cot,
        mod,
        w_out,
        *after,
    )


def heads_back(q_ref, k_ref, v_ref, strip_ref, keep, gm_ref, dq_ref, dk_ref, dv_ref, sums_ref, start):
    scale = q_ref.shape[2] ** -0.5
    length = q_ref.shape[1]

    def head(i, carry):
        h = start + i
        q, k, v, gm = q_ref[h], k_ref[h], v_ref[h], gm_ref[i]
        sc = mm_nt(q, k) * scale + bias_of(strip_ref[h])
        sc = jnp.where(keep, sc, -1e30)
        ex = jnp.exp(sc - jnp.max(sc, axis=-1, keepdims=True))
        soft = ex / jnp.sum(ex, axis=-1, keepdims=True)
        dv_ref[i] = mm_tn(soft.astype(BF), gm).astype(BF)
        dp = mm_nt(gm, v)
        ds = (soft * (dp - jnp.sum(dp * soft, axis=-1, keepdims=True))).astype(BF)
        dq_ref[i] = (mm(ds, k) * scale).astype(BF)
        dk_ref[i] = (mm_tn(ds, q) * scale).astype(BF)
        dsf = ds.astype(F32)
        total = jnp.zeros((GRID, sums_ref.shape[2]), F32)
        blank = jnp.zeros((GRID, sums_ref.shape[2] - length), F32)
        for y in range(GRID):
            rows = jnp.concatenate([dsf[y * GRID : (y + 1) * GRID, :], blank], axis=1)
            by = (GRID - 1 - y) * GRID
            total = total + (pltpu.roll(rows, by, 1) if by else rows)
        sums_ref[i] = total
        return carry

    lax.fori_loop(0, dq_ref.shape[0], head, 0, unroll=2)


def first_heads_kernel(qh_ref, kh_ref, vh_ref, strip_ref, keep_ref, g_mixed_ref, *rest):
    dq_ref, dk_ref, dv_ref, sums_ref, gm_ref = rest[-5:]
    hd = qh_ref.shape[2]
    for i in range(HEADS // 2):
        gm_ref[i] = g_mixed_ref[:, i * hd : (i + 1) * hd]
    heads_back(
        qh_ref, kh_ref, vh_ref, strip_ref, keep_ref[...] > 0.0, gm_ref, dq_ref, dk_ref, dv_ref, sums_ref, 0
    )


def first_heads(qh, kh, vh, strip, keep, g_mixed, after=()):
    heads, length, hd = qh.shape
    some = shape((heads // 2, length, hd), BF)
    return pl.pallas_call(
        first_heads_kernel,
        out_shape=(some, some, some, shape((heads // 2,) + strip.shape[1:], F32)),
        in_specs=[WHOLE] * 6 + [HBM] * len(after),
        out_specs=(WHOLE,) * 4,
        scratch_shapes=[pltpu.VMEM((heads // 2, length, hd), BF)],
        compiler_params=params(),
        cost_estimate=cost(5 * length * length * heads * hd, 16e6),
        name="first_heads",
    )(qh, kh, vh, strip, keep, g_mixed, *after)


def last_heads_kernel(
    side_ref,
    qh_ref,
    kh_ref,
    vh_ref,
    strip_ref,
    keep_ref,
    g_mixed_ref,
    g_att_ref,
    fq_ref,
    fk_ref,
    fv_ref,
    fsum_ref,
    *rest,
):
    mine_ref, top_ref, low_ref, lo_ref, hi_ref, sums_ref, both_ref, gm_ref, dq_ref, dk_ref, dv_ref, strips_ref = rest[-12:]
    theirs_ref = both_ref
    width = g_mixed_ref.shape[1]
    hd = qh_ref.shape[2]
    half = HEADS // 2
    for i in range(half):
        gm_ref[i] = g_mixed_ref[:, (half + i) * hd : (half + i + 1) * hd]
    heads_back(
        qh_ref, kh_ref, vh_ref, strip_ref, keep_ref[...] > 0.0, gm_ref, dq_ref, dk_ref, dv_ref, strips_ref, half
    )
    for s, (qk_at, v_at) in enumerate(((mine_ref, theirs_ref), (theirs_ref, mine_ref))):

        @pl.when(side_ref[0] == s)
        def _():
            for h in range(HEADS):
                q, k, v = (fq_ref, fk_ref, fv_ref) if h < half else (dq_ref, dk_ref, dv_ref)
                i = h % half
                qk_at[:, h * hd : (h + 1) * hd] = q[i]
                qk_at[:, width + h * hd : width + (h + 1) * hd] = k[i]
                v_at[:, h * hd : (h + 1) * hd] = v[i]
            v_at[:, width:] = g_att_ref[...]
            sums_ref[0:1, :] = jnp.sum(qk_at[:, 0:width].astype(F32), axis=0, keepdims=True)
            sums_ref[1:2, :] = jnp.sum(v_at[:, 0:width].astype(F32), axis=0, keepdims=True)

    length = both_ref.shape[0]
    top_ref[...] = both_ref[0 : length // 2, :]
    low_ref[...] = both_ref[length // 2 :, :]
    lanes = lo_ref.shape[1]
    for part, ref in enumerate((fsum_ref, strips_ref)):
        lo = jnp.zeros((half, lanes), F32)
        hi = jnp.zeros((half, lanes), F32)
        j = lax.broadcasted_iota(jnp.int32, lo.shape, 1) % GRID
        for i in range(GRID):
            k = GRID - 1 - i
            row = ref[:, i, :]
            a = jnp.where(j < GRID - k, row, 0.0)
            lo = lo + (pltpu.roll(a, k, 1) if k else a)
            if k:
                hi = hi + pltpu.roll(jnp.where(j < GRID - k, 0.0, row), lanes - (GRID - k), 1)
        lo_ref[part * half : (part + 1) * half, :] = lo
        hi_ref[part * half : (part + 1) * half, :] = hi


def last_heads(side, qh, kh, vh, strip, keep, g_mixed, g_att, firsts, after=()):
    length, width = g_mixed.shape
    heads, _, hd = qh.shape
    per_head = pltpu.VMEM((heads // 2, length, hd), BF)
    window = shape((heads, strip.shape[2]), F32)
    return pl.pallas_call(
        last_heads_kernel,
        out_shape=(
            shape((length, 2 * width), BF),
            shape((length // 2, 2 * width), BF),
            shape((length // 2, 2 * width), BF),
            window,
            window,
            shape((8, width), F32),
        ),
        in_specs=[SCALAR] + [WHOLE] * 11 + [HBM] * len(after),
        out_specs=(WHOLE,) * 6,
        scratch_shapes=[pltpu.VMEM((length, 2 * width), BF)]
        + [per_head] * 4 + [pltpu.VMEM((heads // 2,) + strip.shape[1:], F32)],
        compiler_params=params(),
        cost_estimate=cost(5 * length * length * width, 16e6),
        name="last_heads",
    )(side, qh, kh, vh, strip, keep, g_mixed, g_att, *firsts, *after)


def tokens_back_kernel(
    side_ref,
    own_ref,
    other_ref,
    mine_ref,
    top_ref,
    low_ref,
    x_ref,
    g_middle_ref,
    mod_ref,
    place_ref,
    *rest,
):
    out_ref, sums_ref, w_ref, acc_ref, qk_ref, v_ref, sem = rest[-7:]
    length, width = x_ref.shape
    wait = fetch_halves(side_ref, own_ref, other_ref, w_ref, sem)
    half = length // 2

    @pl.when(side_ref[0] == 0)
    def _():
        qk_ref[...] = mine_ref[...]
        v_ref[0:half, :] = top_ref[:, 0:width]
        v_ref[half:, :] = low_ref[:, 0:width]

    @pl.when(side_ref[0] == 1)
    def _():
        qk_ref[0:half, :] = top_ref[...]
        qk_ref[half:, :] = low_ref[...]
        v_ref[...] = mine_ref[:, 0:width]

    wait(0)
    acc_ref[...] = mm_nt(qk_ref[...], w_ref[0])
    wait(1)
    g_n1 = acc_ref[...] + mm_nt(v_ref[...], w_ref[1, :, 0:width])
    n1, inv1 = normal(x_ref[...])
    sums_ref[0:1, :] = jnp.sum(g_n1, axis=0, keepdims=True)
    sums_ref[1:2, :] = jnp.sum(g_n1 * n1, axis=0, keepdims=True)
    g_x = g_middle_ref[...] + normal_back(g_n1 * (1.0 + mod_ref[1:2, :]), n1, inv1)
    out_ref[...] = mm_tn(place_ref[...], g_x.astype(BF)).astype(BF)


def tokens_back(side, own, other, mine, theirs, x, g_middle, mod, place, after=()):
    length, width = x.shape
    return pl.pallas_call(
        tokens_back_kernel,
        out_shape=(shape((length, width), BF), shape((8, width), F32)),
        in_specs=[SCALAR, HBM, HBM] + [WHOLE] * 7 + [HBM] * len(after),
        out_specs=(WHOLE,) * 2,
        scratch_shapes=[
            pltpu.VMEM((2, width, 2 * width), BF),
            pltpu.VMEM((length, width), F32),
            pltpu.VMEM((length, 2 * width), BF),
            pltpu.VMEM((length, width), BF),
            pltpu.SemaphoreType.DMA((2,)),
        ],
        compiler_params=params(),
        cost_estimate=cost(6 * length * width * width, 16e6),
        name="tokens_back",
    )(side, own, other, mine, *theirs, x, g_middle, mod, place, *after)


def local(
    n,
    tokens,
    condition,
    kept_index,
    kept_count,
    cotangent,
    w_ada,
    w_qkv,
    w_proj,
    w_fc1,
    w_fc2,
    b_ada,
    b_qv,
    b_proj,
    b_fc1,
    b_fc2,
    rel_table,
):
    side = lax.axis_index("stream")
    chip = lax.axis_index("dp")
    length, width = tokens.shape[2], tokens.shape[3]
    ff = w_fc1.shape[1]
    rows = width // n
    cut = ff // (2 * n)
    first = side == 0
    side_word = side.astype(jnp.int32).reshape(1)
    chip_word = chip.astype(jnp.int32).reshape(1)

    order_first, order_parts = orders_out(n)
    firsts = tuple(part[-1] for part in order_parts)

    ordinal = jnp.arange(length, dtype=jnp.int32)
    count = jnp.where(first, length, kept_count[0])
    position = jnp.where(first, ordinal, kept_index[0])
    place = ((position[None, :] == ordinal[:, None]) & (ordinal[None, :] < count)).astype(BF)
    present = jnp.sum(place.astype(F32), axis=1)
    keep = present.reshape(1, length)
    present = present.reshape(length, 1)
    x = mm(place, tokens[0, 0])
    cot = mm(place, cotangent[0, 0])
    bias = bias_strip(rel_table)

    cond = condition[0, 0]
    sig = jax.nn.sigmoid(cond)
    cond_act = (cond * sig).astype(BF)
    shard_a = attn_shard(side_word, w_qkv, w_proj)
    all_a = Gathering(chip_word, shard_a, n)
    acts = trade(hold(jnp.broadcast_to(cond_act[None], (n, width)), shard_a))
    acts_part = lax.dynamic_slice_in_dim(acts, chip * rows, rows, axis=1)
    shard_bc = mlp_shard(n, side_word, w_fc1, w_fc2, after=(shard_a,))
    last = all_a.step(shard_bc, acts_part)
    all_bc = Gathering(chip_word, hold(shard_bc, *last), n)
    for _ in range(len(order_parts[0]) - 2 + len(order_first) - 1):
        last = all_a.step(*last)
    while all_bc.turn < all_bc.cut_at:
        last = all_bc.step(*last)
    acts_twin = swap_stream(acts_part)
    if {p[-1] for p in order_parts} == {p[0] for p in order_parts}:
        last, result_a, on_bc = merge_steps(all_a, all_bc, acts_twin, bias, x, cot)
        mod_part = trade(hold(mm(acts_part, w_ada), *last))
        last = on_bc(mod_part)
    else:
        last = all_a.step(*last, acts_twin, bias, x, cot)
        result_a = all_a.result
        mod_part = trade(hold(mm(acts_part, w_ada), *last))
        last = all_bc.step(mod_part)
    a_own = result_a(*last)
    a_other = swap_stream(a_own)
    last = (a_own,)
    while not all_bc.done():
        last = all_bc.step(*last)
    mod_part = hold(mod_part, *last)
    modulation = jnp.sum(mod_part, axis=0) + b_ada
    mod = modulation.reshape(6, width)
    n1, _ = normal(x)
    normed = (n1 * (1.0 + mod[1]) + mod[0]).astype(BF)
    qh, kh, vh, lhs_mine, lhs_theirs, attended, middle, normed_two, w_out = attention(
        side_word,
        a_own,
        a_other,
        normed,
        b_qv.reshape(1, -1),
        bias,
        keep,
        x,
        mod,
        b_proj.reshape(1, -1),
    )

    bf1 = jnp.transpose(b_fc1.reshape(n, 2, 2, cut // 2), (1, 2, 0, 3)).reshape(2, 1, ff // 2)
    bf1_own, bf1_other = jnp.where(first, bf1[0], bf1[1]), jnp.where(first, bf1[1], bf1[0])
    bf2 = b_fc2.reshape(1, -1)
    bc_own = all_bc.result(normed_two, bf1_own, bf1_other, bf2, present, place)
    bc_other = swap_stream(bc_own)
    lhs_twin = swap_stream(lhs_theirs)
    n2_twin = swap_stream(normed_two)
    hid0, slope0, part = mlp(normed_two, bc_own, bf1_own)
    hid1, slope1, g_branch, out_tokens, sums_a = mlp(
        normed_two,
        bc_other,
        bf1_other,
        (part, bf2, middle, cot, mod, place, present),
    )

    parts_c = product(
        chip_word, hid0, swap_stream(hid1), g_branch, swap_stream(g_branch), width, n, firsts
    )
    sum_c = Reduction(chip_word, parts_c, n)
    pre0, pre1, pre_sum, g_middle, g_att, g_mixed, sums_b = mlp_back(
        g_branch,
        (bc_own, bc_other),
        slope0,
        slope1,
        middle,
        attended,
        cot,
        mod,
        w_out,
        after=(parts_c[0][0], lhs_twin, n2_twin),
    )
    kept = step([sum_c], g_mixed)
    pre_twin = swap_stream(pre1)
    one = first_heads(qh, kh, vh, bias, keep, g_mixed, after=kept + (pre_twin,))
    kept = step([sum_c], one[0])
    while not sum_c.parted():
        kept = step([sum_c], *kept)
    parts_b = product(chip_word, normed_two, n2_twin, pre0, pre_twin, width, n, firsts, after=kept)
    sum_b = Reduction(chip_word, parts_b, n)
    g_mine, top, low, lo, hi, sums_c = last_heads(
        side_word, qh, kh, vh, bias, keep, g_mixed, g_att, one, after=(parts_b[0][0],)
    )
    g_theirs = (top, low)
    g_twin = (swap_stream(top), swap_stream(low))
    kept = step([sum_b], g_mine) + g_twin
    grad_tokens, sums_d = tokens_back(
        side_word, a_own, a_other, g_mine, g_theirs, x, g_middle, mod, place, after=kept
    )

    kept = (sums_d,)
    while not sum_b.parted():
        kept = step([sum_b], *kept)
    mod_rows = 6 * width // 128
    group = -(-mod_rows // 8) * 8
    told = pack(
        side_word, (sums_a, sums_b, sums_c, sums_d, lo, hi, pre_sum), SUM_ROWS + group, after=kept
    )
    bits = all_bits(n)[::-1]
    came = swap(told, bits[0], n)
    sum_b.take(sum_c)
    kept = (told,)
    while not sum_b.done():
        kept = step([sum_b], *kept)
    told = meet(chip_word, told, came, bits[0], group, after=kept)
    told = meet(chip_word, told, swap(told, bits[1], n), bits[1], group)
    came = swap(told, bits[2], n)
    parts_a = product(
        chip_word, lhs_mine, lhs_twin, g_mine, g_twin, width, n, firsts, after=(told,) + kept
    )
    told = meet(chip_word, told, came, bits[2], group, after=(parts_a[0][0],))
    sum_a = Reduction(chip_word, parts_a, n)
    for b in bits[3:]:
        told = meet(chip_word, told, swap(told, b, n), b, group)
    d_cb = sum_b.result()
    kept = step([sum_a], told, d_cb)
    d_cb_twin = swap_stream(d_cb)
    grad_w_fc2 = fc2_rows(side_word, d_cb, d_cb_twin)
    grad_w_fc1 = fc1_rows(n, side_word, d_cb, d_cb_twin)
    kept = step([sum_a], told, grad_w_fc2)
    twin = swap_stream(told)

    def mods_of(t):
        return t[SUM_ROWS:].reshape(n, -1, 128)[:, :mod_rows].reshape(n, -1)

    g_own, g_twin = mods_of(told), mods_of(twin)
    grad_w_ada = mm_tn(acts_part, g_own.astype(BF)) + mm_tn(acts_twin, g_twin.astype(BF))
    grad_b_ada = jnp.sum(g_own, axis=0) + jnp.sum(g_twin, axis=0)
    kept = step([sum_a], *kept, grad_w_ada, grad_b_ada)
    while not sum_a.done():
        kept = step([sum_a], *kept)
    g_acts = trade(hold(mm_nt(g_own.astype(BF), w_ada), *kept)).reshape(width)
    grad_condition = g_acts * sig * (1.0 + cond * (1.0 - sig))
    sums = told[:SUM_ROWS] + twin[:SUM_ROWS]
    per = width // 128
    at = 4 * per + ff // 128
    grad_b_fc1 = jnp.transpose(sums[4 * per : at].reshape(2, 2, n, cut // 2), (2, 0, 1, 3)).reshape(-1)
    windows = jnp.transpose(sums[at:].reshape(2, -1, HEADS, 128), (0, 2, 1, 3)).reshape(2, HEADS, -1)
    parts = (
        sums[: 2 * per].reshape(-1),
        sums[2 * per : 3 * per].reshape(-1),
        grad_b_fc1,
        sums[3 * per : 4 * per].reshape(-1),
        table_of(windows[0], windows[1]),
    )
    keep_a, came_a = sum_a.pairs[0]
    grad_w_qkv, grad_w_proj = attn_rows(
        side_word,
        keep_a,
        came_a,
        swap_stream(keep_a),
        swap_stream(came_a),
        after=(g_acts, grad_w_fc1) + parts,
    )
    return (
        out_tokens[None, None],
        grad_tokens[None, None],
        grad_condition[None, None],
        grad_w_ada,
        grad_w_qkv,
        grad_w_proj,
        grad_w_fc1,
        grad_w_fc2,
        grad_b_ada,
        *parts,
    )


def solution(mesh):
    n = mesh.shape["dp"]

    def body(*args):
        return local(n, *args)

    return jax.shard_map(
        body,
        mesh=mesh,
        in_specs=(
            P("stream", "dp", None, None),
            P("stream", "dp", None),
            P("dp", None),
            P("dp"),
            P("stream", "dp", None, None),
            P("dp", None),
            P("dp", None),
            P("dp", None),
            P("dp", None),
            P("dp", None),
            P(),
            P(),
            P(),
            P(),
            P(),
            P(),
        ),
        out_specs=(
            P("stream", "dp", None, None),
            P("stream", "dp", None, None),
            P("stream", "dp", None),
            P("dp", None),
            P("dp", None),
            P("dp", None),
            P("dp", None),
            P("dp", None),
            P(),
            P(),
            P(),
            P(),
            P(),
            P(),
        ),
        check_vma=False,
    )
```

```python
import functools
import math

import jax
import jax.numpy as jnp
from jax import lax
from jax.experimental import pallas as pl
from jax.experimental.pallas import tpu as pltpu
from jax.sharding import PartitionSpec as P

HEADS = 16
GRID = 16
BF = jnp.bfloat16
F32 = jnp.float32


def swap(v, bit, n):
    return lax.ppermute(v, "dp", [(i, i ^ bit) for i in range(n)])


def swap_stream(v):
    return lax.ppermute(v, "stream", [(0, 1), (1, 0)])


def axis_bits(n):
    k = n.bit_length() - 1
    s = k // 3
    xs = [1 << i for i in range(s)]
    ys = [1 << (s + i) for i in range(s)]
    zs = [1 << i for i in range(2 * s, k)]
    return xs, ys, zs


def all_bits(n):
    return [1 << i for i in range(n.bit_length() - 1)]


def orders_out(n):
    xs, ys, zs = axis_bits(n)
    near = zs[:1]
    return zs[1:][::-1], (near + ys + xs, xs + near + ys, ys + xs + near)


def trade(v):
    return lax.all_to_all(v, "dp", 0, 0, tiled=True)


def mm(a, b):
    return lax.dot_general(a, b, (((1,), (0,)), ((), ())), preferred_element_type=F32)


def mm_nt(a, b):
    return lax.dot_general(a, b, (((1,), (1,)), ((), ())), preferred_element_type=F32)


def mm_tn(a, b):
    return lax.dot_general(a, b, (((0,), (0,)), ((), ())), preferred_element_type=F32)


def normal(v):
    center = v - jnp.mean(v, axis=-1, keepdims=True)
    inv = lax.rsqrt(jnp.mean(center * center, axis=-1, keepdims=True) + 1e-06)
    return center * inv, inv


def normal_back(g, n, inv):
    return inv * (g - jnp.mean(g, axis=-1, keepdims=True) - n * jnp.mean(g * n, axis=-1, keepdims=True))


def bias_windows(table):
    w = 2 * GRID - 1
    t = jnp.transpose(table.reshape(w, w, HEADS)[::-1, ::-1], (2, 0, 1))
    t = jnp.pad(t, ((0, 0), (0, 1), (0, 1))).reshape(HEADS, w + 1, 2, GRID)
    return t[:, :, 0].reshape(HEADS, -1), t[:, :, 1].reshape(HEADS, -1)


def table_of(lo, hi):
    w = 2 * GRID - 1
    t = jnp.stack([lo.reshape(HEADS, w + 1, GRID), hi.reshape(HEADS, w + 1, GRID)], axis=2)
    t = t.reshape(HEADS, w + 1, 2 * GRID)[:, :w, :w]
    return jnp.transpose(t, (1, 2, 0))[::-1, ::-1].reshape(w * w, HEADS)


def gelu_parts(x):
    k = math.sqrt(2.0 / math.pi)
    th = jnp.tanh(k * (x + 0.044715 * x * x * x))
    value = 0.5 * x * (1.0 + th)
    slope = 0.5 * (1.0 + th) + 0.5 * x * (1.0 - th * th) * k * (1.0 + 3 * 0.044715 * x * x)
    return value, slope


VMEM_BYTES = 56 * 1024 * 1024
SUM_ROWS = 200
WHOLE = pl.BlockSpec(memory_space=pltpu.VMEM)
HBM = pl.BlockSpec(memory_space=pl.ANY)
SCALAR = pl.BlockSpec(memory_space=pltpu.SMEM)


def shape(dims, dtype):
    return jax.ShapeDtypeStruct(dims, dtype)


def params():
    return pltpu.CompilerParams(vmem_limit_bytes=VMEM_BYTES)


def cost(flops, size):
    return pl.CostEstimate(flops=int(flops), bytes_accessed=int(size), transcendentals=0)


def strips(total, tile, body):
    def step(i, carry):
        body(pl.multiple_of(i * tile, tile))
        return carry

    lax.fori_loop(0, total // tile, step, 0)


def fetch_halves(side_ref, own_ref, other_ref, w_ref, sem):
    side = side_ref[0]
    mine = pltpu.make_async_copy(own_ref, w_ref.at[side], sem.at[side])
    twin = pltpu.make_async_copy(other_ref, w_ref.at[1 - side], sem.at[1 - side])
    mine.start()
    twin.start()

    def wait(slot):
        pltpu.make_async_copy(own_ref, w_ref.at[slot], sem.at[slot]).wait()

    return wait


def pieces(n, rows, cut, s):
    half = cut // 2
    for part in range(2):
        for k in range(n):
            yield (k * 2 + s) * cut + part * half, (part * n + k) * half, half


def fc1_rows_kernel(n, side_ref, own_ref, other_ref, out_ref):
    rows, ff = out_ref.shape
    cut = ff // (2 * n)
    for s in range(2):

        @pl.when(side_ref[0] == s)
        def _():
            for half, ref in ((s, own_ref), (1 - s, other_ref)):
                for src, dst, w in pieces(n, rows, cut, half):
                    out_ref[:, src : src + w] = ref[:, ff // 2 + dst : ff // 2 + dst + w]


def fc1_rows(n, side, own, other):
    return pl.pallas_call(
        functools.partial(fc1_rows_kernel, n),
        out_shape=shape(own.shape, F32),
        in_specs=[SCALAR, WHOLE, WHOLE],
        out_specs=WHOLE,
        compiler_params=params(),
        name="fc1_rows",
    )(side, own, other)


def strip_kernel(lo_ref, hi_ref, out_ref):
    lanes = lo_ref.shape[1]
    lo, hi = lo_ref[...], hi_ref[...]
    j = lax.broadcasted_iota(jnp.int32, lo.shape, 1) % GRID
    for i in range(GRID):
        k = GRID - 1 - i
        a = pltpu.roll(lo, lanes - k, 1) if k else lo
        out_ref[:, i, :] = jnp.where(j < GRID - k, a, pltpu.roll(hi, GRID - k, 1))


def bias_strip(table):
    lo, hi = bias_windows(table)
    return pl.pallas_call(
        strip_kernel,
        out_shape=shape((HEADS, GRID, lo.shape[1]), F32),
        in_specs=[WHOLE, WHOLE],
        out_specs=WHOLE,
        name="bias_strip",
    )(lo, hi)


def bias_of(strip):
    return jnp.concatenate(
        [strip[:, (GRID - 1 - y) * GRID : (2 * GRID - 1 - y) * GRID] for y in range(GRID)], axis=0
    )


def put(i, pos):
    return (i >> pos) << (pos + 1) | (i & ((1 << pos) - 1))


def attn_shard_kernel(side_ref, qkv_ref, proj_ref, out_ref):
    width = proj_ref.shape[1]
    for s in range(2):

        @pl.when(side_ref[0] == s)
        def _():
            if s == 0:
                out_ref[0] = qkv_ref[:, 0 : 2 * width]
            else:
                out_ref[0, :, 0:width] = qkv_ref[:, 2 * width :]
                out_ref[0, :, width:] = proj_ref[...]


def mlp_shard_kernel(n, side_ref, f1_ref, f2_ref, *rest):
    out_ref = rest[-1]
    rows, ff = f1_ref.shape
    width = f2_ref.shape[1]
    cut = ff // (2 * n)
    for s in range(2):

        @pl.when(side_ref[0] == s)
        def _():
            for src, dst, w in pieces(n, rows, cut, s):
                out_ref[0, :, dst : dst + w] = f1_ref[:, src : src + w]
            for part in range(2):
                lo = s * cut + part * rows
                cols = slice(ff // 2 + part * width, ff // 2 + (part + 1) * width)
                out_ref[0, :, cols] = f2_ref[lo : lo + rows, :]


def mlp_shard(n, side, f1, f2, after=()):
    return pl.pallas_call(
        functools.partial(mlp_shard_kernel, n),
        out_shape=shape((1,) + f1.shape, BF),
        in_specs=[SCALAR, WHOLE, WHOLE] + [HBM] * len(after),
        out_specs=WHOLE,
        compiler_params=params(),
        name="mlp_shard",
    )(side, f1, f2, *after)


def attn_shard(side, w_qkv, w_proj):
    rows, width = w_proj.shape
    return pl.pallas_call(
        attn_shard_kernel,
        out_shape=shape((1, rows, 2 * width), BF),
        in_specs=[SCALAR, WHOLE, WHOLE],
        out_specs=WHOLE,
        compiler_params=params(),
        name="attn_shard",
    )(side, w_qkv, w_proj)


def join_kernel(jobs, chip_ref, *refs):
    outs = refs[-sum(len(cols) for _, cols in jobs) :]
    at = 0
    for k, (bit, cols) in enumerate(jobs):
        v_ref, r_ref = refs[2 * k], refs[2 * k + 1]
        m = v_ref.shape[0]
        up = (chip_ref[0] & bit) // bit
        lo = 0
        for c in cols:
            for i in range(m):
                outs[at][up * m + i] = v_ref[i, :, lo : lo + c]
                outs[at][(1 - up) * m + i] = r_ref[i, :, lo : lo + c]
            lo += c
            at += 1


def join(chip, jobs, after=()):
    flat = [t for v, r, _, _ in jobs for t in (v, r)]
    return pl.pallas_call(
        functools.partial(join_kernel, [(bit, cols) for _, _, bit, cols in jobs]),
        out_shape=tuple(
            shape((2 * v.shape[0], v.shape[1], c), v.dtype) for v, _, _, cols in jobs for c in cols
        ),
        in_specs=[SCALAR] + [WHOLE] * len(flat) + [HBM] * len(after),
        out_specs=(WHOLE,) * sum(len(cols) for _, _, _, cols in jobs),
        compiler_params=params(),
        name="join",
    )(chip, *flat, *after)


def assemble_kernel(orders, chip_ref, *refs):
    out_ref = refs[-1]
    lo = 0
    m = out_ref.shape[0] // 2
    for k, bits in enumerate(orders):
        v_ref, r_ref = refs[2 * k], refs[2 * k + 1]
        c = v_ref.shape[2]
        last = bits[-1]
        up = (chip_ref[0] & last) // last
        lead = bits[:-1][::-1]
        for i in range(m):
            base = sum(b for j, b in enumerate(lead) if (i >> (len(lead) - 1 - j)) & 1)
            out_ref[base + up * last, :, lo : lo + c] = v_ref[i]
            out_ref[base + (1 - up) * last, :, lo : lo + c] = r_ref[i]
        lo += c


def assemble(chip, orders, pairs, after=()):
    flat = [t for pair in pairs for t in pair]
    m, rows = 1 << (len(orders[0]) - 1), flat[0].shape[1]
    cols = sum(v.shape[2] for v, _ in pairs)
    out = pl.pallas_call(
        functools.partial(assemble_kernel, orders),
        out_shape=shape((2 * m, rows, cols), BF),
        in_specs=[SCALAR] + [WHOLE] * len(flat) + [HBM] * len(after),
        out_specs=WHOLE,
        compiler_params=params(),
        name="assemble",
    )(chip, *flat, *after)
    return out.reshape(2 * m * rows, cols)


class Gathering:
    def __init__(self, chip, v, n):
        first, parts = orders_out(n)
        self.chip, self.n = chip, n
        self.orders = [first + part for part in parts]
        self.turn, self.cut_at = 0, len(first)
        self.parts = [v]
        self.exchange()

    def exchange(self):
        self.came = [swap(v, self.orders[k][self.turn], self.n) for k, v in enumerate(self.parts)]
        self.turn += 1

    def step(self, *after):
        jobs = []
        for k, (v, r) in enumerate(zip(self.parts, self.came)):
            c = v.shape[2]
            cut = (c // 3,) * 3 if self.turn == self.cut_at else (c,)
            jobs.append((v, r, self.orders[k][self.turn - 1], cut))
        self.parts = list(join(self.chip, jobs, after))
        self.exchange()
        return tuple(self.parts)

    def done(self):
        return self.turn == len(self.orders[0])

    def result(self, *after):
        return assemble(self.chip, self.orders, tuple(zip(self.parts, self.came)), after=after)


def merge_kernel(bits, mates, chip_ref, *refs):
    small, (v_ref, r_ref), outs = refs[:6], refs[6:8], refs[-3:]
    up = lambda bit: (chip_ref[0] & bit) // bit
    m = small[0].shape[0]
    c = small[0].shape[2]
    far = v_ref.shape[0]
    for k in range(3):
        for ref, side in ((small[2 * k], up(bits[k])), (small[2 * k + 1], 1 - up(bits[k]))):
            for i in range(m):
                outs[k][side * m + i] = ref[i]
    for k in range(3):
        out_ref = outs[mates[k]]
        wide = v_ref.shape[2] // 3
        for ref, side in ((v_ref, up(bits[3])), (r_ref, 1 - up(bits[3]))):
            for h in range(wide // c):
                for i in range(far):
                    lo = k * wide + h * c
                    out_ref[2 * m + h * 2 * far + side * far + i] = ref[i, :, lo : lo + c]


def cross_kernel(bits, skip, chip_ref, *refs):
    outs = refs[-3:]
    for k, bit in enumerate(bits):
        v_ref, r_ref, out_ref = refs[2 * k], refs[2 * k + 1], outs[k]
        up = (chip_ref[0] & bit) // bit
        c = v_ref.shape[2]
        m = out_ref.shape[0] // 2
        for ref, side in ((v_ref, up), (r_ref, 1 - up)):
            for h in range(out_ref.shape[2] // c):
                for i in range(m):
                    out_ref[side * m + i, :, h * c : (h + 1) * c] = ref[skip + h * m + i]


def merge_steps(small, large, *after):
    n, turn = small.n, len(small.orders[0]) - 1
    next_small = [order[turn] for order in small.orders]
    next_large = [order[large.cut_at] for order in large.orders]
    mates = [next_small.index(bit) for bit in next_large]
    bits = [order[turn - 1] for order in small.orders] + [large.orders[0][large.cut_at - 1]]
    v, r = large.parts[0], large.came[0]
    _, rows, c = small.parts[0].shape
    m = 2 * small.parts[0].shape[0]
    far = 2 * v.shape[0]
    wide = v.shape[2] // 3
    flat = [t for pair in zip(small.parts, small.came) for t in pair]
    outs = pl.pallas_call(
        functools.partial(merge_kernel, bits, mates),
        out_shape=(shape((m + far * (wide // c), rows, c), BF),) * 3,
        in_specs=[SCALAR] + [WHOLE] * 8 + [HBM] * len(after),
        out_specs=(WHOLE,) * 3,
        compiler_params=params(),
        name="merge",
    )(small.chip, *flat, v, r, *after)
    came = [swap(t, bit, n) for t, bit in zip(outs, next_small)]

    def small_result(*after):
        return assemble(small.chip, small.orders, tuple(zip(outs, came)), after=after)

    def large_on(*after):
        pairs = [t for k in range(3) for t in (outs[mates[k]], came[mates[k]])]
        parts = pl.pallas_call(
            functools.partial(cross_kernel, next_large, m),
            out_shape=(shape((2 * far, rows, wide), BF),) * 3,
            in_specs=[SCALAR] + [WHOLE] * 6 + [HBM] * len(after),
            out_specs=(WHOLE,) * 3,
            compiler_params=params(),
            name="cross",
        )(large.chip, *pairs, *after)
        large.parts = list(parts)
        large.turn = large.cut_at + 1
        large.exchange()
        return tuple(parts)

    return outs, small_result, large_on


def product_kernel(n, firsts, two_l, two_r, count, chip_ref, l0_ref, l1_ref, *rest):
    r_refs, outs, (turned_ref, buf_ref, sem) = rest[:count], rest[-9:-3], rest[-3:]
    length = l0_ref.shape[0]
    width = turned_ref.shape[1]
    rows = width // n
    tile = width // 3
    for k in range(turned_ref.shape[0]):
        cols = slice(k * width, (k + 1) * width)
        turned_ref[k, :, 0:length] = l0_ref[:, cols].T
        turned_ref[k, :, length:] = l1_ref[:, cols].T

    def times(slot, lo, w):
        total, at = None, 0
        for r_ref in r_refs:
            m = r_ref.shape[0]
            term = mm(turned_ref[slot, :, at : at + m], r_ref[:, lo : lo + w])
            total = term if total is None else total + term
            at += m
        return total

    copies = []
    for t, bit in enumerate(firsts):
        (s0, c0), (s1, c1) = (
            (q // 3 if two_l else 0, (q if two_r else q % 3) * tile) for q in (2 * t, 2 * t + 1)
        )
        if s0 == s1 and c1 == c0 + tile:
            value = times(s0, c0, 2 * tile)
        else:
            value = jnp.concatenate([times(s0, c0, tile), times(s1, c1, tile)], axis=1)
        up = (chip_ref[0] & bit) // bit
        for k in range(n):
            at = (k // (2 * bit)) * bit + k % bit
            goes = 1 - up if k & bit else up
            buf_ref[t, goes, at] = value[k * rows : (k + 1) * rows].astype(BF)
        for goes in range(2):
            copy = pltpu.make_async_copy(buf_ref.at[t, goes], outs[2 * t + goes], sem.at[2 * t + goes])
            copy.start()
            copies.append(copy)
    for copy in copies:
        copy.wait()


def product(chip, l0, l1, r0, r1, width, n, firsts, after=()):
    length = l0.shape[0]
    rights = (r0,) + (r1 if isinstance(r1, tuple) else (r1,))
    two_l, two_r = l0.shape[1] > width, r0.shape[1] > width
    block = (n // 2, width // n, 2 * width // 3)
    out = pl.pallas_call(
        functools.partial(product_kernel, n, firsts, two_l, two_r, len(rights)),
        out_shape=(shape(block, BF),) * 6,
        in_specs=[SCALAR] + [WHOLE] * (2 + len(rights)) + [HBM] * len(after),
        out_specs=(HBM,) * 6,
        scratch_shapes=[
            pltpu.VMEM((1 + two_l, width, 2 * length), BF),
            pltpu.VMEM((3, 2) + block, BF),
            pltpu.SemaphoreType.DMA((6,)),
        ],
        compiler_params=params(),
        cost_estimate=cost(8 * length * width * width, 12e6),
        name="product",
    )(chip, l0, l1, *rights, *after)
    return tuple((out[2 * k], out[2 * k + 1]) for k in range(3))


def split_kernel(jobs, chip_ref, *refs):
    outs = refs[-2 * len(jobs) :]
    at = 0
    for k, (bit, pos, count) in enumerate(jobs):
        keep_ref, send_ref = outs[2 * k], outs[2 * k + 1]
        up = (chip_ref[0] & bit) // bit
        lo = 0
        for _ in range(count):
            v_ref, r_ref = refs[at], refs[at + 1]
            at += 2
            c = v_ref.shape[2]
            for i in range(keep_ref.shape[0]):
                for out_ref, goes in ((send_ref, 1 - up), (keep_ref, up)):
                    j = put(i, pos) + goes * (1 << pos)
                    total = v_ref[j].astype(F32) + r_ref[j].astype(F32)
                    out_ref[i, :, lo : lo + c] = total.astype(BF)
            lo += c


def split(chip, jobs, after=()):
    flat = [t for pairs, _, _ in jobs for pair in pairs for t in pair]
    outs, plan = [], []
    for pairs, bit, left in jobs:
        m, rows, _ = pairs[0][0].shape
        cols = sum(v.shape[2] for v, _ in pairs)
        outs += [shape((m // 2, rows, cols), BF)] * 2
        plan.append((bit, len(left) - 1 - left.index(bit), len(pairs)))
    out = pl.pallas_call(
        functools.partial(split_kernel, plan),
        out_shape=tuple(outs),
        in_specs=[SCALAR] + [WHOLE] * len(flat) + [HBM] * len(after),
        out_specs=(WHOLE,) * len(outs),
        compiler_params=params(),
        name="split",
    )(chip, *flat, *after)
    return [(out[2 * k], out[2 * k + 1]) for k in range(len(jobs))]


def finish_kernel(v_ref, r_ref, *rest):
    rest[-1][...] = v_ref[0].astype(F32) + r_ref[0].astype(F32)


def finish(v, r, after=()):
    return pl.pallas_call(
        finish_kernel,
        out_shape=shape(v.shape[1:], F32),
        in_specs=[WHOLE] * 2 + [HBM] * len(after),
        out_specs=WHOLE,
        compiler_params=params(),
        name="finish",
    )(v, r, *after)


def pack_kernel(side_ref, a_ref, b_ref, c_ref, d_ref, lo_ref, hi_ref, pre_ref, *rest):
    out_ref = rest[-1]
    lanes = out_ref.shape[1]
    per = a_ref.shape[1] // lanes

    def row(at, ref, i, rounded=False):
        for k in range(ref.shape[1] // lanes):
            value = ref[i : i + 1, k * lanes : (k + 1) * lanes]
            out_ref[at + k : at + k + 1, :] = value.astype(BF).astype(F32) if rounded else value

    for k, (ref, i) in enumerate(((c_ref, 0), (c_ref, 1), (b_ref, 3), (a_ref, 1))):
        row(k * per, ref, i)
    many = pre_ref.shape[1] // lanes
    for s in range(2):

        @pl.when(side_ref[0] == s)
        def _():
            for i in range(2):
                row(4 * per + (s ^ i) * many, pre_ref, i)

    at = 4 * per + 2 * many
    for ref in (lo_ref, hi_ref):
        for k in range(ref.shape[1] // lanes):
            out_ref[at : at + HEADS, :] = ref[:, k * lanes : (k + 1) * lanes]
            at += HEADS
    out_ref[at:, :] = jnp.zeros((out_ref.shape[0] - at, lanes), F32)
    parts = ((d_ref, 0), (d_ref, 1), (b_ref, 2), (b_ref, 0), (b_ref, 1), (a_ref, 0))
    for k, (ref, i) in enumerate(parts):
        row(at + k * per, ref, i, True)


def pack(side, arrays, rows, after=()):
    return pl.pallas_call(
        pack_kernel,
        out_shape=shape((rows, 128), F32),
        in_specs=[SCALAR] + [WHOLE] * len(arrays) + [HBM] * len(after),
        out_specs=WHOLE,
        compiler_params=params(),
        name="pack",
    )(side, *arrays, *after)


def meet_kernel(bit, rows, chip_ref, v_ref, r_ref, *rest):
    out_ref = rest[-1]
    out_ref[0:SUM_ROWS, :] = v_ref[0:SUM_ROWS, :] + r_ref[0:SUM_ROWS, :]
    up = (chip_ref[0] & bit) // bit
    for i in range((v_ref.shape[0] - SUM_ROWS) // rows):
        src = slice(SUM_ROWS + i * rows, SUM_ROWS + (i + 1) * rows)
        for ref, side in ((v_ref, up), (r_ref, 1 - up)):
            at = pl.multiple_of(SUM_ROWS + (2 * i + side) * rows, 8)
            out_ref[pl.ds(at, rows), :] = ref[src, :]


def meet(chip, v, r, bit, rows, after=()):
    total = 2 * v.shape[0] - SUM_ROWS
    return pl.pallas_call(
        functools.partial(meet_kernel, bit, rows),
        out_shape=shape((total, v.shape[1]), F32),
        in_specs=[SCALAR, WHOLE, WHOLE] + [HBM] * len(after),
        out_specs=WHOLE,
        compiler_params=params(),
        name="meet",
    )(chip, v, r, *after)


class Reduction:
    def __init__(self, chip, parts, n):
        last, orders = orders_out(n)
        self.chip, self.n = chip, n
        self.orders = [part[::-1] for part in orders]
        self.tail = last[::-1]
        self.left = [all_bits(n)[::-1] for _ in range(3)]
        self.pairs = [
            (keep, self.exchange(k, self.orders[k].pop(0), send)) for k, (keep, send) in enumerate(parts)
        ]

    def exchange(self, k, bit, send):
        self.left[k] = [b for b in self.left[k] if b != bit]
        return swap(send, bit, self.n)

    def plan(self):
        chains = [[k] for k in range(len(self.pairs))]
        if len(self.pairs) > 1 and not self.orders[0]:
            chains = [list(range(len(self.pairs)))]
            self.orders = [list(self.tail)]
        bits = [self.orders[chain[0]].pop(0) for chain in chains]
        return [
            ([self.pairs[j] for j in chain], bit, list(self.left[chain[0]]))
            for chain, bit in zip(chains, bits)
        ]

    def parted(self):
        return len(self.pairs) > 1 and not self.orders[0]

    def take(self, other):
        self.pairs = other.pairs + self.pairs

    def go(self, jobs, outs):
        self.pairs = [
            (keep, self.exchange(k, bit, send))
            for k, ((_, bit, _), (keep, send)) in enumerate(zip(jobs, outs))
        ]

    def done(self):
        return len(self.pairs) == 1 and not self.orders[0]

    def result(self, *after):
        return finish(*self.pairs[0], after)


def step(sums, *after):
    plans = [s.plan() for s in sums]
    outs = split(sums[0].chip, [job for jobs in plans for job in jobs], after)
    kept = tuple(keep for keep, _ in outs)
    for s, jobs in zip(sums, plans):
        s.go(jobs, outs[: len(jobs)])
        outs = outs[len(jobs) :]
    return kept


def fc2_rows_kernel(side_ref, own_ref, other_ref, out_ref):
    rows = own_ref.shape[0]
    width = out_ref.shape[1]
    for s in range(2):

        @pl.when(side_ref[0] == s)
        def _():
            for half, ref in ((s, own_ref), (1 - s, other_ref)):
                for part in range(2):
                    lo = (2 * half + part) * rows
                    out_ref[lo : lo + rows, :] = ref[:, part * width : (part + 1) * width]


def fc2_rows(side, own, other):
    return pl.pallas_call(
        fc2_rows_kernel,
        out_shape=shape((4 * own.shape[0], own.shape[1] // 4), F32),
        in_specs=[SCALAR, WHOLE, WHOLE],
        out_specs=WHOLE,
        compiler_params=params(),
        name="fc2_rows",
    )(side, own, other)


def attn_rows_kernel(side_ref, keep_ref, came_ref, keep_twin_ref, came_twin_ref, *rest):
    qkv_ref, proj_ref = rest[-2:]
    width = proj_ref.shape[1]
    own = keep_ref[0].astype(F32) + came_ref[0].astype(F32)
    other = keep_twin_ref[0].astype(F32) + came_twin_ref[0].astype(F32)
    for s in range(2):

        @pl.when(side_ref[0] == s)
        def _():
            low, high = (own, other) if s == 0 else (other, own)
            qkv_ref[:, 0 : 2 * width] = low
            qkv_ref[:, 2 * width :] = high[:, 0:width]
            proj_ref[...] = high[:, width:]


def attn_rows(side, keep, came, keep_twin, came_twin, after=()):
    _, rows, cols = keep.shape
    width = cols // 2
    return pl.pallas_call(
        attn_rows_kernel,
        out_shape=(shape((rows, 3 * width), F32), shape((rows, width), F32)),
        in_specs=[SCALAR] + [WHOLE] * 4 + [HBM] * len(after),
        out_specs=(WHOLE, WHOLE),
        compiler_params=params(),
        name="attn_rows",
    )(side, keep, came, keep_twin, came_twin, *after)


def hold_kernel(*refs):
    pass


def hold(values, *after):
    many = isinstance(values, tuple)
    values = values if many else (values,)
    out = pl.pallas_call(
        hold_kernel,
        out_shape=tuple(shape(v.shape, v.dtype) for v in values),
        in_specs=[HBM] * (len(values) + len(after)),
        out_specs=(HBM,) * len(values),
        input_output_aliases={k: k for k in range(len(values))},
        name="hold",
    )(*values, *after)
    return out if many else out[0]


def attention_kernel(
    side_ref,
    own_ref,
    other_ref,
    normed_ref,
    bqv_ref,
    strip_ref,
    keep_ref,
    x_ref,
    mod_ref,
    bproj_ref,
    qh_ref,
    kh_ref,
    vh_ref,
    mine_ref,
    theirs_ref,
    attended_ref,
    middle_ref,
    normed_two_ref,
    w_out_ref,
    w_ref,
    flat_ref,
    mix_ref,
    sem,
):
    length, width = x_ref.shape
    hd = width // HEADS
    tile = 384
    wait = fetch_halves(side_ref, own_ref, other_ref, w_ref, sem)
    normed = normed_ref[...]

    def project(slot, lo, cols, at, bias_at):
        def body(o):
            y = mm(normed, w_ref[slot, :, pl.ds(lo + o, tile)])
            if bias_at is not None:
                y = y + bqv_ref[:, pl.ds(bias_at + o, tile)]
            flat_ref[:, pl.ds(at + o, tile)] = y.astype(BF)

        strips(cols, tile, body)

    wait(0)
    project(0, 0, width, 0, 0)
    project(0, width, width, width, None)
    wait(1)
    keep_out = pltpu.make_async_copy(w_ref.at[1, :, pl.ds(width, width)], w_out_ref, sem.at[2])
    keep_out.start()
    project(1, 0, width, 2 * width, width)
    for h in range(HEADS):
        qh_ref[h] = flat_ref[:, h * hd : (h + 1) * hd]
        kh_ref[h] = flat_ref[:, width + h * hd : width + (h + 1) * hd]
        vh_ref[h] = flat_ref[:, 2 * width + h * hd : 2 * width + (h + 1) * hd]
    keep = keep_ref[...] > 0.0

    def head(h, carry):
        sc = mm_nt(qh_ref[h], kh_ref[h]) * (hd**-0.5) + bias_of(strip_ref[h])
        sc = jnp.where(keep, sc, -1e30)
        ex = jnp.exp(sc - jnp.max(sc, axis=-1, keepdims=True))
        soft = ex / jnp.sum(ex, axis=-1, keepdims=True)
        mix_ref[h] = mm(soft.astype(BF), vh_ref[h]).astype(BF)
        return carry

    lax.fori_loop(0, HEADS, head, 0, unroll=2)
    for h in range(HEADS):
        flat_ref[:, h * hd : (h + 1) * hd] = mix_ref[h]
    mixed = flat_ref[:, 0:width]
    mine_ref[:, 0:width] = normed
    theirs_ref[:, 0:width] = normed
    for s, (normed_at, mixed_at) in enumerate(((mine_ref, theirs_ref), (theirs_ref, mine_ref))):

        @pl.when(side_ref[0] == s)
        def _():
            normed_at[:, width:] = normed
            mixed_at[:, width:] = mixed

    def out(o):
        y = mm(mixed, w_ref[1, :, pl.ds(width + o, tile)]) + bproj_ref[:, pl.ds(o, tile)]
        attended_ref[:, pl.ds(o, tile)] = y

    strips(width, tile, out)
    middle = x_ref[...] + mod_ref[2:3, :] * attended_ref[...]
    middle_ref[...] = middle
    n2, _ = normal(middle)
    normed_two_ref[...] = (n2 * (1.0 + mod_ref[4:5, :]) + mod_ref[3:4, :]).astype(BF)
    keep_out.wait()


def attention(side, own, other, normed, b_qv, bias, keep, x, mod, b_proj):
    length, width = x.shape
    hd = width // HEADS
    per_head = shape((HEADS, length, hd), BF)
    return pl.pallas_call(
        attention_kernel,
        out_shape=(
            per_head,
            per_head,
            per_head,
            shape((length, 2 * width), BF),
            shape((length, 2 * width), BF),
            shape((length, width), F32),
            shape((length, width), F32),
            shape((length, width), BF),
            shape((width, width), BF),
        ),
        in_specs=[SCALAR, HBM, HBM] + [WHOLE] * 7,
        out_specs=(WHOLE,) * 8 + (HBM,),
        scratch_shapes=[
            pltpu.VMEM((2, width, 2 * width), BF),
            pltpu.VMEM((length, 3 * width), BF),
            pltpu.VMEM((HEADS, length, hd), BF),
            pltpu.SemaphoreType.DMA((3,)),
        ],
        compiler_params=params(),
        cost_estimate=cost(8 * length * width * width + 4 * length * length * width, 24e6),
        name="attention",
    )(side, own, other, normed, b_qv, bias, keep, x, mod, b_proj)


def fc2_tiles(width, half, tile):
    part = tile // 2
    per = width // part
    at = lambda q: (q % per, half // width + q // per)
    return [pl.BlockSpec((part, width), lambda t, k=k: at(2 * t + k)) for k in range(2)]


def mlp_half(normed_two_ref, b_ref, c0_ref, c1_ref, bf1_ref, hid_ref, slope_ref):
    act, slope = gelu_parts(mm(normed_two_ref[...], b_ref[...]) + bf1_ref[...])
    hid = act.astype(BF)
    hid_ref[...] = hid
    slope_ref[...] = slope
    return mm(hid, jnp.concatenate([c0_ref[...], c1_ref[...]], axis=0))


def mlp_first_kernel(normed_two_ref, b_ref, c0_ref, c1_ref, bf1_ref, hid_ref, slope_ref, part_ref):
    total = mlp_half(normed_two_ref, b_ref, c0_ref, c1_ref, bf1_ref, hid_ref, slope_ref)

    @pl.when(pl.program_id(0) == 0)
    def _():
        part_ref[...] = total

    @pl.when(pl.program_id(0) > 0)
    def _():
        part_ref[...] += total


def mlp_last_kernel(
    normed_two_ref,
    b_ref,
    c0_ref,
    c1_ref,
    bf1_ref,
    part_ref,
    bf2_ref,
    middle_ref,
    cot_ref,
    mod_ref,
    place_ref,
    present_ref,
    hid_ref,
    slope_ref,
    g_branch_ref,
    out_ref,
    sums_ref,
    acc_ref,
):
    t = pl.program_id(0)
    total = mlp_half(normed_two_ref, b_ref, c0_ref, c1_ref, bf1_ref, hid_ref, slope_ref)

    @pl.when(t == 0)
    def _():
        acc_ref[...] = part_ref[...] + total

    @pl.when(t > 0)
    def _():
        acc_ref[...] += total

    @pl.when(t == pl.num_programs(0) - 1)
    def _():
        branch = acc_ref[...] + bf2_ref[...]
        cot = cot_ref[...]
        gate = mod_ref[5:6, :]
        result = middle_ref[...] + gate * branch
        out = jnp.where(present_ref[...] > 0.0, result, 0.0).astype(BF)
        out_ref[...] = mm_tn(place_ref[...], out).astype(BF)
        g_branch = (cot * gate).astype(BF)
        g_branch_ref[...] = g_branch
        sums_ref[0:1, :] = jnp.sum(cot * branch, axis=0, keepdims=True)
        sums_ref[1:2, :] = jnp.sum(g_branch.astype(F32), axis=0, keepdims=True)


def mlp(normed_two, weights, bf1, last=None):
    length, width = normed_two.shape
    half = weights.shape[1] // 2
    tile = 2 * width // 3
    fixed = lambda a: pl.BlockSpec(a.shape, lambda t: (0, 0))
    cols = lambda r: pl.BlockSpec((r, tile), lambda t: (0, t))
    rows = fc2_tiles(width, half, tile)
    whole = lambda r: pl.BlockSpec((r, width), lambda t: (0, 0))
    more = last or ()
    outs = [shape((length, half), BF), shape((length, half), F32)]
    if last:
        outs += [shape((length, width), BF), shape((length, width), BF), shape((8, width), F32)]
    else:
        outs += [shape((length, width), F32)]
    return pl.pallas_call(
        mlp_last_kernel if last else mlp_first_kernel,
        grid=(half // tile,),
        out_shape=tuple(outs),
        in_specs=[fixed(normed_two), cols(width)] + rows + [cols(1)] + [fixed(a) for a in more],
        out_specs=tuple([cols(length), cols(length)] + [whole(o.shape[0]) for o in outs[2:]]),
        scratch_shapes=[pltpu.VMEM((length, width), F32)] if last else [],
        compiler_params=params(),
        cost_estimate=cost(4 * length * width * half, 16e6),
        name="mlp",
    )(normed_two, weights, weights, weights, bf1, *more)


def mlp_back_kernel(
    g_branch_ref,
    b0_ref,
    b1_ref,
    c00_ref,
    c01_ref,
    c10_ref,
    c11_ref,
    slope0_ref,
    slope1_ref,
    middle_ref,
    attended_ref,
    cot_ref,
    mod_ref,
    w_out_ref,
    *rest,
):
    pre0_ref, pre1_ref, bsum_ref, g_middle_ref, g_att_ref, g_mixed_ref, sums_ref, acc_ref = rest[-8:]
    t = pl.program_id(0)
    g_branch = g_branch_ref[...]
    total = None
    for i, (b_ref, c_refs, slope_ref, pre_ref) in enumerate(
        (
            (b0_ref, (c00_ref, c01_ref), slope0_ref, pre0_ref),
            (b1_ref, (c10_ref, c11_ref), slope1_ref, pre1_ref),
        )
    ):
        c = jnp.concatenate([ref[...] for ref in c_refs], axis=0)
        pre = (mm_nt(g_branch, c) * slope_ref[...]).astype(BF)
        pre_ref[...] = pre
        bsum_ref[i : i + 1, :] = jnp.sum(pre.astype(F32), axis=0, keepdims=True)
        part = mm_nt(pre, b_ref[...])
        total = part if total is None else total + part

    @pl.when(t == 0)
    def _():
        acc_ref[...] = total

    @pl.when(t > 0)
    def _():
        acc_ref[...] += total

    @pl.when(t == pl.num_programs(0) - 1)
    def _():
        g_n2 = acc_ref[...]
        n2, inv2 = normal(middle_ref[...])
        sums_ref[0:1, :] = jnp.sum(g_n2, axis=0, keepdims=True)
        sums_ref[1:2, :] = jnp.sum(g_n2 * n2, axis=0, keepdims=True)
        g_middle = cot_ref[...] + normal_back(g_n2 * (1.0 + mod_ref[4:5, :]), n2, inv2)
        g_middle_ref[...] = g_middle
        sums_ref[2:3, :] = jnp.sum(g_middle * attended_ref[...], axis=0, keepdims=True)
        g_att = (g_middle * mod_ref[2:3, :]).astype(BF)
        g_att_ref[...] = g_att
        sums_ref[3:4, :] = jnp.sum(g_att.astype(F32), axis=0, keepdims=True)
        g_mixed_ref[...] = mm_nt(g_att, w_out_ref[...]).astype(BF)


def mlp_back(g_branch, weights, slope0, slope1, middle, attended, cot, mod, w_out, after=()):
    length, width = middle.shape
    half = weights[0].shape[1] // 2
    tile = 2 * width // 3
    fixed = lambda a: pl.BlockSpec(a.shape, lambda t: (0, 0))
    cols = lambda r: pl.BlockSpec((r, tile), lambda t: (0, t))
    rows = fc2_tiles(width, half, tile)
    whole = lambda r: pl.BlockSpec((r, width), lambda t: (0, 0))
    return pl.pallas_call(
        mlp_back_kernel,
        grid=(half // tile,),
        out_shape=(
            shape((length, half), BF),
            shape((length, half), BF),
            shape((2, half), F32),
            shape((length, width), F32),
            shape((length, width), BF),
            shape((length, width), BF),
            shape((8, width), F32),
        ),
        in_specs=[
            fixed(g_branch),
            cols(width),
            cols(width),
            *rows,
            *rows,
            cols(length),
            cols(length),
            fixed(middle),
            fixed(attended),
            fixed(cot),
            fixed(mod),
            fixed(w_out),
        ]
        + [HBM] * len(after),
        out_specs=(
            cols(length),
            cols(length),
            cols(2),
            whole(length),
            whole(length),
            whole(length),
            whole(8),
        ),
        scratch_shapes=[pltpu.VMEM((length, width), F32)],
        compiler_params=params(),
        cost_estimate=cost(8 * length * width * half, 32e6),
        name="mlp_back",
    )(
        g_branch,
        *weights,
        weights[0],
        weights[0],
        weights[1],
        weights[1],
        slope0,
        slope1,
        middle,
        attended,
        cot,
        mod,
        w_out,
        *after,
    )


def heads_back(q_ref, k_ref, v_ref, strip_ref, keep, gm_ref, dq_ref, dk_ref, dv_ref, sums_ref, start):
    scale = q_ref.shape[2] ** -0.5
    length = q_ref.shape[1]

    def head(i, carry):
        h = start + i
        q, k, v, gm = q_ref[h], k_ref[h], v_ref[h], gm_ref[i]
        sc = mm_nt(q, k) * scale + bias_of(strip_ref[h])
        sc = jnp.where(keep, sc, -1e30)
        ex = jnp.exp(sc - jnp.max(sc, axis=-1, keepdims=True))
        soft = ex / jnp.sum(ex, axis=-1, keepdims=True)
        dv_ref[i] = mm_tn(soft.astype(BF), gm).astype(BF)
        dp = mm_nt(gm, v)
        ds = (soft * (dp - jnp.sum(dp * soft, axis=-1, keepdims=True))).astype(BF)
        dq_ref[i] = (mm(ds, k) * scale).astype(BF)
        dk_ref[i] = (mm_tn(ds, q) * scale).astype(BF)
        dsf = ds.astype(F32)
        total = jnp.zeros((GRID, sums_ref.shape[2]), F32)
        blank = jnp.zeros((GRID, sums_ref.shape[2] - length), F32)
        for y in range(GRID):
            rows = jnp.concatenate([dsf[y * GRID : (y + 1) * GRID, :], blank], axis=1)
            by = (GRID - 1 - y) * GRID
            total = total + (pltpu.roll(rows, by, 1) if by else rows)
        sums_ref[i] = total
        return carry

    lax.fori_loop(0, dq_ref.shape[0], head, 0, unroll=4)


def first_heads_kernel(qh_ref, kh_ref, vh_ref, strip_ref, keep_ref, g_mixed_ref, *rest):
    dq_ref, dk_ref, dv_ref, sums_ref, gm_ref = rest[-5:]
    hd = qh_ref.shape[2]
    for i in range(HEADS // 2):
        gm_ref[i] = g_mixed_ref[:, i * hd : (i + 1) * hd]
    heads_back(
        qh_ref, kh_ref, vh_ref, strip_ref, keep_ref[...] > 0.0, gm_ref, dq_ref, dk_ref, dv_ref, sums_ref, 0
    )


def first_heads(qh, kh, vh, strip, keep, g_mixed, after=()):
    heads, length, hd = qh.shape
    some = shape((heads // 2, length, hd), BF)
    return pl.pallas_call(
        first_heads_kernel,
        out_shape=(some, some, some, shape((heads // 2,) + strip.shape[1:], F32)),
        in_specs=[WHOLE] * 6 + [HBM] * len(after),
        out_specs=(WHOLE,) * 4,
        scratch_shapes=[pltpu.VMEM((heads // 2, length, hd), BF)],
        compiler_params=params(),
        cost_estimate=cost(5 * length * length * heads * hd, 16e6),
        name="first_heads",
    )(qh, kh, vh, strip, keep, g_mixed, *after)


def last_heads_kernel(
    side_ref,
    qh_ref,
    kh_ref,
    vh_ref,
    strip_ref,
    keep_ref,
    g_mixed_ref,
    g_att_ref,
    fq_ref,
    fk_ref,
    fv_ref,
    fsum_ref,
    *rest,
):
    mine_ref, top_ref, low_ref, lo_ref, hi_ref, sums_ref, both_ref, gm_ref, dq_ref, dk_ref, dv_ref, strips_ref = rest[-12:]
    theirs_ref = both_ref
    width = g_mixed_ref.shape[1]
    hd = qh_ref.shape[2]
    half = HEADS // 2
    for i in range(half):
        gm_ref[i] = g_mixed_ref[:, (half + i) * hd : (half + i + 1) * hd]
    heads_back(
        qh_ref, kh_ref, vh_ref, strip_ref, keep_ref[...] > 0.0, gm_ref, dq_ref, dk_ref, dv_ref, strips_ref, half
    )
    for s, (qk_at, v_at) in enumerate(((mine_ref, theirs_ref), (theirs_ref, mine_ref))):

        @pl.when(side_ref[0] == s)
        def _():
            for h in range(HEADS):
                q, k, v = (fq_ref, fk_ref, fv_ref) if h < half else (dq_ref, dk_ref, dv_ref)
                i = h % half
                qk_at[:, h * hd : (h + 1) * hd] = q[i]
                qk_at[:, width + h * hd : width + (h + 1) * hd] = k[i]
                v_at[:, h * hd : (h + 1) * hd] = v[i]
            v_at[:, width:] = g_att_ref[...]
            sums_ref[0:1, :] = jnp.sum(qk_at[:, 0:width].astype(F32), axis=0, keepdims=True)
            sums_ref[1:2, :] = jnp.sum(v_at[:, 0:width].astype(F32), axis=0, keepdims=True)

    length = both_ref.shape[0]
    top_ref[...] = both_ref[0 : length // 2, :]
    low_ref[...] = both_ref[length // 2 :, :]
    lanes = lo_ref.shape[1]
    for part, ref in enumerate((fsum_ref, strips_ref)):
        lo = jnp.zeros((half, lanes), F32)
        hi = jnp.zeros((half, lanes), F32)
        j = lax.broadcasted_iota(jnp.int32, lo.shape, 1) % GRID
        for i in range(GRID):
            k = GRID - 1 - i
            row = ref[:, i, :]
            a = jnp.where(j < GRID - k, row, 0.0)
            lo = lo + (pltpu.roll(a, k, 1) if k else a)
            if k:
                hi = hi + pltpu.roll(jnp.where(j < GRID - k, 0.0, row), lanes - (GRID - k), 1)
        lo_ref[part * half : (part + 1) * half, :] = lo
        hi_ref[part * half : (part + 1) * half, :] = hi


def last_heads(side, qh, kh, vh, strip, keep, g_mixed, g_att, firsts, after=()):
    length, width = g_mixed.shape
    heads, _, hd = qh.shape
    per_head = pltpu.VMEM((heads // 2, length, hd), BF)
    window = shape((heads, strip.shape[2]), F32)
    return pl.pallas_call(
        last_heads_kernel,
        out_shape=(
            shape((length, 2 * width), BF),
            shape((length // 2, 2 * width), BF),
            shape((length // 2, 2 * width), BF),
            window,
            window,
            shape((8, width), F32),
        ),
        in_specs=[SCALAR] + [WHOLE] * 11 + [HBM] * len(after),
        out_specs=(WHOLE,) * 6,
        scratch_shapes=[pltpu.VMEM((length, 2 * width), BF)]
        + [per_head] * 4 + [pltpu.VMEM((heads // 2,) + strip.shape[1:], F32)],
        compiler_params=params(),
        cost_estimate=cost(5 * length * length * width, 16e6),
        name="last_heads",
    )(side, qh, kh, vh, strip, keep, g_mixed, g_att, *firsts, *after)


def tokens_back_kernel(
    side_ref,
    own_ref,
    other_ref,
    mine_ref,
    top_ref,
    low_ref,
    x_ref,
    g_middle_ref,
    mod_ref,
    place_ref,
    *rest,
):
    out_ref, sums_ref, w_ref, acc_ref, qk_ref, v_ref, sem = rest[-7:]
    length, width = x_ref.shape
    wait = fetch_halves(side_ref, own_ref, other_ref, w_ref, sem)
    half = length // 2

    @pl.when(side_ref[0] == 0)
    def _():
        qk_ref[...] = mine_ref[...]
        v_ref[0:half, :] = top_ref[:, 0:width]
        v_ref[half:, :] = low_ref[:, 0:width]

    @pl.when(side_ref[0] == 1)
    def _():
        qk_ref[0:half, :] = top_ref[...]
        qk_ref[half:, :] = low_ref[...]
        v_ref[...] = mine_ref[:, 0:width]

    wait(0)
    acc_ref[...] = mm_nt(qk_ref[...], w_ref[0])
    wait(1)
    g_n1 = acc_ref[...] + mm_nt(v_ref[...], w_ref[1, :, 0:width])
    n1, inv1 = normal(x_ref[...])
    sums_ref[0:1, :] = jnp.sum(g_n1, axis=0, keepdims=True)
    sums_ref[1:2, :] = jnp.sum(g_n1 * n1, axis=0, keepdims=True)
    g_x = g_middle_ref[...] + normal_back(g_n1 * (1.0 + mod_ref[1:2, :]), n1, inv1)
    out_ref[...] = mm_tn(place_ref[...], g_x.astype(BF)).astype(BF)


def tokens_back(side, own, other, mine, theirs, x, g_middle, mod, place, after=()):
    length, width = x.shape
    return pl.pallas_call(
        tokens_back_kernel,
        out_shape=(shape((length, width), BF), shape((8, width), F32)),
        in_specs=[SCALAR, HBM, HBM] + [WHOLE] * 7 + [HBM] * len(after),
        out_specs=(WHOLE,) * 2,
        scratch_shapes=[
            pltpu.VMEM((2, width, 2 * width), BF),
            pltpu.VMEM((length, width), F32),
            pltpu.VMEM((length, 2 * width), BF),
            pltpu.VMEM((length, width), BF),
            pltpu.SemaphoreType.DMA((2,)),
        ],
        compiler_params=params(),
        cost_estimate=cost(6 * length * width * width, 16e6),
        name="tokens_back",
    )(side, own, other, mine, *theirs, x, g_middle, mod, place, *after)


def local(
    n,
    tokens,
    condition,
    kept_index,
    kept_count,
    cotangent,
    w_ada,
    w_qkv,
    w_proj,
    w_fc1,
    w_fc2,
    b_ada,
    b_qv,
    b_proj,
    b_fc1,
    b_fc2,
    rel_table,
):
    side = lax.axis_index("stream")
    chip = lax.axis_index("dp")
    length, width = tokens.shape[2], tokens.shape[3]
    ff = w_fc1.shape[1]
    rows = width // n
    cut = ff // (2 * n)
    first = side == 0
    side_word = side.astype(jnp.int32).reshape(1)
    chip_word = chip.astype(jnp.int32).reshape(1)

    order_first, order_parts = orders_out(n)
    firsts = tuple(part[-1] for part in order_parts)

    ordinal = jnp.arange(length, dtype=jnp.int32)
    count = jnp.where(first, length, kept_count[0])
    position = jnp.where(first, ordinal, kept_index[0])
    place = ((position[None, :] == ordinal[:, None]) & (ordinal[None, :] < count)).astype(BF)
    present = jnp.sum(place.astype(F32), axis=1)
    keep = present.reshape(1, length)
    present = present.reshape(length, 1)
    x = mm(place, tokens[0, 0])
    cot = mm(place, cotangent[0, 0])
    bias = bias_strip(rel_table)

    cond = condition[0, 0]
    sig = jax.nn.sigmoid(cond)
    cond_act = (cond * sig).astype(BF)
    shard_a = attn_shard(side_word, w_qkv, w_proj)
    all_a = Gathering(chip_word, shard_a, n)
    acts = trade(hold(jnp.broadcast_to(cond_act[None], (n, width)), shard_a))
    acts_part = lax.dynamic_slice_in_dim(acts, chip * rows, rows, axis=1)
    shard_bc = mlp_shard(n, side_word, w_fc1, w_fc2, after=(shard_a,))
    last = all_a.step(shard_bc, acts_part)
    all_bc = Gathering(chip_word, hold(shard_bc, *last), n)
    for _ in range(len(order_parts[0]) - 2 + len(order_first) - 1):
        last = all_a.step(*last)
    while all_bc.turn < all_bc.cut_at:
        last = all_bc.step(*last)
    acts_twin = swap_stream(acts_part)
    if {p[-1] for p in order_parts} == {p[0] for p in order_parts}:
        last, result_a, on_bc = merge_steps(all_a, all_bc, acts_twin, bias, x, cot)
        mod_part = trade(hold(mm(acts_part, w_ada), *last))
        last = on_bc(mod_part)
    else:
        last = all_a.step(*last, acts_twin, bias, x, cot)
        result_a = all_a.result
        mod_part = trade(hold(mm(acts_part, w_ada), *last))
        last = all_bc.step(mod_part)
    a_own = result_a(*last)
    a_other = swap_stream(a_own)
    last = (a_own,)
    while not all_bc.done():
        last = all_bc.step(*last)
    mod_part = hold(mod_part, *last)
    modulation = jnp.sum(mod_part, axis=0) + b_ada
    mod = modulation.reshape(6, width)
    n1, _ = normal(x)
    normed = (n1 * (1.0 + mod[1]) + mod[0]).astype(BF)
    qh, kh, vh, lhs_mine, lhs_theirs, attended, middle, normed_two, w_out = attention(
        side_word,
        a_own,
        a_other,
        normed,
        b_qv.reshape(1, -1),
        bias,
        keep,
        x,
        mod,
        b_proj.reshape(1, -1),
    )

    bf1 = jnp.transpose(b_fc1.reshape(n, 2, 2, cut // 2), (1, 2, 0, 3)).reshape(2, 1, ff // 2)
    bf1_own, bf1_other = jnp.where(first, bf1[0], bf1[1]), jnp.where(first, bf1[1], bf1[0])
    bf2 = b_fc2.reshape(1, -1)
    bc_own = all_bc.result(normed_two, bf1_own, bf1_other, bf2, present, place)
    bc_other = swap_stream(bc_own)
    lhs_twin = swap_stream(lhs_theirs)
    n2_twin = swap_stream(normed_two)
    hid0, slope0, part = mlp(normed_two, bc_own, bf1_own)
    hid1, slope1, g_branch, out_tokens, sums_a = mlp(
        normed_two,
        bc_other,
        bf1_other,
        (part, bf2, middle, cot, mod, place, present),
    )

    parts_c = product(
        chip_word, hid0, swap_stream(hid1), g_branch, swap_stream(g_branch), width, n, firsts
    )
    sum_c = Reduction(chip_word, parts_c, n)
    pre0, pre1, pre_sum, g_middle, g_att, g_mixed, sums_b = mlp_back(
        g_branch,
        (bc_own, bc_other),
        slope0,
        slope1,
        middle,
        attended,
        cot,
        mod,
        w_out,
        after=(parts_c[0][0], lhs_twin, n2_twin),
    )
    kept = step([sum_c], g_mixed)
    pre_twin = swap_stream(pre1)
    one = first_heads(qh, kh, vh, bias, keep, g_mixed, after=kept + (pre_twin,))
    kept = step([sum_c], one[0])
    while not sum_c.parted():
        kept = step([sum_c], *kept)
    parts_b = product(chip_word, normed_two, n2_twin, pre0, pre_twin, width, n, firsts, after=kept)
    sum_b = Reduction(chip_word, parts_b, n)
    g_mine, top, low, lo, hi, sums_c = last_heads(
        side_word, qh, kh, vh, bias, keep, g_mixed, g_att, one, after=(parts_b[0][0],)
    )
    g_theirs = (top, low)
    g_twin = (swap_stream(top), swap_stream(low))
    kept = step([sum_b], g_mine) + g_twin
    grad_tokens, sums_d = tokens_back(
        side_word, a_own, a_other, g_mine, g_theirs, x, g_middle, mod, place, after=kept
    )

    kept = (sums_d,)
    while not sum_b.parted():
        kept = step([sum_b], *kept)
    mod_rows = 6 * width // 128
    group = -(-mod_rows // 8) * 8
    told = pack(
        side_word, (sums_a, sums_b, sums_c, sums_d, lo, hi, pre_sum), SUM_ROWS + group, after=kept
    )
    bits = all_bits(n)[::-1]
    came = swap(told, bits[0], n)
    sum_b.take(sum_c)
    kept = (told,)
    while not sum_b.done():
        kept = step([sum_b], *kept)
    told = meet(chip_word, told, came, bits[0], group, after=kept)
    told = meet(chip_word, told, swap(told, bits[1], n), bits[1], group)
    came = swap(told, bits[2], n)
    parts_a = product(
        chip_word, lhs_mine, lhs_twin, g_mine, g_twin, width, n, firsts, after=(told,) + kept
    )
    told = meet(chip_word, told, came, bits[2], group, after=(parts_a[0][0],))
    sum_a = Reduction(chip_word, parts_a, n)
    for b in bits[3:]:
        told = meet(chip_word, told, swap(told, b, n), b, group)
    d_cb = sum_b.result()
    kept = step([sum_a], told, d_cb)
    d_cb_twin = swap_stream(d_cb)
    grad_w_fc2 = fc2_rows(side_word, d_cb, d_cb_twin)
    grad_w_fc1 = fc1_rows(n, side_word, d_cb, d_cb_twin)
    kept = step([sum_a], told, grad_w_fc2)
    twin = swap_stream(told)

    def mods_of(t):
        return t[SUM_ROWS:].reshape(n, -1, 128)[:, :mod_rows].reshape(n, -1)

    g_own, g_twin = mods_of(told), mods_of(twin)
    grad_w_ada = mm_tn(acts_part, g_own.astype(BF)) + mm_tn(acts_twin, g_twin.astype(BF))
    grad_b_ada = jnp.sum(g_own, axis=0) + jnp.sum(g_twin, axis=0)
    kept = step([sum_a], *kept, grad_w_ada, grad_b_ada)
    while not sum_a.done():
        kept = step([sum_a], *kept)
    g_acts = trade(hold(mm_nt(g_own.astype(BF), w_ada), *kept)).reshape(width)
    grad_condition = g_acts * sig * (1.0 + cond * (1.0 - sig))
    sums = told[:SUM_ROWS] + twin[:SUM_ROWS]
    per = width // 128
    at = 4 * per + ff // 128
    grad_b_fc1 = jnp.transpose(sums[4 * per : at].reshape(2, 2, n, cut // 2), (2, 0, 1, 3)).reshape(-1)
    windows = jnp.transpose(sums[at:].reshape(2, -1, HEADS, 128), (0, 2, 1, 3)).reshape(2, HEADS, -1)
    parts = (
        sums[: 2 * per].reshape(-1),
        sums[2 * per : 3 * per].reshape(-1),
        grad_b_fc1,
        sums[3 * per : 4 * per].reshape(-1),
        table_of(windows[0], windows[1]),
    )
    keep_a, came_a = sum_a.pairs[0]
    grad_w_qkv, grad_w_proj = attn_rows(
        side_word,
        keep_a,
        came_a,
        swap_stream(keep_a),
        swap_stream(came_a),
        after=(g_acts, grad_w_fc1) + parts,
    )
    return (
        out_tokens[None, None],
        grad_tokens[None, None],
        grad_condition[None, None],
        grad_w_ada,
        grad_w_qkv,
        grad_w_proj,
        grad_w_fc1,
        grad_w_fc2,
        grad_b_ada,
        *parts,
    )


def solution(mesh):
    n = mesh.shape["dp"]

    def body(*args):
        return local(n, *args)

    return jax.shard_map(
        body,
        mesh=mesh,
        in_specs=(
            P("stream", "dp", None, None),
            P("stream", "dp", None),
            P("dp", None),
            P("dp"),
            P("stream", "dp", None, None),
            P("dp", None),
            P("dp", None),
            P("dp", None),
            P("dp", None),
            P("dp", None),
            P(),
            P(),
            P(),
            P(),
            P(),
            P(),
        ),
        out_specs=(
            P("stream", "dp", None, None),
            P("stream", "dp", None, None),
            P("stream", "dp", None),
            P("dp", None),
            P("dp", None),
            P("dp", None),
            P("dp", None),
            P("dp", None),
            P(),
            P(),
            P(),
            P(),
            P(),
            P(),
        ),
        check_vma=False,
    )
```
